256 devices in a mesh: lat: 8 (over x, core), lon: 32 (over z, y).
Axes of the slice: x: 4, y: 4, z: 8, core: 2. Of those that a mesh axis runs over, the one named last changes fastest.
Arguments:
- heat_anomaly: float32 [62, 128, 4096], P(None, 'lat', 'lon'), may hold values from -6 to 6
- saltiness_anomaly: float32 [62, 128, 4096], P(None, 'lat', 'lon'), may hold values from -6 to 6
- zonal_current_array: float32 [62, 128, 4096], P(None, 'lat', 'lon'), may hold values from -6 to 6
- meridional_current_array: float32 [62, 128, 4096], P(None, 'lat', 'lon'), may hold values from -6 to 6
- sea_height_prior: float32 [128, 4096], P('lat', 'lon'), may hold values from -4 to 4
- ocean_layer_number: int32 [128, 4096], P('lat', 'lon'), may hold values from 0 to 62, as said below
Outputs:
- heat_anomaly_next: float32 [62, 128, 4096], P(None, 'lat', 'lon')
- saltiness_next: float32 [62, 128, 4096], P(None, 'lat', 'lon')
- zonal_current_next: float32 [62, 128, 4096], P(None, 'lat', 'lon')
- meridional_current_next: float32 [62, 128, 4096], P(None, 'lat', 'lon')
- sea_height_result: float32 [128, 4096], P('lat', 'lon')
The draws below stay inside these ranges and needn't reach their ends.
Inputs may be any that keep to these rules, and one draw needn't show every extreme that they name: `ocean_layer_number`: 0 marks land; elsewhere the number of wet levels counted from the top.
All inputs are finite; a program needn't handle non-finite values.
Results may differ from the reference program's by a relative error of at most 0.0003.
Values sent between devices are 32-bit elements; how exact they have to be, the bound alone decides.
No kernel may reach another device: no remote copies, remote signals or barrier semaphores. Data moves between devices by JAX's collectives and lax.ppermute only.
A program may use at most 128 MiB of HBM per device.

```python
import jax
import jax.numpy as jnp
from jax import lax

VERTICAL_LAYERS = 62
ITERATIONS = 32
MERIDIAN_CELLS = 128
PARALLEL_CELLS = 4096


def draw_sea_height_prior(key, part):
    key = jax.random.fold_in(key, 11)
    return jnp.clip(jax.random.normal(key, (MERIDIAN_CELLS, PARALLEL_CELLS), jnp.float32), -4.0, 4.0)


def draw_ocean_layer_number(key, part):
    key = jax.random.fold_in(key, 7)
    raw_levels = jax.random.randint(key, (MERIDIAN_CELLS, PARALLEL_CELLS), -(VERTICAL_LAYERS // 3), VERTICAL_LAYERS + 4, dtype=jnp.int32)
    return jnp.clip(raw_levels, 0, VERTICAL_LAYERS)


def block_scale(stream_key, extent, split, low, top_value):
    def one(dim, shards_of):
        steps = jax.random.uniform(jax.random.fold_in(jax.random.fold_in(stream_key, 6), dim), (shards_of,), jnp.float32, low / len(split), top_value / len(split))
        return jnp.repeat(jnp.exp(steps), extent[dim] // shards_of).reshape((-1,) + (1,) * (len(extent) - dim - 1))

    loudness = one(*split[0])
    for cut in split[1:]:
        loudness = loudness * one(*cut)
    return loudness


def bell_draw(own_key, dims, scale, most, split=(), kind=jnp.bfloat16):
    gain = block_scale(own_key, dims, split, -0.22, 0.18) if split else 1.0
    entries = jax.random.normal(own_key, dims, jnp.float32) * scale * gain
    return jnp.minimum(jnp.maximum(entries, -most), most).astype(kind)


def setup_inputs(seed: int = 0) -> dict:
    key_list = jax.random.split(jax.random.key(seed), 7)
    return {
        "heat_anomaly": bell_draw(key_list[0], (VERTICAL_LAYERS, MERIDIAN_CELLS, PARALLEL_CELLS), 1.0, 6.0, ((1, 8), (2, 32)), jnp.float32),
        "saltiness_anomaly": bell_draw(key_list[1], (VERTICAL_LAYERS, MERIDIAN_CELLS, PARALLEL_CELLS), 1.0, 6.0, ((1, 8), (2, 32)), jnp.float32),
        "zonal_current_array": bell_draw(key_list[2], (VERTICAL_LAYERS, MERIDIAN_CELLS, PARALLEL_CELLS), 1.0, 6.0, ((1, 8), (2, 32)), jnp.float32),
        "meridional_current_array": bell_draw(key_list[3], (VERTICAL_LAYERS, MERIDIAN_CELLS, PARALLEL_CELLS), 1.0, 6.0, ((1, 8), (2, 32)), jnp.float32),
        "sea_height_prior": draw_sea_height_prior(jax.random.fold_in(key_list[6], 71), 0),
        "ocean_layer_number": draw_ocean_layer_number(jax.random.fold_in(key_list[6], 71), 0),
    }


TIME_STEP = 0.1
MIX_TRACER = 0.05
MIX_MOMENTUM = 0.05
HEAT_INDEX = 0.2
SALT_INDEX = 0.2
CORIOLIS = 2.0
SURFACE_TERM = 0.0005
TRANSPORT_SCALE = 0.05


def chebyshev_weights(total_steps):
    low_bound = SURFACE_TERM / (SURFACE_TERM + 4.0)
    high_bound = 2.0 - low_bound
    spread_ratio = (high_bound - low_bound) / (high_bound + low_bound)
    middle = 0.5 * (high_bound + low_bound)
    weights = [1.0]
    for number in range(1, total_steps):
        if number == 1:
            weights.append(2.0 / (2.0 - spread_ratio * spread_ratio))
        else:
            weights.append(1.0 / (1.0 - spread_ratio * spread_ratio * weights[-1] / 4.0))
    scales = jnp.asarray([weight_value / middle for weight_value in weights], jnp.float32)
    carries = jnp.asarray([weight_value - 1.0 for weight_value in weights], jnp.float32)
    return scales, carries


def east_of(source):
    return jnp.roll(source, -1, axis=-1)


def west_of(source):
    return jnp.roll(source, 1, axis=-1)


def north_of(source):
    return jnp.concatenate([source[1:], jnp.zeros_like(source[:1])], axis=0)


def south_of(source):
    return jnp.concatenate([jnp.zeros_like(source[:1]), source[:-1]], axis=0)


def laplacian(source, mask_field):
    centre = source
    return mask_field * (((east_of(mask_field) * (east_of(source) - centre) + west_of(mask_field) * (west_of(source) - centre)) + north_of(mask_field) * (north_of(source) - centre)) + south_of(mask_field) * (south_of(source) - centre))


def advection(tracer, eastward, northward, water_indicator):
    east_flux = 0.25 * (eastward + east_of(eastward)) * (tracer + east_of(tracer)) * (water_indicator * east_of(water_indicator))
    north_flux = 0.25 * (northward + north_of(northward)) * (tracer + north_of(tracer)) * (water_indicator * north_of(water_indicator))
    return (east_flux - west_of(east_flux)) + (north_flux - south_of(north_flux))


def scalar_stepper(tracer, eastward, northward, water_indicator):
    mixing = laplacian(laplacian(tracer, water_indicator), water_indicator)
    advected = advection(tracer, eastward, northward, water_indicator)
    return water_indicator * (tracer - TIME_STEP * (advected + MIX_TRACER * mixing))


def reference(heat_anomaly, saltiness_anomaly, zonal_current_array, meridional_current_array, sea_height_prior, ocean_layer_number):
    row_position = jnp.arange(MERIDIAN_CELLS, dtype=jnp.int32).astype(jnp.float32)[:, None]
    coriolis = CORIOLIS * (2.0 * (row_position + 0.5) / MERIDIAN_CELLS - 1.0)

    def layer_stepper(running, inputs):
        hydrostatic_load, zonal_sum, north_sum = running
        level_index, temp_level, salt_level, zonal_level, north_level = inputs
        water_indicator = (level_index < ocean_layer_number).astype(jnp.float32)
        temp_new = scalar_stepper(temp_level, zonal_level, north_level, water_indicator)
        salt_new = scalar_stepper(salt_level, zonal_level, north_level, water_indicator)
        hydrostatic_load = hydrostatic_load + (SALT_INDEX * salt_level - HEAT_INDEX * temp_level) * water_indicator
        zonal_mix = laplacian(laplacian(zonal_level, water_indicator), water_indicator)
        north_mix = laplacian(laplacian(north_level, water_indicator), water_indicator)
        zonal_grad = 0.5 * (east_of(hydrostatic_load) - west_of(hydrostatic_load))
        north_grad = 0.5 * (north_of(hydrostatic_load) - south_of(hydrostatic_load))
        eastward_following = water_indicator * (zonal_level + TIME_STEP * ((coriolis * north_level - zonal_grad) - MIX_MOMENTUM * zonal_mix))
        northward_following = water_indicator * (north_level - TIME_STEP * ((coriolis * zonal_level + north_grad) + MIX_MOMENTUM * north_mix))
        return (hydrostatic_load, zonal_sum + eastward_following, north_sum + northward_following), (temp_new, salt_new, eastward_following, northward_following)

    empty_sheet = jnp.zeros((MERIDIAN_CELLS, PARALLEL_CELLS), jnp.float32)
    layer_numbers = jnp.arange(VERTICAL_LAYERS, dtype=jnp.int32)
    vertical_integrals, joined_arrays = lax.scan(layer_stepper, (empty_sheet, empty_sheet, empty_sheet), (layer_numbers, heat_anomaly, saltiness_anomaly, zonal_current_array, meridional_current_array))
    zonal_transport, north_transport = vertical_integrals[1], vertical_integrals[2]
    heat_anomaly_next, saltiness_next, zonal_current_next, meridional_current_next = joined_arrays

    ocean = (ocean_layer_number > 0).astype(jnp.float32)
    zonal_flow = zonal_transport * (ocean * east_of(ocean))
    north_flow = north_transport * (ocean * north_of(ocean))
    divergence = (zonal_flow - west_of(zonal_flow)) + (north_flow - south_of(north_flow))
    right_side = SURFACE_TERM * sea_height_prior - TRANSPORT_SCALE * divergence

    depth_plane = ocean_layer_number.astype(jnp.float32)
    east_face = jnp.minimum(depth_plane, east_of(depth_plane)) / VERTICAL_LAYERS
    north_face = jnp.minimum(depth_plane, north_of(depth_plane)) / VERTICAL_LAYERS
    west_face = west_of(east_face)
    south_face = south_of(north_face)
    diagonal_term = SURFACE_TERM + ((east_face + west_face) + north_face) + south_face
    scales, carries = chebyshev_weights(ITERATIONS)
    height = sea_height_prior
    change = jnp.zeros_like(sea_height_prior)
    for number in range(ITERATIONS):
        applied = diagonal_term * height - (((east_face * east_of(height) + west_face * west_of(height)) + north_face * north_of(height)) + south_face * south_of(height))
        residual = right_side - applied
        change = scales[number] * residual / diagonal_term + carries[number] * change
        height = height + change
    sea_height_result = ocean * height
    return heat_anomaly_next, saltiness_next, zonal_current_next, meridional_current_next, sea_height_result
```

```python
import functools

import jax
import jax.numpy as jnp
from jax import lax
from jax.experimental import pallas as pl
from jax.experimental.pallas import tpu as pltpu
from jax.sharding import PartitionSpec as P

ITERATIONS = 32

TIME_STEP = 0.1
MIX_TRACER = 0.05
MIX_MOMENTUM = 0.05
HEAT_INDEX = 0.2
SALT_INDEX = 0.2
CORIOLIS = 2.0
SURFACE_TERM = 0.0005
TRANSPORT_SCALE = 0.05

ROWS = 16
COLS = 128
GROUP = 8
TILE = (GROUP, COLS)


def chebyshev_weights(total_steps):
    low_bound = SURFACE_TERM / (SURFACE_TERM + 4.0)
    high_bound = 2.0 - low_bound
    spread_ratio = (high_bound - low_bound) / (high_bound + low_bound)
    middle = 0.5 * (high_bound + low_bound)
    weights = [1.0]
    for number in range(1, total_steps):
        if number == 1:
            weights.append(2.0 / (2.0 - spread_ratio * spread_ratio))
        else:
            weights.append(1.0 / (1.0 - spread_ratio * spread_ratio * weights[-1] / 4.0))
    return [weight / middle for weight in weights], [weight - 1.0 for weight in weights]


def lanes():
    return lax.broadcasted_iota(jnp.int32, TILE, 1)


def sublanes():
    return lax.broadcasted_iota(jnp.int32, TILE, 0)


def turn(value, by, axis=1):
    size = value.shape[axis]
    by = by % size
    return value if by == 0 else pltpu.roll(value, by, axis)


def row_of(ref, row):
    return jnp.broadcast_to(ref[pl.ds(row, 1), :], TILE)


def masked(mask, value):
    return jnp.where(mask, value, 0.0)


def pack_kernel(levels, t, s, u, v, depth, prior, to_north, to_south, to_sides, to_corners, wide):
    fields = (t, s, u, v)
    groups = -(-levels // GROUP)
    lane = lanes()
    slot = lane // 4
    near = ((lane + 4) & 63) < 8

    def body(g, corner):
        start = jnp.minimum(GROUP * g, levels - GROUP) * ROWS
        packs = []
        for pair in range(2):
            pack = jnp.zeros(TILE, jnp.float32)
            for f in range(2):
                field = 2 * pair + f
                for r in range(ROWS):
                    x = fields[field][pl.ds(start + r, GROUP, stride=ROWS), :]
                    if r < 2:
                        to_south[(r * 4 + field) * groups + g] = x
                    if r >= ROWS - 2:
                        to_north[((r - ROWS + 2) * 4 + field) * groups + g] = x
                    pack = jnp.where(slot == 16 * f + r, turn(x, 64 * f + 4 * r + 2), pack)
            to_sides[pair * groups + g] = pack
            packs.append(pack)
        both = jnp.where(near, packs[0], turn(packs[1], 8))
        place = 16 * (g % 4)
        corner = jnp.where(((lane + 4 - place) & 63) < 16, pltpu.roll(both, place, 1), corner)
        to_corners[g // 4] = corner
        return corner

    lax.fori_loop(0, groups, body, jnp.zeros(TILE, jnp.float32))
    pack = jnp.zeros(TILE, jnp.float32)
    for r in range(ROWS):
        x = row_of(depth, r)
        for f in range(2):
            pack = jnp.where(slot == 16 * f + r, turn(x, 64 * f + 4 * r + 2), pack)
    to_sides[2 * groups] = pack
    to_corners[2] = pack
    for half in range(2):
        for place, plane in ((half, depth), (2 + half, prior)):
            x = plane[GROUP * half : GROUP * (half + 1), :]
            wide[place] = x
            to_north[8 * groups + place] = x
            to_south[8 * groups + place] = x
            to_sides[2 * groups + 1 + place] = x
            to_corners[3 + place] = x


class Depths:
    def __init__(self, groups, store, depth, north, south, east, west, own, ne, nw, se, sw):
        lane = lanes()
        self.store = store
        column = lane & 3
        row = (lane // 4) & 15
        self.column, self.row = column, row
        self.lane = lane
        self.column_2 = column == 2
        self.column_low = column < 2
        d_own, d_east, d_west = own[2 * groups], east[2 * groups], west[2 * groups]
        k_ne, k_nw = turn(ne[2], 60), turn(nw[2], 60)
        k_se, k_sw = turn(se[2], 68), turn(sw[2], 68)
        self.corner_depths = (k_ne, k_nw, k_se, k_sw)
        q_west = jnp.where(self.column_low, d_west, d_own)
        q_east = jnp.where(self.column_low, d_own, d_east)
        self.side_depths = []
        for q, k_north, k_south in ((q_west, k_nw, k_sw), (q_east, k_ne, k_se)):
            self.side_depths.append((q,) + self.around(q, k_north, k_south))
        ring = self.join(q_west, q_east)
        ring_south, ring_north = self.join(k_sw, k_se), self.join(k_nw, k_ne)
        for j in range(-2, ROWS + 2):
            if j < 0:
                d = jnp.broadcast_to(south[8 * groups + 1][8 + j : 9 + j, :], TILE)
            elif j < ROWS:
                d = row_of(depth, j)
            else:
                d = jnp.broadcast_to(north[8 * groups][j - ROWS : j - ROWS + 1, :], TILE)
            store[3 * (j + 2)] = d
            if -1 <= j <= ROWS:
                edge = ring_south if j < 0 else ring_north if j == ROWS else ring
                d_e, d_w = self.sideways(d, edge, 0, min(max(j, 0), ROWS - 1))
                store[3 * (j + 2) + 1] = d_e
                store[3 * (j + 2) + 2] = d_w

    def around(self, q, k_north, k_south):
        north = jnp.where(self.row == ROWS - 1, k_north, turn(q, -4))
        south = jnp.where(self.row == 0, k_south, turn(q, 4))
        return turn(q, -1), turn(q, 1), north, south

    def join(self, q_west, q_east):
        return jnp.where(self.column_2, q_east, turn(q_west, 2))

    def sideways(self, q, edge, f, r):
        edge = turn(edge, 127 - (64 * f + 4 * r + 2))
        east = jnp.where(self.lane == COLS - 1, edge, turn(q, -1))
        west = jnp.where(self.lane == 0, edge, turn(q, 1))
        return east, west

    def of(self, j):
        return self.store[3 * (j + 2)]

    def east(self, j):
        return self.store[3 * (j + 2) + 1]

    def west(self, j):
        return self.store[3 * (j + 2) + 2]


class Edges:
    def __init__(self, dep, g, groups, level, pairs, with_laplacian, own, east, west, ne, nw, se, sw):
        place = 16 * (g % 4)
        corners = []
        for message, base in ((ne, 60), (nw, 60), (se, 68), (sw, 68)):
            tile = message[g // 4]
            corners.append(pltpu.roll(tile, (base + 128 - place) & 127, 1))
        corner_masks = [level < d for d in dep.corner_depths]
        self.ring, self.south, self.north, self.lap = {}, {}, {}, {}
        for pair in pairs:
            k_ne, k_nw, k_se, k_sw = [
                masked(m, turn(k, -8 * pair)) for k, m in zip(corners, corner_masks)
            ]
            tile_own, tile_east, tile_west = [m[pair * groups + g] for m in (own, east, west)]
            sides = []
            laps = []
            for q, d_all, k_north, k_south in (
                (jnp.where(dep.column_low, tile_west, tile_own), dep.side_depths[0], k_nw, k_sw),
                (jnp.where(dep.column_low, tile_own, tile_east), dep.side_depths[1], k_ne, k_se),
            ):
                here = level < d_all[0]
                q = masked(here, q)
                sides.append(q)
                if pair in with_laplacian:
                    e, w, n, s = dep.around(q, k_north, k_south)
                    count = sum(jnp.where(level < d, 1.0, 0.0) for d in d_all[1:])
                    laps.append(masked(here, ((e + w) + n) + s - count * q))
            self.ring[pair] = dep.join(*sides)
            self.south[pair] = dep.join(k_sw, k_se)
            self.north[pair] = dep.join(k_nw, k_ne)
            if laps:
                self.lap[pair] = dep.join(*laps)

    def edge(self, pair, j):
        return self.south[pair] if j < 0 else self.north[pair] if j == ROWS else self.ring[pair]


def field_row(ref, north, south, field, groups, g, start, j):
    if j < 0:
        return south[((j + 2) * 4 + field) * groups + g]
    if j >= ROWS:
        return north[((j - ROWS) * 4 + field) * groups + g]
    return ref[pl.ds(start + j, GROUP, stride=ROWS), :]


def prefix(x, sub):
    for by in (1, 2, 4):
        x = x + jnp.where(sub >= by, turn(x, by, 0), 0.0)
    return x


def momentum_kernel(
    levels, lat_total, row0, t, s, u, v, depth, north, south, east, west, own, ne, nw, se, sw,
    u_next, v_next, transport, store, sum_x, sum_y, sum_u, sum_v,
):
    groups = -(-levels // GROUP)
    dep = Depths(groups, store, depth, north, south, east, west, own, ne, nw, se, sw)
    sub = sublanes()
    zero = jnp.zeros(TILE, jnp.float32)
    for r in range(ROWS):
        for ref in (sum_x, sum_y):
            ref[GROUP * r : GROUP * (r + 1), :] = zero
        for ref in (sum_u, sum_v):
            ref[r] = zero
    first_row = row0[0].astype(jnp.float32)

    def body(g, carry):
        first = jnp.minimum(GROUP * g, levels - GROUP)
        start = first * ROWS
        level = (first + sub).astype(jnp.float32)
        fresh = first + sub >= GROUP * g
        last = jnp.where(g == groups - 1, GROUP * (groups - 1) - (levels - GROUP), 0)
        last = GROUP - 1 - last
        edges = Edges(dep, g, groups, level, (0, 1), (1,), own, east, west, ne, nw, se, sw)
        load = functools.partial(field_row, north=north, south=south, groups=groups, g=g, start=start)
        edge_load = edges.ring[0]
        edge_load = turn(edge_load, 64) - edge_load
        wet, q, lap, dens, dens_raw, side = {}, {}, {}, {}, {}, {}
        for j in range(-2, ROWS + 2):
            wet[j] = level < dep.of(j)
            q[j] = [masked(wet[j], load(u, field=2, j=j)), masked(wet[j], load(v, field=3, j=j))]
            if -1 <= j <= ROWS:
                dens[j] = masked(wet[j], load(s, field=1, j=j) - load(t, field=0, j=j))
            i = j - 1
            if i >= -1:
                count = (
                    jnp.where(level < dep.east(i), 1.0, 0.0) + jnp.where(level < dep.west(i), 1.0, 0.0)
                ) + (jnp.where(wet[i + 1], 1.0, 0.0) + jnp.where(wet[i - 1], 1.0, 0.0))
                lap[i] = []
                for f in range(2):
                    e, w = dep.sideways(
                        q[i][f], edges.edge(1, i), f, min(max(i, 0), ROWS - 1)
                    )
                    total = (e + w) + (q[i + 1][f] + q[i - 1][f])
                    lap[i].append((masked(wet[i], total - count * q[i][f]), count))
            r = j - 2
            if r >= 0:
                mixes = []
                for f in range(2):
                    here, count = lap[r][f]
                    e, w = dep.sideways(here, edges.lap[1], f, r)
                    mixes.append((e + w) + (lap[r + 1][f][0] + lap[r - 1][f][0]) - count * here)
                e, w = dep.sideways(dens[r], edge_load, 0, r)
                grad_x = prefix(e - w, sub) + row_of(sum_x, GROUP * r + last)
                grad_y = prefix(dens[r + 1] - dens[r - 1], sub) + row_of(sum_y, GROUP * r + last)
                sum_x[GROUP * r : GROUP * (r + 1), :] = grad_x
                sum_y[GROUP * r : GROUP * (r + 1), :] = grad_y
                turning = TIME_STEP * CORIOLIS * (2.0 * (first_row + (r + 0.5)) / lat_total - 1.0)
                pull = TIME_STEP * 0.5 * SALT_INDEX
                mix = TIME_STEP * MIX_MOMENTUM
                new_u = masked(
                    wet[r], q[r][0] + ((turning * q[r][1] - pull * grad_x) - mix * mixes[0])
                )
                new_v = masked(
                    wet[r], q[r][1] - ((turning * q[r][0] + pull * grad_y) + mix * mixes[1])
                )
                u_next[pl.ds(start + r, GROUP, stride=ROWS), :] = new_u
                v_next[pl.ds(start + r, GROUP, stride=ROWS), :] = new_v
                sum_u[r] += masked(fresh, new_u)
                sum_v[r] += masked(fresh, new_v)
        return carry

    lax.fori_loop(0, groups, body, 0)
    for r in range(ROWS):
        transport[0, r : r + 1, :] = jnp.sum(sum_u[r], axis=0, keepdims=True)
        transport[1, r : r + 1, :] = jnp.sum(sum_v[r], axis=0, keepdims=True)


def tracer_kernel(
    levels, t, s, u, v, depth, north, south, east, west, own, ne, nw, se, sw, t_next, s_next, store
):
    groups = -(-levels // GROUP)
    dep = Depths(groups, store, depth, north, south, east, west, own, ne, nw, se, sw)
    sub = sublanes()

    def body(g, carry):
        first = jnp.minimum(GROUP * g, levels - GROUP)
        start = first * ROWS
        level = (first + sub).astype(jnp.float32)
        edges = Edges(dep, g, groups, level, (0, 1), (0,), own, east, west, ne, nw, se, sw)
        load = functools.partial(field_row, north=north, south=south, groups=groups, g=g, start=start)
        wet, q, sides, lap, flow = {}, {}, {}, {}, {}
        for j in range(-2, ROWS + 2):
            wet[j] = level < dep.of(j)
            q[j] = [masked(wet[j], load(t, field=0, j=j)), masked(wet[j], load(s, field=1, j=j))]
            if -1 <= j <= ROWS:
                flow[j] = [masked(wet[j], load(u, field=2, j=j)), masked(wet[j], load(v, field=3, j=j))]
            i = j - 1
            if i >= -1:
                count = (
                    jnp.where(level < dep.east(i), 1.0, 0.0) + jnp.where(level < dep.west(i), 1.0, 0.0)
                ) + (jnp.where(wet[i + 1], 1.0, 0.0) + jnp.where(wet[i - 1], 1.0, 0.0))
                lap[i], sides[i] = [], []
                for f in range(2):
                    e, w = dep.sideways(
                        q[i][f], edges.edge(0, i), f, min(max(i, 0), ROWS - 1)
                    )
                    sides[i].append((e, w))
                    total = (e + w) + (q[i + 1][f] + q[i - 1][f])
                    lap[i].append((masked(wet[i], total - count * q[i][f]), count))
            r = j - 2
            if r >= 0:
                e, w = dep.sideways(flow[r][0], edges.ring[1], 0, r)
                u_e = masked(level < dep.east(r), flow[r][0] + e)
                u_w = masked(level < dep.west(r), flow[r][0] + w)
                v_n = masked(wet[r + 1], flow[r][1] + flow[r + 1][1])
                v_s = masked(wet[r - 1], flow[r][1] + flow[r - 1][1])
                for f, out in ((0, t_next), (1, s_next)):
                    here, count = lap[r][f]
                    e, w = dep.sideways(here, edges.lap[0], f, r)
                    mix = (e + w) + (lap[r + 1][f][0] + lap[r - 1][f][0]) - count * here
                    mid = q[r][f]
                    e, w = sides[r][f]
                    advected = (u_e * (mid + e) - u_w * (mid + w)) + (
                        v_n * (mid + q[r + 1][f]) - v_s * (mid + q[r - 1][f])
                    )
                    out[pl.ds(start + r, GROUP, stride=ROWS), :] = masked(
                        wet[r],
                        mid - (0.25 * TIME_STEP * advected + TIME_STEP * MIX_TRACER * mix),
                    )
        return carry

    lax.fori_loop(0, groups, body, 0)


PLACES = [(b, c) for b in (-2, -1, 0, 1, 2) for c in (-1, 0, 1)]
STEPS = 5 * ROWS // GROUP


class Plane:
    def __init__(self, own, rim):
        self.own, self.rim = own, rim

    def map(self, other, fn):
        if isinstance(other, Plane):
            return Plane(
                [fn(a, b) for a, b in zip(self.own, other.own)],
                [fn(a, b) for a, b in zip(self.rim, other.rim)],
            )
        return Plane([fn(a, other) for a in self.own], [fn(a, other) for a in self.rim])

    def __add__(self, other):
        return self.map(other, lambda a, b: a + b)

    def __sub__(self, other):
        return self.map(other, lambda a, b: a - b)

    def __mul__(self, other):
        return self.map(other, lambda a, b: a * b)

    def low(self, other):
        return self.map(other, jnp.minimum)

    def side(self, by, lane):
        at = lanes() == lane
        pairs = [(turn(a, by), turn(b, by)) for a, b in zip(self.own, self.rim)]
        return Plane([jnp.where(at, b, a) for a, b in pairs], [jnp.where(at, a, b) for a, b in pairs])

    def east(self):
        return self.side(-1, COLS - 1)

    def west(self):
        return self.side(1, 0)

    def north(self):
        return Plane(*[x[1:] + [turn(x[0], -1, 0)] for x in (self.own, self.rim)])

    def south(self):
        return Plane(*[[turn(x[-1], 1, 0)] + x[:-1] for x in (self.own, self.rim)])


def solve_kernel(levels, *refs):
    count = len(PLACES)
    wide, moved = refs[:count], refs[count : 2 * count]
    offsets = {}
    out = refs[2 * count]
    own_buf, rim_buf = refs[2 * count + 1 :]
    lane = lanes()
    east_half = lane < COLS // 2

    def gather(read):
        for b in range(-2, 3):
            for half in range(2):
                at = ROWS * (b + 2) + GROUP * half
                own_buf[at : at + GROUP, :] = read((b, 0), half)
                rim_buf[at : at + GROUP, :] = jnp.where(
                    east_half, read((b, 1), half), read((b, -1), half)
                )
        return Plane(
            *[[buf[pl.ds(t, GROUP, stride=STEPS), :] for t in range(STEPS)] for buf in (own_buf, rim_buf)]
        )

    def wide_tile(plane):
        def read(place, half):
            ref = wide[PLACES.index(place)]
            return ref[ref.shape[0] - 4 + 2 * plane + half]

        return read

    def moved_tile(plane):
        return lambda place, half: moved[PLACES.index(place)][plane, GROUP * half : GROUP * (half + 1), :]

    depth = gather(wide_tile(0))
    prior = gather(wide_tile(1))
    zonal = gather(moved_tile(0))
    northward = gather(moved_tile(1))

    ocean = depth.map(0.0, lambda a, b: jnp.where(a > b, 1.0, 0.0))
    depth_east, depth_north = depth.low(depth.east()), depth.low(depth.north())
    zonal_flow = zonal.map(depth_east, lambda a, b: masked(b > 0.0, a))
    north_flow = northward.map(depth_north, lambda a, b: masked(b > 0.0, a))
    divergence = (zonal_flow - zonal_flow.west()) + (north_flow - north_flow.south())
    right_side = prior * SURFACE_TERM - divergence * TRANSPORT_SCALE
    east_face, north_face = depth_east * (1.0 / levels), depth_north * (1.0 / levels)
    west_face, south_face = east_face.west(), north_face.south()
    diagonal = (((east_face + west_face) + north_face) + south_face) + SURFACE_TERM
    inverse = diagonal.map(1.0, lambda a, b: b / a)
    right_side, east_face, west_face, north_face, south_face = [
        x * inverse for x in (right_side, east_face, west_face, north_face, south_face)
    ]
    height, change = prior, None
    scales, carries = chebyshev_weights(ITERATIONS)
    for scale, carry in zip(scales, carries):
        spread = (east_face * height.east() + west_face * height.west()) + (
            north_face * height.north() + south_face * height.south()
        )
        residual = (right_side - height) + spread
        step = residual * scale
        change = step if change is None else step + change * carry
        height = height + change
    height = height * ocean
    for t in range(STEPS):
        own_buf[pl.ds(t, GROUP, stride=STEPS), :] = height.own[t]
    out[...] = own_buf[2 * ROWS : 3 * ROWS, :]


def moved_by(value, lat_by, lon_by):
    lat, lon = lax.axis_size("lat"), lax.axis_size("lon")
    pairs = [
        ((i + lat_by) * lon + (j + lon_by) % lon, i * lon + j)
        for i in range(lat)
        if 0 <= i + lat_by < lat
        for j in range(lon)
    ]
    return lax.ppermute(value, ("lat", "lon"), pairs)


def shape(*dims):
    return jax.ShapeDtypeStruct(dims, jnp.float32)


VMEM = pl.BlockSpec(memory_space=pltpu.VMEM)


def call(kernel, outs, scratch, *args, smem=0, cost=0):
    return pl.pallas_call(
        kernel,
        out_shape=outs,
        in_specs=[pl.BlockSpec(memory_space=pltpu.SMEM)] * smem + [VMEM] * (len(args) - smem),
        out_specs=jax.tree.map(lambda _: VMEM, outs),
        scratch_shapes=scratch,
        compiler_params=pltpu.CompilerParams(vmem_limit_bytes=32 * 2**20),
        cost_estimate=pl.CostEstimate(flops=cost, bytes_accessed=4 * 2**20, transcendentals=0),
    )(*args)


def per_device(
    heat_anomaly,
    saltiness_anomaly,
    zonal_current_array,
    meridional_current_array,
    sea_height_prior,
    ocean_layer_number,
):
    levels, rows, cols = heat_anomaly.shape
    groups = -(-levels // GROUP)
    lat_total = rows * lax.axis_size("lat")
    fields = [
        x.reshape(levels * rows, cols)
        for x in (heat_anomaly, saltiness_anomaly, zonal_current_array, meridional_current_array)
    ]
    depth = ocean_layer_number.astype(jnp.float32)
    to_north, to_south, own, corners, wide = call(
        functools.partial(pack_kernel, levels),
        (
            shape(8 * groups + 4, *TILE),
            shape(8 * groups + 4, *TILE),
            shape(2 * groups + 5, *TILE),
            shape(7, *TILE),
            shape(4, *TILE),
        ),
        [],
        *fields,
        depth,
        sea_height_prior,
        cost=10**7,
    )
    north, south = moved_by(to_south, 1, 0), moved_by(to_north, -1, 0)
    east, west = moved_by(own, 0, 1), moved_by(own, 0, -1)
    diagonals = {(i, j): moved_by(corners, i, j) for i in (1, -1) for j in (1, -1)}
    ne, nw, se, sw = (diagonals[p] for p in ((1, 1), (1, -1), (-1, 1), (-1, -1)))
    wides = {(0, 0): wide, (1, 0): north, (-1, 0): south, (0, 1): east, (0, -1): west, **diagonals}
    for i in (2, -2):
        for j in (-1, 0, 1):
            wides[i, j] = moved_by(wide, i, j)

    args = (*fields, depth, north, south, east, west, own, ne, nw, se, sw)
    store = pltpu.VMEM((3 * (ROWS + 4), *TILE), jnp.float32)
    row0 = (lax.axis_index("lat") * rows).astype(jnp.int32).reshape(1)
    u_next, v_next, transport = call(
        functools.partial(momentum_kernel, levels, lat_total),
        (shape(levels * rows, cols), shape(levels * rows, cols), shape(2, rows, cols)),
        [store]
        + [pltpu.VMEM((GROUP * ROWS, COLS), jnp.float32)] * 2
        + [pltpu.VMEM((ROWS, *TILE), jnp.float32)] * 2,
        row0,
        *args,
        smem=1,
        cost=10**7,
    )
    moved = [transport if p == (0, 0) else moved_by(transport, *p) for p in PLACES]
    t_next, s_next = call(
        functools.partial(tracer_kernel, levels),
        (shape(levels * rows, cols), shape(levels * rows, cols)),
        [store],
        *args,
        cost=10**7,
    )
    height = call(
        functools.partial(solve_kernel, levels),
        shape(rows, cols),
        [pltpu.VMEM((5 * ROWS, COLS), jnp.float32)] * 2,
        *[wides[p] for p in PLACES],
        *moved,
        cost=10**7,
    )
    return (
        *[x.reshape(levels, rows, cols) for x in (t_next, s_next, u_next, v_next)],
        height,
    )


def solution(mesh):
    cells, plane = P(None, "lat", "lon"), P("lat", "lon")
    return jax.shard_map(
        per_device,
        mesh=mesh,
        in_specs=(cells,) * 4 + (plane,) * 2,
        out_specs=(cells,) * 4 + (plane,),
        check_vma=False,
    )
```

```python
import functools

import jax
import jax.numpy as jnp
from jax import lax
from jax.experimental import pallas as pl
from jax.experimental.pallas import tpu as pltpu
from jax.sharding import PartitionSpec as P

ITERATIONS = 32

TIME_STEP = 0.1
MIX_TRACER = 0.05
MIX_MOMENTUM = 0.05
HEAT_INDEX = 0.2
SALT_INDEX = 0.2
CORIOLIS = 2.0
SURFACE_TERM = 0.0005
TRANSPORT_SCALE = 0.05

ROWS = 16
COLS = 128
GROUP = 8
GROUPS = 8
TILE = (GROUP, COLS)
PADDED = GROUPS * GROUP * ROWS
HALO = 2 * 4 * GROUPS
PACKS = 2 * GROUPS
SIDE = PACKS + 4
BLOCK = 8
STRIP = 2


def chebyshev_weights(total_steps):
    low_bound = SURFACE_TERM / (SURFACE_TERM + 4.0)
    high_bound = 2.0 - low_bound
    spread_ratio = (high_bound - low_bound) / (high_bound + low_bound)
    middle = 0.5 * (high_bound + low_bound)
    weights = [1.0]
    for number in range(1, total_steps):
        if number == 1:
            weights.append(2.0 / (2.0 - spread_ratio * spread_ratio))
        else:
            weights.append(1.0 / (1.0 - spread_ratio * spread_ratio * weights[-1] / 4.0))
    return [weight / middle for weight in weights], [weight - 1.0 for weight in weights]


def lanes():
    return lax.broadcasted_iota(jnp.int32, TILE, 1)


def sublanes():
    return lax.broadcasted_iota(jnp.int32, TILE, 0)


def turn(value, by, axis=1):
    size = value.shape[axis]
    by = by % size
    return value if by == 0 else pltpu.roll(value, by, axis)


def row_of(ref, row):
    return jnp.broadcast_to(ref[pl.ds(row, 1), :], TILE)


def masked(mask, value):
    return jnp.where(mask, value, 0.0)


def evens():
    return lax.axis_index("lat") % 2 == 0, lax.axis_index("lon") % 2 == 0


def load_kernel(levels, t, s, u, v, depth, t_out, s_out, u_out, v_out, swap_0, swap_1, depth_out, sems):
    lat_even, _ = evens()
    fields, kept = (t, s, u, v), (t_out, s_out, u_out, v_out)
    copies = []
    for part in range(GROUPS // 2):
        first = 2 * GROUP * ROWS * part
        size = min(2 * GROUP * ROWS, levels * ROWS - first)
        for field in range(4):
            span = pl.ds(first, size)
            copies.append(
                pltpu.make_async_copy(
                    fields[field].at[span, :], kept[field].at[span, :], sems.at[4 * part + field]
                )
            )
            copies[-1].start()
    outer = jnp.where(lat_even, ROWS - 2, 0)
    for half in range(2):
        x = depth[GROUP * half : GROUP * (half + 1), :].astype(jnp.float32)
        depth_out[GROUP * half : GROUP * (half + 1), :] = x
        swap_0[HALO + half] = x
        swap_1[HALO + half] = x
    for part in range(GROUPS // 2):
        for field in range(4):
            copies[4 * part + field].wait()
            for g in (2 * part, 2 * part + 1):
                for r in range(2):
                    for swap, row in ((swap_0, outer), (swap_1, ROWS - 2 - outer)):
                        swap[(r * 4 + field) * GROUPS + g] = kept[field][
                            pl.ds(GROUP * ROWS * g + row + r, GROUP, stride=ROWS), :
                        ]


def side_kernel(t, s, u, v, depth, side):
    fields = (t, s, u, v)
    slot = lanes() // 4

    def body(g, carry):
        for pair in range(2):
            pack = jnp.zeros(TILE, jnp.float32)
            for f in range(2):
                for r in range(ROWS):
                    x = fields[2 * pair + f][pl.ds(GROUP * ROWS * g + r, GROUP, stride=ROWS), :]
                    pack = jnp.where(slot == 16 * f + r, turn(x, 64 * f + 4 * r + 2), pack)
            side[pair * GROUPS + g] = pack
        return carry

    lax.fori_loop(0, GROUPS, body, 0)
    pack = jnp.zeros(TILE, jnp.float32)
    for r in range(ROWS):
        x = row_of(depth, r)
        for f in range(2):
            pack = jnp.where(slot == 16 * f + r, turn(x, 64 * f + 4 * r + 2), pack)
    side[PACKS] = pack


def halo_depth(lat_even, swap_0, swap_1, j):
    if j < 0:
        tile, row, first, second = HALO + 1, GROUP + j, swap_1, swap_0
    else:
        tile, row, first, second = HALO, j - ROWS, swap_0, swap_1
    x = jnp.where(lat_even, first[tile, row : row + 1, :], second[tile, row : row + 1, :])
    return jnp.broadcast_to(x, TILE)


def halo_row(lat_even, swap_0, swap_1, field, g, j):
    if j < 0:
        at, first, second = j + 2, swap_1, swap_0
    else:
        at, first, second = j - ROWS, swap_0, swap_1
    index = (at * 4 + field) * GROUPS + g
    return jnp.where(lat_even, first[index], second[index])


def corner_kernel(swap_0, swap_1, side_in, side):
    lat_even, _ = evens()
    slot = lanes() // 4
    side[: PACKS + 1] = side_in[...]
    ends = ((-1, 0), (ROWS, 60))
    for half in range(2):
        pack = jnp.zeros(TILE, jnp.float32)
        for place in range(4):
            for field in range(4):
                for j, end in ends:
                    x = halo_row(lat_even, swap_0, swap_1, field, 4 * half + place, j)
                    base = (16 * place + 8 * (field // 2) + 64 * (field % 2) + end) % COLS
                    pack = jnp.where(slot == base // 4, turn(x, base + 2), pack)
        side[PACKS + 1 + half] = pack
    pack = jnp.zeros(TILE, jnp.float32)
    for j, end in ends:
        x = halo_depth(lat_even, swap_0, swap_1, j)
        for f in range(2):
            base = 64 * f + end
            pack = jnp.where(slot == base // 4, turn(x, base + 2), pack)
    side[PACKS + 3] = pack


class Depths:
    def __init__(self, store, depth, swap_0, swap_1, own, side_0, side_1):
        lane = lanes()
        self.lat_even, self.lon_even = evens()
        self.store, self.lane = store, lane
        self.swaps, self.sides = (swap_0, swap_1), (own, side_0, side_1)
        self.row = (lane // 4) & 15
        self.column_2, self.column_low = (lane & 3) == 2, (lane & 3) < 2
        d_own = own[PACKS]
        d_east, d_west = self.beside(PACKS)
        self.corner_depths = self.beside(PACKS + 3)
        q_west = jnp.where(self.column_low, d_west, d_own)
        q_east = jnp.where(self.column_low, d_own, d_east)
        k_east, k_west = self.corner_depths
        self.side_depths = [
            (q, *self.around(q, k)) for q, k in ((q_west, k_west), (q_east, k_east))
        ]
        ring, corner = self.join(q_west, q_east), self.join(k_west, k_east)
        for j in range(-2, ROWS + 2):
            if 0 <= j < ROWS:
                d = row_of(depth, j)
            else:
                d = halo_depth(self.lat_even, swap_0, swap_1, j)
            store[3 * (j + 2)] = d
            if -1 <= j <= ROWS:
                edge = ring if 0 <= j < ROWS else corner
                d_e, d_w = self.sideways(d, edge, 0, min(max(j, 0), ROWS - 1))
                store[3 * (j + 2) + 1] = d_e
                store[3 * (j + 2) + 2] = d_w

    def beside(self, tile):
        _, first, second = self.sides
        a, b = first[tile], second[tile]
        return jnp.where(self.lon_even, a, b), jnp.where(self.lon_even, b, a)

    def around(self, q, corner):
        north = jnp.where(self.row == ROWS - 1, corner, turn(q, -4))
        south = jnp.where(self.row == 0, corner, turn(q, 4))
        return turn(q, -1), turn(q, 1), north, south

    def join(self, q_west, q_east):
        return jnp.where(self.column_2, q_east, turn(q_west, 2))

    def sideways(self, q, edge, f, r):
        edge = turn(edge, 127 - (64 * f + 4 * r + 2))
        east = jnp.where(self.lane == COLS - 1, edge, turn(q, -1))
        west = jnp.where(self.lane == 0, edge, turn(q, 1))
        return east, west

    def of(self, j):
        return self.store[3 * (j + 2)]

    def east(self, j):
        return self.store[3 * (j + 2) + 1]

    def west(self, j):
        return self.store[3 * (j + 2) + 2]


class Edges:
    def __init__(self, dep, g, level, pairs, with_laplacian):
        place = 16 * (g % 4)
        corners = dep.beside(PACKS + 1 + g // 4)
        corner_masks = [level < d for d in dep.corner_depths]
        self.ring, self.corner, self.lap = {}, {}, {}
        for pair in pairs:
            k_east, k_west = [
                masked(m, pltpu.roll(k, COLS - 8 * pair - place, 1))
                for k, m in zip(corners, corner_masks)
            ]
            tile_own = dep.sides[0][pair * GROUPS + g]
            tile_east, tile_west = dep.beside(pair * GROUPS + g)
            sides, laps = [], []
            for q, d_all, corner in (
                (jnp.where(dep.column_low, tile_west, tile_own), dep.side_depths[0], k_west),
                (jnp.where(dep.column_low, tile_own, tile_east), dep.side_depths[1], k_east),
            ):
                here = level < d_all[0]
                q = masked(here, q)
                sides.append(q)
                if pair in with_laplacian:
                    e, w, n, s = dep.around(q, corner)
                    count = sum(jnp.where(level < d, 1.0, 0.0) for d in d_all[1:])
                    laps.append(masked(here, ((e + w) + n) + s - count * q))
            self.ring[pair] = dep.join(*sides)
            self.corner[pair] = dep.join(k_west, k_east)
            if laps:
                self.lap[pair] = dep.join(*laps)

    def edge(self, pair, j):
        return self.ring[pair] if 0 <= j < ROWS else self.corner[pair]


def field_row(dep, g, ref, field, j):
    if 0 <= j < ROWS:
        return ref[pl.ds(GROUP * ROWS * g + j, GROUP, stride=ROWS), :]
    return halo_row(dep.lat_even, *dep.swaps, field, g, j)


def prefix(x, sub):
    for by in (1, 2, 4):
        x = x + jnp.where(sub >= by, turn(x, by, 0), 0.0)
    return x


def momentum_kernel(
    lat_total, t, s, u, v, depth, prior, swap_0, swap_1, own, side_0, side_1,
    u_next, v_next, block, strip_0, strip_1, store, sum_x, sum_y, sum_u, sum_v,
):
    dep = Depths(store, depth, swap_0, swap_1, own, side_0, side_1)
    sub = sublanes()
    zero = jnp.zeros(TILE, jnp.float32)
    for r in range(ROWS):
        for ref in (sum_x, sum_y):
            ref[GROUP * r : GROUP * (r + 1), :] = zero
        for ref in (sum_u, sum_v):
            ref[r] = zero
    first_row = (lax.axis_index("lat") * ROWS).astype(jnp.float32)

    def body(g, carry):
        start = GROUP * ROWS * g
        level = (GROUP * g + sub).astype(jnp.float32)
        edges = Edges(dep, g, level, (0, 1), (1,))
        load = functools.partial(field_row, dep, g)
        edge_load = edges.ring[0]
        edge_load = turn(edge_load, 64) - edge_load
        wet, q, lap, dens = {}, {}, {}, {}
        for j in range(-2, ROWS + 2):
            wet[j] = level < dep.of(j)
            q[j] = [masked(wet[j], load(u, 2, j)), masked(wet[j], load(v, 3, j))]
            if -1 <= j <= ROWS:
                dens[j] = masked(wet[j], load(s, 1, j) - load(t, 0, j))
            i = j - 1
            if i >= -1:
                count = (
                    jnp.where(level < dep.east(i), 1.0, 0.0) + jnp.where(level < dep.west(i), 1.0, 0.0)
                ) + (jnp.where(wet[i + 1], 1.0, 0.0) + jnp.where(wet[i - 1], 1.0, 0.0))
                lap[i] = []
                for f in range(2):
                    e, w = dep.sideways(q[i][f], edges.edge(1, i), f, min(max(i, 0), ROWS - 1))
                    total = (e + w) + (q[i + 1][f] + q[i - 1][f])
                    lap[i].append((masked(wet[i], total - count * q[i][f]), count))
            r = j - 2
            if r >= 0:
                mixes = []
                for f in range(2):
                    here, count = lap[r][f]
                    e, w = dep.sideways(here, edges.lap[1], f, r)
                    mixes.append((e + w) + (lap[r + 1][f][0] + lap[r - 1][f][0]) - count * here)
                e, w = dep.sideways(dens[r], edge_load, 0, r)
                last = GROUP * r + GROUP - 1
                grad_x = prefix(e - w, sub) + row_of(sum_x, last)
                grad_y = prefix(dens[r + 1] - dens[r - 1], sub) + row_of(sum_y, last)
                sum_x[GROUP * r : GROUP * (r + 1), :] = grad_x
                sum_y[GROUP * r : GROUP * (r + 1), :] = grad_y
                turning = TIME_STEP * CORIOLIS * (2.0 * (first_row + (r + 0.5)) / lat_total - 1.0)
                pull = TIME_STEP * 0.5 * SALT_INDEX
                mix = TIME_STEP * MIX_MOMENTUM
                new_u = masked(
                    wet[r], q[r][0] + ((turning * q[r][1] - pull * grad_x) - mix * mixes[0])
                )
                new_v = masked(
                    wet[r], q[r][1] - ((turning * q[r][0] + pull * grad_y) + mix * mixes[1])
                )
                u_next[pl.ds(start + r, GROUP, stride=ROWS), :] = new_u
                v_next[pl.ds(start + r, GROUP, stride=ROWS), :] = new_v
                sum_u[r] += new_u
                sum_v[r] += new_v
        return carry

    lax.fori_loop(0, GROUPS, body, 0)
    for r in range(ROWS):
        half, row = divmod(r, GROUP)
        block[4 + half, row : row + 1, :] = jnp.sum(sum_u[r], axis=0, keepdims=True)
        block[6 + half, row : row + 1, :] = jnp.sum(sum_v[r], axis=0, keepdims=True)
    quarter = lanes() // 32
    for half in range(2):
        rows = slice(GROUP * half, GROUP * (half + 1))
        block[half] = depth[rows, :]
        block[2 + half] = prior[rows, :]
        planes = [block[2 * plane + half] for plane in range(4)]
        strips = []
        for first in (96, 0):
            strip = zero
            for plane, x in enumerate(planes):
                strip = jnp.where(quarter == plane, turn(x, 32 * plane - first), strip)
            strips.append(strip)
        strip_0[half] = jnp.where(dep.lon_even, strips[0], strips[1])
        strip_1[half] = jnp.where(dep.lon_even, strips[1], strips[0])


def tracer_kernel(
    levels, t, s, u, v, depth, swap_0, swap_1, own, side_0, side_1, u_next, v_next,
    t_out, s_out, u_out, v_out, store, t_next, s_next, sems, sems_flow,
):
    flows = [
        pltpu.make_async_copy(src.at[pl.ds(0, levels * ROWS), :], dst, sems_flow.at[i])
        for i, (src, dst) in enumerate(((u_next, u_out), (v_next, v_out)))
    ]
    for copy in flows:
        copy.start()
    dep = Depths(store, depth, swap_0, swap_1, own, side_0, side_1)
    sub = sublanes()

    def body(g, carry):
        start = GROUP * ROWS * g
        level = (GROUP * g + sub).astype(jnp.float32)
        edges = Edges(dep, g, level, (0, 1), (0,))
        load = functools.partial(field_row, dep, g)
        wet, q, sides, lap, flow = {}, {}, {}, {}, {}
        for j in range(-2, ROWS + 2):
            wet[j] = level < dep.of(j)
            q[j] = [masked(wet[j], load(t, 0, j)), masked(wet[j], load(s, 1, j))]
            if -1 <= j <= ROWS:
                flow[j] = [masked(wet[j], load(u, 2, j)), masked(wet[j], load(v, 3, j))]
            i = j - 1
            if i >= -1:
                count = (
                    jnp.where(level < dep.east(i), 1.0, 0.0) + jnp.where(level < dep.west(i), 1.0, 0.0)
                ) + (jnp.where(wet[i + 1], 1.0, 0.0) + jnp.where(wet[i - 1], 1.0, 0.0))
                lap[i], sides[i] = [], []
                for f in range(2):
                    e, w = dep.sideways(q[i][f], edges.edge(0, i), f, min(max(i, 0), ROWS - 1))
                    sides[i].append((e, w))
                    total = (e + w) + (q[i + 1][f] + q[i - 1][f])
                    lap[i].append((masked(wet[i], total - count * q[i][f]), count))
            r = j - 2
            if r >= 0:
                e, w = dep.sideways(flow[r][0], edges.ring[1], 0, r)
                u_e = masked(level < dep.east(r), flow[r][0] + e)
                u_w = masked(level < dep.west(r), flow[r][0] + w)
                v_n = masked(wet[r + 1], flow[r][1] + flow[r + 1][1])
                v_s = masked(wet[r - 1], flow[r][1] + flow[r - 1][1])
                for f, out in ((0, t_next), (1, s_next)):
                    here, count = lap[r][f]
                    e, w = dep.sideways(here, edges.lap[0], f, r)
                    mix = (e + w) + (lap[r + 1][f][0] + lap[r - 1][f][0]) - count * here
                    mid = q[r][f]
                    e, w = sides[r][f]
                    advected = (u_e * (mid + e) - u_w * (mid + w)) + (
                        v_n * (mid + q[r + 1][f]) - v_s * (mid + q[r - 1][f])
                    )
                    out[pl.ds(start + r, GROUP, stride=ROWS), :] = masked(
                        wet[r],
                        mid - (0.25 * TIME_STEP * advected + TIME_STEP * MIX_TRACER * mix),
                    )
        return carry

    copies = []
    for part in range(GROUPS // 2):
        lax.fori_loop(2 * part, 2 * part + 2, body, 0)
        first = 2 * GROUP * ROWS * part
        span = pl.ds(first, min(2 * GROUP * ROWS, levels * ROWS - first))
        for i, (src, dst) in enumerate(((t_next, t_out), (s_next, s_out))):
            copies.append(
                pltpu.make_async_copy(src.at[span, :], dst.at[span, :], sems.at[2 * part + i])
            )
            copies[-1].start()
    for copy in flows + copies:
        copy.wait()


STEPS = 5 * ROWS // GROUP


class Plane:
    def __init__(self, own, rim):
        self.own, self.rim = own, rim

    def map(self, other, fn):
        if isinstance(other, Plane):
            return Plane(
                [fn(a, b) for a, b in zip(self.own, other.own)],
                [fn(a, b) for a, b in zip(self.rim, other.rim)],
            )
        return Plane([fn(a, other) for a in self.own], [fn(a, other) for a in self.rim])

    def __add__(self, other):
        return self.map(other, lambda a, b: a + b)

    def __sub__(self, other):
        return self.map(other, lambda a, b: a - b)

    def __mul__(self, other):
        return self.map(other, lambda a, b: a * b)

    def low(self, other):
        return self.map(other, jnp.minimum)

    def side(self, by, lane):
        at = lanes() == lane
        pairs = [(turn(a, by), turn(b, by)) for a, b in zip(self.own, self.rim)]
        return Plane([jnp.where(at, b, a) for a, b in pairs], [jnp.where(at, a, b) for a, b in pairs])

    def east(self):
        return self.side(-1, COLS - 1)

    def west(self):
        return self.side(1, 0)

    def north(self):
        return Plane(*[x[1:] + [turn(x[0], -1, 0)] for x in (self.own, self.rim)])

    def south(self):
        return Plane(*[[turn(x[-1], 1, 0)] + x[:-1] for x in (self.own, self.rim)])


def solve_kernel(levels, own, core, chip_0, chip_1, out, own_buf, rim_buf):
    lat_even, lon_even = evens()
    chip_even = lax.axis_index("lat") // 2 % 2 == 0
    lane = lanes()

    def tile(b, index):
        if b == 0:
            return own[index]
        message = BLOCK + 2 * STRIP
        to_first = chip_even if b > 0 else jnp.logical_not(chip_even)
        if abs(b) == 2:
            return jnp.where(to_first, chip_0[index], chip_1[index])
        far = jnp.where(to_first, chip_0[message + index], chip_1[message + index])
        return jnp.where(lat_even if b > 0 else jnp.logical_not(lat_even), core[index], far)

    def gather(plane):
        for b in range(-2, 3):
            for half in range(2):
                at = ROWS * (b + 2) + GROUP * half
                own_buf[at : at + GROUP, :] = tile(b, 2 * plane + half)
                first, second = tile(b, BLOCK + half), tile(b, BLOCK + STRIP + half)
                east = turn(jnp.where(lon_even, first, second), -32 * plane)
                west = turn(jnp.where(lon_even, second, first), 96 - 32 * plane)
                rim_buf[at : at + GROUP, :] = jnp.where(
                    lane < 32, east, jnp.where(lane >= 96, west, 0.0)
                )
        return Plane(
            *[[buf[pl.ds(t, GROUP, stride=STEPS), :] for t in range(STEPS)] for buf in (own_buf, rim_buf)]
        )

    depth, prior, zonal, northward = [gather(plane) for plane in range(4)]

    ocean = depth.map(0.0, lambda a, b: jnp.where(a > b, 1.0, 0.0))
    depth_east, depth_north = depth.low(depth.east()), depth.low(depth.north())
    zonal_flow = zonal.map(depth_east, lambda a, b: masked(b > 0.0, a))
    north_flow = northward.map(depth_north, lambda a, b: masked(b > 0.0, a))
    divergence = (zonal_flow - zonal_flow.west()) + (north_flow - north_flow.south())
    right_side = prior * SURFACE_TERM - divergence * TRANSPORT_SCALE
    east_face, north_face = depth_east * (1.0 / levels), depth_north * (1.0 / levels)
    west_face, south_face = east_face.west(), north_face.south()
    diagonal = (((east_face + west_face) + north_face) + south_face) + SURFACE_TERM
    inverse = diagonal.map(1.0, lambda a, b: b / a)
    right_side, east_face, west_face, north_face, south_face = [
        x * inverse for x in (right_side, east_face, west_face, north_face, south_face)
    ]
    height, change = prior, None
    scales, carries = chebyshev_weights(ITERATIONS)
    for scale, carry in zip(scales, carries):
        spread = (east_face * height.east() + west_face * height.west()) + (
            north_face * height.north() + south_face * height.south()
        )
        residual = (right_side - height) + spread
        step = residual * scale
        change = step if change is None else step + change * carry
        height = height + change
    height = height * ocean
    for t in range(STEPS):
        own_buf[pl.ds(t, GROUP, stride=STEPS), :] = height.own[t]
    out[...] = own_buf[2 * ROWS : 3 * ROWS, :]


def swap(value, axis, partner):
    count = lax.axis_size(axis)
    pairs = [(i, partner(i) % count) for i in range(count) if axis == "lon" or 0 <= partner(i) < count]
    return lax.ppermute(value, axis, pairs)


def even_first(i):
    return i + 1 if i % 2 == 0 else i - 1


def odd_first(i):
    return i - 1 if i % 2 == 0 else i + 1


def chip_even_first(i):
    return i + 2 if i // 2 % 2 == 0 else i - 2


def chip_odd_first(i):
    return i - 2 if i // 2 % 2 == 0 else i + 2


def shape(*dims):
    return jax.ShapeDtypeStruct(dims, jnp.float32)


VMEM = pl.BlockSpec(memory_space=pltpu.VMEM)
HBM = pl.BlockSpec(memory_space=pltpu.HBM)


def call(kernel, outs, scratch, *args, ins=None, out_specs=None, cost=0):
    return pl.pallas_call(
        kernel,
        out_shape=outs,
        in_specs=ins or [VMEM] * len(args),
        out_specs=out_specs or jax.tree.map(lambda _: VMEM, outs),
        scratch_shapes=scratch,
        compiler_params=pltpu.CompilerParams(vmem_limit_bytes=32 * 2**20),
        cost_estimate=pl.CostEstimate(flops=cost, bytes_accessed=4 * 2**20, transcendentals=0),
    )(*args)


def per_device(
    heat_anomaly,
    saltiness_anomaly,
    zonal_current_array,
    meridional_current_array,
    sea_height_prior,
    ocean_layer_number,
):
    levels, rows, cols = heat_anomaly.shape
    lat_total = rows * lax.axis_size("lat")
    fields = [
        x.reshape(levels * rows, cols)
        for x in (heat_anomaly, saltiness_anomaly, zonal_current_array, meridional_current_array)
    ]
    padded, tiles = shape(PADDED, cols), lambda n: shape(n, *TILE)
    *kept, to_0, to_1, depth = call(
        functools.partial(load_kernel, levels),
        (padded,) * 4 + (tiles(HALO + 2), tiles(HALO + 2), shape(rows, cols)),
        [pltpu.SemaphoreType.DMA((2 * GROUPS,))],
        *[pltpu.with_memory_space_constraint(x, pltpu.HBM) for x in fields],
        ocean_layer_number,
        ins=[HBM] * 4 + [VMEM],
        cost=10**6,
    )
    swap_0, swap_1 = swap(to_0, "lat", even_first), swap(to_1, "lat", odd_first)
    side = call(side_kernel, tiles(PACKS + 1), [], *kept, depth, cost=10**7)
    side = call(corner_kernel, tiles(SIDE), [], swap_0, swap_1, side, cost=10**6)
    side_0, side_1 = swap(side, "lon", even_first), swap(side, "lon", odd_first)

    around = (swap_0, swap_1, side, side_0, side_1)
    store = pltpu.VMEM((3 * (ROWS + 4), *TILE), jnp.float32)
    u_next, v_next, block, strip_0, strip_1 = call(
        functools.partial(momentum_kernel, lat_total),
        (padded, padded, tiles(BLOCK), tiles(STRIP), tiles(STRIP)),
        [store]
        + [pltpu.VMEM((GROUP * ROWS, COLS), jnp.float32)] * 2
        + [pltpu.VMEM((ROWS, *TILE), jnp.float32)] * 2,
        *kept,
        depth,
        sea_height_prior,
        *around,
        cost=10**7,
    )
    strips = [swap(strip_0, "lon", even_first), swap(strip_1, "lon", odd_first)]
    own = jnp.concatenate([block, *strips])
    core = swap(own, "lat", even_first)
    chip = jnp.concatenate([own, core])
    chip_0, chip_1 = swap(chip, "lat", chip_even_first), swap(chip, "lat", chip_odd_first)
    out = shape(levels * rows, cols)
    results = call(
        functools.partial(tracer_kernel, levels),
        (out,) * 4,
        [
            store,
            pltpu.VMEM((PADDED, COLS), jnp.float32),
            pltpu.VMEM((PADDED, COLS), jnp.float32),
            pltpu.SemaphoreType.DMA((GROUPS,)),
            pltpu.SemaphoreType.DMA((2,)),
        ],
        *kept,
        depth,
        *around,
        u_next,
        v_next,
        out_specs=(HBM,) * 4,
        cost=10**7,
    )
    height = call(
        functools.partial(solve_kernel, levels),
        shape(rows, cols),
        [pltpu.VMEM((5 * ROWS, COLS), jnp.float32)] * 2,
        own,
        core,
        chip_0,
        chip_1,
        cost=10**7,
    )
    return *[x.reshape(levels, rows, cols) for x in results], height


def solution(mesh):
    cells, plane = P(None, "lat", "lon"), P("lat", "lon")
    return jax.shard_map(
        per_device,
        mesh=mesh,
        in_specs=(cells,) * 4 + (plane,) * 2,
        out_specs=(cells,) * 4 + (plane,),
        check_vma=False,
    )
```

```python
import functools

import jax
import jax.numpy as jnp
from jax import lax
from jax.experimental import pallas as pl
from jax.experimental.pallas import tpu as pltpu
from jax.sharding import PartitionSpec as P

ITERATIONS = 32

TIME_STEP = 0.1
MIX_TRACER = 0.05
MIX_MOMENTUM = 0.05
HEAT_INDEX = 0.2
SALT_INDEX = 0.2
CORIOLIS = 2.0
SURFACE_TERM = 0.0005
TRANSPORT_SCALE = 0.05

ROWS = 16
COLS = 128
GROUP = 8
GROUPS = 8
TILE = (GROUP, COLS)
PADDED = GROUPS * GROUP * ROWS
PARTS = 4
PART = PADDED // PARTS
HALO = 2 * 4 * GROUPS
PACKS = 2 * GROUPS
SIDE = PACKS + 4
BLOCK = 8
STRIP = 2


def chebyshev_weights(total_steps):
    low_bound = SURFACE_TERM / (SURFACE_TERM + 4.0)
    high_bound = 2.0 - low_bound
    spread_ratio = (high_bound - low_bound) / (high_bound + low_bound)
    middle = 0.5 * (high_bound + low_bound)
    weights = [1.0]
    for number in range(1, total_steps):
        if number == 1:
            weights.append(2.0 / (2.0 - spread_ratio * spread_ratio))
        else:
            weights.append(1.0 / (1.0 - spread_ratio * spread_ratio * weights[-1] / 4.0))
    return [weight / middle for weight in weights], [weight - 1.0 for weight in weights]


def lanes():
    return lax.broadcasted_iota(jnp.int32, TILE, 1)


def sublanes():
    return lax.broadcasted_iota(jnp.int32, TILE, 0)


def turn(value, by, axis=1):
    size = value.shape[axis]
    by = by % size
    return value if by == 0 else pltpu.roll(value, by, axis)


def row_of(ref, row):
    return jnp.broadcast_to(ref[pl.ds(row, 1), :], TILE)


def masked(mask, value):
    return jnp.where(mask, value, 0.0)


def evens():
    return lax.axis_index("lat") % 2 == 0, lax.axis_index("lon") % 2 == 0


def load_kernel(
    levels, t, s, u, v, depth_in, prior_in, t_out, s_out, u_out, v_out, swap_0, swap_1, depth_out, prior,
    depth, sems, sems_plane,
):
    lat_even, _ = evens()
    fields, kept = (t, s, u, v), (t_out, s_out, u_out, v_out)
    copies = []
    planes = [
        pltpu.make_async_copy(src, dst, sems_plane.at[i])
        for i, (src, dst) in enumerate(((depth_in, depth), (prior_in, prior)))
    ]
    for copy in planes:
        copy.start()
    for part in range(GROUPS // 2):
        first = 2 * GROUP * ROWS * part
        size = min(2 * GROUP * ROWS, levels * ROWS - first)
        for field in range(4):
            span = pl.ds(first, size)
            copies.append(
                pltpu.make_async_copy(
                    fields[field].at[span, :], kept[field].at[span, :], sems.at[4 * part + field]
                )
            )
            copies[-1].start()
    outer = jnp.where(lat_even, ROWS - 2, 0)
    for copy in planes:
        copy.wait()
    for half in range(2):
        x = depth[GROUP * half : GROUP * (half + 1), :].astype(jnp.float32)
        depth_out[GROUP * half : GROUP * (half + 1), :] = x
        swap_0[HALO + half] = x
        swap_1[HALO + half] = x
    for part in range(GROUPS // 2):
        for field in range(4):
            copies[4 * part + field].wait()
            for g in (2 * part, 2 * part + 1):
                for r in range(2):
                    for swap, row in ((swap_0, outer), (swap_1, ROWS - 2 - outer)):
                        swap[(r * 4 + field) * GROUPS + g] = kept[field][
                            pl.ds(GROUP * ROWS * g + row + r, GROUP, stride=ROWS), :
                        ]


def side_kernel(t, s, u, v, depth, side):
    fields = (t, s, u, v)
    slot = lanes() // 4

    def body(g, carry):
        for pair in range(2):
            pack = jnp.zeros(TILE, jnp.float32)
            for f in range(2):
                for r in range(ROWS):
                    x = fields[2 * pair + f][pl.ds(GROUP * ROWS * g + r, GROUP, stride=ROWS), :]
                    pack = jnp.where(slot == 16 * f + r, turn(x, 64 * f + 4 * r + 2), pack)
            side[pair * GROUPS + g] = pack
        return carry

    lax.fori_loop(0, GROUPS, body, 0)
    pack = jnp.zeros(TILE, jnp.float32)
    for r in range(ROWS):
        x = row_of(depth, r)
        for f in range(2):
            pack = jnp.where(slot == 16 * f + r, turn(x, 64 * f + 4 * r + 2), pack)
    side[PACKS] = pack


def halo_depth(lat_even, swap_0, swap_1, j):
    if j < 0:
        tile, row, first, second = HALO + 1, GROUP + j, swap_1, swap_0
    else:
        tile, row, first, second = HALO, j - ROWS, swap_0, swap_1
    x = jnp.where(lat_even, first[tile, row : row + 1, :], second[tile, row : row + 1, :])
    return jnp.broadcast_to(x, TILE)


def halo_row(lat_even, swap_0, swap_1, field, g, j):
    if j < 0:
        at, first, second = j + 2, swap_1, swap_0
    else:
        at, first, second = j - ROWS, swap_0, swap_1
    index = (at * 4 + field) * GROUPS + g
    return jnp.where(lat_even, first[index], second[index])


def corner_kernel(swap_0, swap_1, side_in, side):
    lat_even, _ = evens()
    slot = lanes() // 4
    side[: PACKS + 1] = side_in[...]
    ends = ((-1, 0), (ROWS, 60))
    for half in range(2):
        pack = jnp.zeros(TILE, jnp.float32)
        for place in range(4):
            for field in range(4):
                for j, end in ends:
                    x = halo_row(lat_even, swap_0, swap_1, field, 4 * half + place, j)
                    base = (16 * place + 8 * (field // 2) + 64 * (field % 2) + end) % COLS
                    pack = jnp.where(slot == base // 4, turn(x, base + 2), pack)
        side[PACKS + 1 + half] = pack
    pack = jnp.zeros(TILE, jnp.float32)
    for j, end in ends:
        x = halo_depth(lat_even, swap_0, swap_1, j)
        for f in range(2):
            base = 64 * f + end
            pack = jnp.where(slot == base // 4, turn(x, base + 2), pack)
    side[PACKS + 3] = pack


class Depths:
    def __init__(self, store, depth, swap_0, swap_1, own, side_0, side_1, build=True):
        lane = lanes()
        self.lat_even, self.lon_even = evens()
        self.store, self.lane = store, lane
        self.swaps, self.sides = (swap_0, swap_1), (own, side_0, side_1)
        self.row = (lane // 4) & 15
        self.column_2, self.column_low = (lane & 3) == 2, (lane & 3) < 2
        d_own = own[PACKS]
        d_east, d_west = self.beside(PACKS)
        self.corner_depths = self.beside(PACKS + 3)
        q_west = jnp.where(self.column_low, d_west, d_own)
        q_east = jnp.where(self.column_low, d_own, d_east)
        k_east, k_west = self.corner_depths
        self.side_depths = [
            (q, *self.around(q, k)) for q, k in ((q_west, k_west), (q_east, k_east))
        ]
        if not build:
            return
        ring, corner = self.join(q_west, q_east), self.join(k_west, k_east)
        for j in range(-2, ROWS + 2):
            if 0 <= j < ROWS:
                d = row_of(depth, j)
            else:
                d = halo_depth(self.lat_even, swap_0, swap_1, j)
            store[3 * (j + 2)] = d
            if -1 <= j <= ROWS:
                edge = ring if 0 <= j < ROWS else corner
                d_e, d_w = self.sideways(d, edge, 0, min(max(j, 0), ROWS - 1))
                store[3 * (j + 2) + 1] = d_e
                store[3 * (j + 2) + 2] = d_w

    def beside(self, tile):
        _, first, second = self.sides
        a, b = first[tile], second[tile]
        return jnp.where(self.lon_even, a, b), jnp.where(self.lon_even, b, a)

    def around(self, q, corner):
        north = jnp.where(self.row == ROWS - 1, corner, turn(q, -4))
        south = jnp.where(self.row == 0, corner, turn(q, 4))
        return turn(q, -1), turn(q, 1), north, south

    def join(self, q_west, q_east):
        return jnp.where(self.column_2, q_east, turn(q_west, 2))

    def sideways(self, q, edge, f, r):
        edge = turn(edge, 127 - (64 * f + 4 * r + 2))
        east = jnp.where(self.lane == COLS - 1, edge, turn(q, -1))
        west = jnp.where(self.lane == 0, edge, turn(q, 1))
        return east, west

    def of(self, j):
        return self.store[3 * (j + 2)]

    def east(self, j):
        return self.store[3 * (j + 2) + 1]

    def west(self, j):
        return self.store[3 * (j + 2) + 2]


class Edges:
    def __init__(self, dep, g, level, pairs, with_laplacian):
        place = 16 * (g % 4)
        corners = dep.beside(PACKS + 1 + g // 4)
        corner_masks = [level < d for d in dep.corner_depths]
        self.ring, self.corner, self.lap = {}, {}, {}
        for pair in pairs:
            k_east, k_west = [
                masked(m, pltpu.roll(k, COLS - 8 * pair - place, 1))
                for k, m in zip(corners, corner_masks)
            ]
            tile_own = dep.sides[0][pair * GROUPS + g]
            tile_east, tile_west = dep.beside(pair * GROUPS + g)
            sides, laps = [], []
            for q, d_all, corner in (
                (jnp.where(dep.column_low, tile_west, tile_own), dep.side_depths[0], k_west),
                (jnp.where(dep.column_low, tile_own, tile_east), dep.side_depths[1], k_east),
            ):
                here = level < d_all[0]
                q = masked(here, q)
                sides.append(q)
                if pair in with_laplacian:
                    e, w, n, s = dep.around(q, corner)
                    count = sum(jnp.where(level < d, 1.0, 0.0) for d in d_all[1:])
                    laps.append(masked(here, ((e + w) + n) + s - count * q))
            self.ring[pair] = dep.join(*sides)
            self.corner[pair] = dep.join(k_west, k_east)
            if laps:
                self.lap[pair] = dep.join(*laps)

    def edge(self, pair, j):
        return self.ring[pair] if 0 <= j < ROWS else self.corner[pair]


def field_row(dep, g, ref, field, j):
    if 0 <= j < ROWS:
        return ref[pl.ds(GROUP * ROWS * g + j, GROUP, stride=ROWS), :]
    return halo_row(dep.lat_even, *dep.swaps, field, g, j)


def prefix(x, sub):
    for by in (1, 2, 4):
        x = x + jnp.where(sub >= by, turn(x, by, 0), 0.0)
    return x


def momentum_kernel(
    lat_total, t, s, u, v, depth, prior, swap_0, swap_1, own, side_0, side_1,
    u_next, v_next, block, strip_0, strip_1, store, sum_x, sum_y, sum_u, sum_v,
):
    dep = Depths(store, depth, swap_0, swap_1, own, side_0, side_1)
    sub = sublanes()
    zero = jnp.zeros(TILE, jnp.float32)
    for r in range(ROWS):
        for ref in (sum_x, sum_y):
            ref[GROUP * r : GROUP * (r + 1), :] = zero
        for ref in (sum_u, sum_v):
            ref[r] = zero
    first_row = (lax.axis_index("lat") * ROWS).astype(jnp.float32)

    def body(g, carry):
        start = GROUP * ROWS * g
        level = (GROUP * g + sub).astype(jnp.float32)
        edges = Edges(dep, g, level, (0, 1), (1,))
        load = functools.partial(field_row, dep, g)
        edge_load = edges.ring[0]
        edge_load = turn(edge_load, 64) - edge_load
        wet, q, lap, dens = {}, {}, {}, {}
        for j in range(-2, ROWS + 2):
            wet[j] = level < dep.of(j)
            q[j] = [masked(wet[j], load(u, 2, j)), masked(wet[j], load(v, 3, j))]
            if -1 <= j <= ROWS:
                dens[j] = masked(wet[j], load(s, 1, j) - load(t, 0, j))
            i = j - 1
            if i >= -1:
                count = (
                    jnp.where(level < dep.east(i), 1.0, 0.0) + jnp.where(level < dep.west(i), 1.0, 0.0)
                ) + (jnp.where(wet[i + 1], 1.0, 0.0) + jnp.where(wet[i - 1], 1.0, 0.0))
                lap[i] = []
                for f in range(2):
                    e, w = dep.sideways(q[i][f], edges.edge(1, i), f, min(max(i, 0), ROWS - 1))
                    total = (e + w) + (q[i + 1][f] + q[i - 1][f])
                    lap[i].append((masked(wet[i], total - count * q[i][f]), count))
            r = j - 2
            if r >= 0:
                mixes = []
                for f in range(2):
                    here, count = lap[r][f]
                    e, w = dep.sideways(here, edges.lap[1], f, r)
                    mixes.append((e + w) + (lap[r + 1][f][0] + lap[r - 1][f][0]) - count * here)
                e, w = dep.sideways(dens[r], edge_load, 0, r)
                last = GROUP * r + GROUP - 1
                grad_x = prefix(e - w, sub) + row_of(sum_x, last)
                grad_y = prefix(dens[r + 1] - dens[r - 1], sub) + row_of(sum_y, last)
                sum_x[GROUP * r : GROUP * (r + 1), :] = grad_x
                sum_y[GROUP * r : GROUP * (r + 1), :] = grad_y
                turning = TIME_STEP * CORIOLIS * (2.0 * (first_row + (r + 0.5)) / lat_total - 1.0)
                pull = TIME_STEP * 0.5 * SALT_INDEX
                mix = TIME_STEP * MIX_MOMENTUM
                new_u = masked(
                    wet[r], q[r][0] + ((turning * q[r][1] - pull * grad_x) - mix * mixes[0])
                )
                new_v = masked(
                    wet[r], q[r][1] - ((turning * q[r][0] + pull * grad_y) + mix * mixes[1])
                )
                u_next[pl.ds(start + r, GROUP, stride=ROWS), :] = new_u
                v_next[pl.ds(start + r, GROUP, stride=ROWS), :] = new_v
                sum_u[r] += new_u
                sum_v[r] += new_v
        return carry

    lax.fori_loop(0, GROUPS, body, 0)
    for r in range(ROWS):
        half, row = divmod(r, GROUP)
        block[4 + half, row : row + 1, :] = jnp.sum(sum_u[r], axis=0, keepdims=True)
        block[6 + half, row : row + 1, :] = jnp.sum(sum_v[r], axis=0, keepdims=True)
    quarter = lanes() // 32
    for half in range(2):
        rows = slice(GROUP * half, GROUP * (half + 1))
        block[half] = depth[rows, :]
        block[2 + half] = prior[rows, :]
        planes = [block[2 * plane + half] for plane in range(4)]
        strips = []
        for first in (96, 0):
            strip = zero
            for plane, x in enumerate(planes):
                strip = jnp.where(quarter == plane, turn(x, 32 * plane - first), strip)
            strips.append(strip)
        strip_0[half] = jnp.where(dep.lon_even, strips[0], strips[1])
        strip_1[half] = jnp.where(dep.lon_even, strips[1], strips[0])


def tracer_kernel(
    part, t, s, u, v, depth, swap_0, swap_1, own, side_0, side_1, store, t_next, s_next
):
    dep = Depths(store, depth, swap_0, swap_1, own, side_0, side_1, build=False)
    sub = sublanes()

    def body(g, carry):
        start = GROUP * ROWS * g
        level = (GROUP * g + sub).astype(jnp.float32)
        edges = Edges(dep, g, level, (0, 1), (0,))
        load = functools.partial(field_row, dep, g)
        wet, q, sides, lap, flow = {}, {}, {}, {}, {}
        for j in range(-2, ROWS + 2):
            wet[j] = level < dep.of(j)
            q[j] = [masked(wet[j], load(t, 0, j)), masked(wet[j], load(s, 1, j))]
            if -1 <= j <= ROWS:
                flow[j] = [masked(wet[j], load(u, 2, j)), masked(wet[j], load(v, 3, j))]
            i = j - 1
            if i >= -1:
                count = (
                    jnp.where(level < dep.east(i), 1.0, 0.0) + jnp.where(level < dep.west(i), 1.0, 0.0)
                ) + (jnp.where(wet[i + 1], 1.0, 0.0) + jnp.where(wet[i - 1], 1.0, 0.0))
                lap[i], sides[i] = [], []
                for f in range(2):
                    e, w = dep.sideways(q[i][f], edges.edge(0, i), f, min(max(i, 0), ROWS - 1))
                    sides[i].append((e, w))
                    total = (e + w) + (q[i + 1][f] + q[i - 1][f])
                    lap[i].append((masked(wet[i], total - count * q[i][f]), count))
            r = j - 2
            if r >= 0:
                e, w = dep.sideways(flow[r][0], edges.ring[1], 0, r)
                u_e = masked(level < dep.east(r), flow[r][0] + e)
                u_w = masked(level < dep.west(r), flow[r][0] + w)
                v_n = masked(wet[r + 1], flow[r][1] + flow[r + 1][1])
                v_s = masked(wet[r - 1], flow[r][1] + flow[r - 1][1])
                for f, out in ((0, t_next), (1, s_next)):
                    here, count = lap[r][f]
                    e, w = dep.sideways(here, edges.lap[0], f, r)
                    mix = (e + w) + (lap[r + 1][f][0] + lap[r - 1][f][0]) - count * here
                    mid = q[r][f]
                    e, w = sides[r][f]
                    advected = (u_e * (mid + e) - u_w * (mid + w)) + (
                        v_n * (mid + q[r + 1][f]) - v_s * (mid + q[r - 1][f])
                    )
                    out[pl.ds(start - PART * part + r, GROUP, stride=ROWS), :] = masked(
                        wet[r],
                        mid - (0.25 * TIME_STEP * advected + TIME_STEP * MIX_TRACER * mix),
                    )
        return carry

    lax.fori_loop(2 * part, 2 * part + 2, body, 0)


STEPS = 5 * ROWS // GROUP


class Plane:
    def __init__(self, own, rim):
        self.own, self.rim = own, rim

    def map(self, other, fn):
        if isinstance(other, Plane):
            return Plane(
                [fn(a, b) for a, b in zip(self.own, other.own)],
                [fn(a, b) for a, b in zip(self.rim, other.rim)],
            )
        return Plane([fn(a, other) for a in self.own], [fn(a, other) for a in self.rim])

    def __add__(self, other):
        return self.map(other, lambda a, b: a + b)

    def __sub__(self, other):
        return self.map(other, lambda a, b: a - b)

    def __mul__(self, other):
        return self.map(other, lambda a, b: a * b)

    def low(self, other):
        return self.map(other, jnp.minimum)

    def side(self, by, lane):
        at = lanes() == lane
        pairs = [(turn(a, by), turn(b, by)) for a, b in zip(self.own, self.rim)]
        return Plane([jnp.where(at, b, a) for a, b in pairs], [jnp.where(at, a, b) for a, b in pairs])

    def east(self):
        return self.side(-1, COLS - 1)

    def west(self):
        return self.side(1, 0)

    def north(self):
        return Plane(*[x[1:] + [turn(x[0], -1, 0)] for x in (self.own, self.rim)])

    def south(self):
        return Plane(*[[turn(x[-1], 1, 0)] + x[:-1] for x in (self.own, self.rim)])


def solve_kernel(levels, own, core, chip_0, chip_1, u_next, v_next, *refs):
    pieces, (t_out, s_out, u_out, v_out, out, own_buf, rim_buf, sems, sems_flow) = refs[:-9], refs[-9:]
    copies = []
    for part in range(PARTS):
        size = min(PART, levels * ROWS - PART * part)
        for i, dst in enumerate((t_out, s_out)):
            copies.append(
                pltpu.make_async_copy(
                    pieces[2 * part + i].at[pl.ds(0, size), :],
                    dst.at[pl.ds(PART * part, size), :],
                    sems.at[2 * part + i],
                )
            )
    for i, (src, dst) in enumerate(((u_next, u_out), (v_next, v_out))):
        copies.append(
            pltpu.make_async_copy(src.at[pl.ds(0, levels * ROWS), :], dst, sems_flow.at[i])
        )
    for copy in copies:
        copy.start()
    lat_even, lon_even = evens()
    chip_even = lax.axis_index("lat") // 2 % 2 == 0
    lane = lanes()

    def tile(b, index):
        if b == 0:
            return own[index]
        message = BLOCK + 2 * STRIP
        to_first = chip_even if b > 0 else jnp.logical_not(chip_even)
        if abs(b) == 2:
            return jnp.where(to_first, chip_0[index], chip_1[index])
        far = jnp.where(to_first, chip_0[message + index], chip_1[message + index])
        return jnp.where(lat_even if b > 0 else jnp.logical_not(lat_even), core[index], far)

    def gather(plane):
        for b in range(-2, 3):
            for half in range(2):
                at = ROWS * (b + 2) + GROUP * half
                own_buf[at : at + GROUP, :] = tile(b, 2 * plane + half)
                first, second = tile(b, BLOCK + half), tile(b, BLOCK + STRIP + half)
                east = turn(jnp.where(lon_even, first, second), -32 * plane)
                west = turn(jnp.where(lon_even, second, first), 96 - 32 * plane)
                rim_buf[at : at + GROUP, :] = jnp.where(
                    lane < 32, east, jnp.where(lane >= 96, west, 0.0)
                )
        return Plane(
            *[[buf[pl.ds(t, GROUP, stride=STEPS), :] for t in range(STEPS)] for buf in (own_buf, rim_buf)]
        )

    depth, prior, zonal, northward = [gather(plane) for plane in range(4)]

    ocean = depth.map(0.0, lambda a, b: jnp.where(a > b, 1.0, 0.0))
    depth_east, depth_north = depth.low(depth.east()), depth.low(depth.north())
    zonal_flow = zonal.map(depth_east, lambda a, b: masked(b > 0.0, a))
    north_flow = northward.map(depth_north, lambda a, b: masked(b > 0.0, a))
    divergence = (zonal_flow - zonal_flow.west()) + (north_flow - north_flow.south())
    right_side = prior * SURFACE_TERM - divergence * TRANSPORT_SCALE
    east_face, north_face = depth_east * (1.0 / levels), depth_north * (1.0 / levels)
    west_face, south_face = east_face.west(), north_face.south()
    diagonal = (((east_face + west_face) + north_face) + south_face) + SURFACE_TERM
    inverse = diagonal.map(1.0, lambda a, b: b / a)
    right_side, east_face, west_face, north_face, south_face = [
        x * inverse for x in (right_side, east_face, west_face, north_face, south_face)
    ]
    height, change = prior, None
    scales, carries = chebyshev_weights(ITERATIONS)
    for scale, carry in zip(scales, carries):
        spread = (east_face * height.east() + west_face * height.west()) + (
            north_face * height.north() + south_face * height.south()
        )
        residual = (right_side - height) + spread
        step = residual * scale
        change = step if change is None else step + change * carry
        height = height + change
    height = height * ocean
    for t in range(STEPS):
        own_buf[pl.ds(t, GROUP, stride=STEPS), :] = height.own[t]
    out[...] = own_buf[2 * ROWS : 3 * ROWS, :]
    for copy in copies:
        copy.wait()


def join_kernel(count, *refs):
    at = 0
    for ref in refs[:count]:
        refs[-1][at : at + ref.shape[0]] = ref[...]
        at += ref.shape[0]


def swap(value, axis, partner):
    count = lax.axis_size(axis)
    pairs = [(i, partner(i) % count) for i in range(count) if axis == "lon" or 0 <= partner(i) < count]
    return lax.ppermute(value, axis, pairs)


def even_first(i):
    return i + 1 if i % 2 == 0 else i - 1


def odd_first(i):
    return i - 1 if i % 2 == 0 else i + 1


def chip_even_first(i):
    return i + 2 if i // 2 % 2 == 0 else i - 2


def chip_odd_first(i):
    return i - 2 if i // 2 % 2 == 0 else i + 2


def shape(*dims):
    return jax.ShapeDtypeStruct(dims, jnp.float32)


VMEM = pl.BlockSpec(memory_space=pltpu.VMEM)
ANY = pl.BlockSpec(memory_space=pl.ANY)
HBM = pl.BlockSpec(memory_space=pltpu.HBM)


def call(kernel, outs, scratch, *args, ins=None, out_specs=None):
    return pl.pallas_call(
        kernel,
        out_shape=outs,
        in_specs=ins or [VMEM] * len(args),
        out_specs=out_specs or jax.tree.map(lambda _: VMEM, outs),
        scratch_shapes=scratch,
        compiler_params=pltpu.CompilerParams(vmem_limit_bytes=32 * 2**20),
        cost_estimate=pl.CostEstimate(flops=0, bytes_accessed=4 * 2**20, transcendentals=0),
    )(*args)


def per_device(
    heat_anomaly,
    saltiness_anomaly,
    zonal_current_array,
    meridional_current_array,
    sea_height_prior,
    ocean_layer_number,
):
    levels, rows, cols = heat_anomaly.shape
    lat_total = rows * lax.axis_size("lat")
    fields = [
        x.reshape(levels * rows, cols)
        for x in (heat_anomaly, saltiness_anomaly, zonal_current_array, meridional_current_array)
    ]
    padded, tiles = shape(PADDED, cols), lambda n: shape(n, *TILE)
    *kept, to_0, to_1, depth, prior = call(
        functools.partial(load_kernel, levels),
        (padded,) * 4 + (tiles(HALO + 2), tiles(HALO + 2), shape(rows, cols), shape(rows, cols)),
        [
            pltpu.VMEM((rows, cols), jnp.int32),
            pltpu.SemaphoreType.DMA((2 * GROUPS,)),
            pltpu.SemaphoreType.DMA((2,)),
        ],
        *[
            pltpu.with_memory_space_constraint(x, pltpu.HBM)
            for x in (*fields, ocean_layer_number, sea_height_prior)
        ],
        ins=[HBM] * 6,
    )
    swap_0, swap_1 = swap(to_0, "lat", even_first), swap(to_1, "lat", odd_first)
    side = call(side_kernel, tiles(PACKS + 1), [], *kept, depth)
    side = call(corner_kernel, tiles(SIDE), [], swap_0, swap_1, side)
    side_0, side_1 = swap(side, "lon", even_first), swap(side, "lon", odd_first)

    around = (swap_0, swap_1, side, side_0, side_1)
    u_next, v_next, block, strip_0, strip_1, store = call(
        functools.partial(momentum_kernel, lat_total),
        (padded, padded, tiles(BLOCK), tiles(STRIP), tiles(STRIP), tiles(3 * (ROWS + 4))),
        [pltpu.VMEM((GROUP * ROWS, COLS), jnp.float32)] * 2
        + [pltpu.VMEM((ROWS, *TILE), jnp.float32)] * 2,
        *kept,
        depth,
        prior,
        *around,
    )
    pieces = []
    for part in range(PARTS):
        pieces += call(
            functools.partial(tracer_kernel, part),
            (shape(PART, cols),) * 2,
            [],
            *kept,
            depth,
            *around,
            store,
        )

    def join(messages, parts):
        made = [piece for part in parts for piece in pieces[2 * part : 2 * part + 2]]
        return call(
            functools.partial(join_kernel, len(messages)),
            tiles(sum(x.shape[0] for x in messages)),
            [],
            *messages,
            *made,
            ins=[VMEM] * len(messages) + [ANY] * len(made),
        )

    strips = [swap(strip_0, "lon", even_first), swap(strip_1, "lon", odd_first)]
    own = join([block, *strips], (0, 1))
    core = swap(own, "lat", even_first)
    chip = join([own, core], (2,))
    chip_0, chip_1 = swap(chip, "lat", chip_even_first), swap(chip, "lat", chip_odd_first)
    out = shape(levels * rows, cols)
    *results, height = call(
        functools.partial(solve_kernel, levels),
        (out,) * 4 + (shape(rows, cols),),
        [pltpu.VMEM((5 * ROWS, COLS), jnp.float32)] * 2
        + [pltpu.SemaphoreType.DMA((2 * PARTS,)), pltpu.SemaphoreType.DMA((2,))],
        own,
        core,
        chip_0,
        chip_1,
        u_next,
        v_next,
        *pieces,
        out_specs=(HBM,) * 4 + (VMEM,),
    )
    return *[x.reshape(levels, rows, cols) for x in results], height


def solution(mesh):
    cells, plane = P(None, "lat", "lon"), P("lat", "lon")
    return jax.shard_map(
        per_device,
        mesh=mesh,
        in_specs=(cells,) * 4 + (plane,) * 2,
        out_specs=(cells,) * 4 + (plane,),
        check_vma=False,
    )
```

```python
import functools

import jax
import jax.numpy as jnp
from jax import lax
from jax.experimental import pallas as pl
from jax.experimental.pallas import tpu as pltpu
from jax.sharding import PartitionSpec as P

ITERATIONS = 32

TIME_STEP = 0.1
MIX_TRACER = 0.05
MIX_MOMENTUM = 0.05
HEAT_INDEX = 0.2
SALT_INDEX = 0.2
CORIOLIS = 2.0
SURFACE_TERM = 0.0005
TRANSPORT_SCALE = 0.05

ROWS = 16
COLS = 128
GROUP = 8
GROUPS = 8
TILE = (GROUP, COLS)
PADDED = GROUPS * GROUP * ROWS
PARTS = 4
PART = PADDED // PARTS
LOADS = 2
HALO = 2 * 4 * GROUPS
PACKS = 2 * GROUPS
SIDE = GROUPS + 1
ROWS_OUT = HALO + 4
BLOCK = 8
STRIP = 2


def chebyshev_weights(total_steps):
    low_bound = SURFACE_TERM / (SURFACE_TERM + 4.0)
    high_bound = 2.0 - low_bound
    spread_ratio = (high_bound - low_bound) / (high_bound + low_bound)
    middle = 0.5 * (high_bound + low_bound)
    weights = [1.0]
    for number in range(1, total_steps):
        if number == 1:
            weights.append(2.0 / (2.0 - spread_ratio * spread_ratio))
        else:
            weights.append(1.0 / (1.0 - spread_ratio * spread_ratio * weights[-1] / 4.0))
    return [weight / middle for weight in weights], [weight - 1.0 for weight in weights]


def lanes():
    return lax.broadcasted_iota(jnp.int32, TILE, 1)


def sublanes():
    return lax.broadcasted_iota(jnp.int32, TILE, 0)


def turn(value, by, axis=1):
    size = value.shape[axis]
    by = by % size
    return value if by == 0 else pltpu.roll(value, by, axis)


def row_of(ref, row):
    return jnp.broadcast_to(ref[pl.ds(row, 1), :], TILE)


def masked(mask, value):
    return jnp.where(mask, value, 0.0)


def place():
    return lax.axis_index("lat"), lax.axis_index("lon")


def evens():
    lat, lon = place()
    return lat % 2 == 0, lon % 2 == 0


def load_kernel(
    levels, t, s, u, v, depth_in, prior_in, t_out, s_out, u_out, v_out, own, side_0, side_1, depth_out,
    prior, depth, sems, sems_plane,
):
    _, lon_even = evens()
    fields, kept = (t, s, u, v), (t_out, s_out, u_out, v_out)
    planes = [
        pltpu.make_async_copy(src, dst, sems_plane.at[i])
        for i, (src, dst) in enumerate(((depth_in, depth), (prior_in, prior)))
    ]
    copies = []
    for part in range(LOADS):
        first = PADDED // LOADS * part
        span = pl.ds(first, min(PADDED // LOADS, levels * ROWS - first))
        for field in range(4):
            copies.append(
                pltpu.make_async_copy(
                    fields[field].at[span, :], kept[field].at[span, :], sems.at[4 * part + field]
                )
            )
    for copy in planes + copies:
        copy.start()
    for copy in planes:
        copy.wait()
    for half in range(2):
        rows = slice(GROUP * half, GROUP * (half + 1))
        depth_out[rows, :] = depth[rows, :].astype(jnp.float32)
    lane = lanes()
    slot, low = lane // 4, (lane & 3) < 2
    pack = jnp.zeros(TILE, jnp.float32)
    for r in range(ROWS):
        x = row_of(depth_out, r)
        for f in range(2):
            pack = jnp.where(slot == 16 * f + r, turn(x, 64 * f + 4 * r + 2), pack)
    own[PACKS] = pack
    side_0[GROUPS] = pack
    side_1[GROUPS] = pack

    def body(g, carry):
        packs = []
        for pair in range(2):
            pack = jnp.zeros(TILE, jnp.float32)
            for f in range(2):
                for r in range(ROWS):
                    x = kept[2 * pair + f][pl.ds(GROUP * ROWS * g + r, GROUP, stride=ROWS), :]
                    pack = jnp.where(slot == 16 * f + r, turn(x, 64 * f + 4 * r + 2), pack)
            own[pair * GROUPS + g] = pack
            packs.append(pack)
        to_east = jnp.where(low, packs[0], turn(packs[1], 2))
        to_west = jnp.where(low, turn(packs[1], -2), packs[0])
        side_0[g] = jnp.where(lon_even, to_east, to_west)
        side_1[g] = jnp.where(lon_even, to_west, to_east)
        return carry

    for part in range(LOADS):
        for copy in copies[4 * part : 4 * part + 4]:
            copy.wait()
        lax.fori_loop(GROUPS // LOADS * part, GROUPS // LOADS * (part + 1), body, 0)


def rows_kernel(t, s, u, v, depth, swap_0, swap_1):
    lat_even, _ = evens()
    fields = (t, s, u, v)
    outer = jnp.where(lat_even, ROWS - 2, 0)

    def body(g, carry):
        for field in range(4):
            for r in range(2):
                for swap, row in ((swap_0, outer), (swap_1, ROWS - 2 - outer)):
                    swap[(r * 4 + field) * GROUPS + g] = fields[field][
                        pl.ds(GROUP * ROWS * g + row + r, GROUP, stride=ROWS), :
                    ]
        return carry

    lax.fori_loop(0, GROUPS, body, 0)
    for half in range(2):
        x = depth[GROUP * half : GROUP * (half + 1), :]
        swap_0[HALO + half] = x
        swap_1[HALO + half] = x


class Around:
    def __init__(self, own, side_0, side_1, swap_0=None, swap_1=None):
        lat, _ = place()
        self.lat_even, self.lon_even = evens()
        self.first, self.final = lat == 0, lat == lax.axis_size("lat") - 1
        lane = lanes()
        self.lane, self.column, self.row = lane, lane & 3, (lane // 4) & 15
        self.low, self.column_2 = self.column < 2, self.column == 2
        self.own, self.sides, self.swaps = own, (side_0, side_1), (swap_0, swap_1)

    def beside(self, tile):
        a, b = self.sides[0][tile], self.sides[1][tile]
        return jnp.where(self.lon_even, a, b), jnp.where(self.lon_even, b, a)

    def beyond(self, north, index):
        a, b = self.swaps if north else self.swaps[::-1]
        return jnp.where(self.lat_even, a[index], b[index])

    def columns(self, pair, g):
        east, west = self.beside(g)
        if pair == 1:
            east, west = turn(east, 2), turn(west, -2)
        own = self.own[pair * GROUPS + g]
        return jnp.where(self.low, west, own), jnp.where(self.low, own, east)

    def depth_columns(self):
        east, west = self.beside(GROUPS)
        own = self.own[PACKS]
        return jnp.where(self.low, west, own), jnp.where(self.low, own, east)

    def corner(self, pair, g):
        at = 4 * (g + GROUPS * pair)
        south = pltpu.roll(self.beyond(False, HALO + 2), (COLS - at) % COLS, 1)
        north = pltpu.roll(self.beyond(True, HALO + 2), (COLS + 60 - at) % COLS, 1)
        return jnp.where(self.row == 0, south, north)

    def corner_depth(self):
        south = jnp.where(self.first, 0.0, self.beyond(False, HALO + 3))
        north = jnp.where(self.final, 0.0, self.beyond(True, HALO + 3))
        return jnp.where(self.row == 0, south, north)

    def row_depth(self, j):
        if j < 0:
            x, outside = self.beyond(False, HALO + 1)[GROUP + j : GROUP + j + 1, :], self.first
        else:
            x, outside = self.beyond(True, HALO)[j - ROWS : j - ROWS + 1, :], self.final
        return jnp.where(outside, 0.0, jnp.broadcast_to(x, TILE))

    def level_row(self, ref, field, g, j):
        if 0 <= j < ROWS:
            return ref[pl.ds(GROUP * ROWS * g + j, GROUP, stride=ROWS), :]
        return self.beyond(j >= ROWS, ((j - ROWS if j >= ROWS else j + 2) * 4 + field) * GROUPS + g)

    def neighbours(self, q, corner):
        north = jnp.where(self.row == ROWS - 1, corner, turn(q, -4))
        south = jnp.where(self.row == 0, corner, turn(q, 4))
        return turn(q, -1), turn(q, 1), north, south

    def join(self, west, east):
        return jnp.where(self.column_2, east, turn(west, 2))

    def sideways(self, q, edge, f, r):
        edge = turn(edge, 127 - (64 * f + 4 * r + 2))
        east = jnp.where(self.lane == COLS - 1, edge, turn(q, -1))
        west = jnp.where(self.lane == 0, edge, turn(q, 1))
        return east, west


def corner_kernel(rows_0, rows_1, own, side_0, side_1, swap_0, swap_1):
    near = Around(own, side_0, side_1)
    slot = near.row
    for swap, rows, upper in (
        (swap_0, rows_0, near.lat_even),
        (swap_1, rows_1, jnp.logical_not(near.lat_even)),
    ):
        swap[: HALO + 2] = rows[...]
        from_row = jnp.where(upper, 4 * (ROWS - 1), 0)
        tile = jnp.zeros(TILE, jnp.float32)
        for pair in range(2):
            for g in range(GROUPS):
                west, east = near.columns(pair, g)
                at = g + GROUPS * pair
                moved = pltpu.roll(jnp.where(near.low, west, east), (4 * at + COLS - from_row) % COLS, 1)
                tile = jnp.where(slot == at, moved, tile)
        swap[HALO + 2] = tile
        west, east = near.depth_columns()
        shift = jnp.where(upper, COLS - 60, 60)
        swap[HALO + 3] = pltpu.roll(jnp.where(near.low, west, east), shift, 1)


class Depths:
    def __init__(self, inner, outer=None):
        self.inner, self.outer = inner, outer

    def tile(self, j, which):
        if 0 <= j < ROWS:
            return self.inner[3 * j + which]
        return self.outer[3 * (j + 2 if j < 0 else j - ROWS + 2) + which]

    def build_inner(self, near, depth):
        ring = near.join(*near.depth_columns())
        for j in range(ROWS):
            d = row_of(depth, j)
            self.inner[3 * j] = d
            self.inner[3 * j + 1], self.inner[3 * j + 2] = near.sideways(d, ring, 0, j)

    def build_outer(self, near):
        corner = near.corner_depth()
        ring = near.join(corner, corner)
        for j in (-2, -1, ROWS, ROWS + 1):
            at = 3 * (j + 2 if j < 0 else j - ROWS + 2)
            d = near.row_depth(j)
            self.outer[at] = d
            d_e, d_w = near.sideways(d, ring, 0, 0 if j < 0 else ROWS - 1)
            self.outer[at + 1], self.outer[at + 2] = d_e, d_w


class Edges:
    def __init__(self, near, g, level, with_laplacian, corners):
        self.ring, self.corner, self.lap = {}, {}, {}
        corner_d = near.corner_depth() if corners else jnp.zeros(TILE, jnp.float32)
        depths = [(d, *near.neighbours(d, corner_d)) for d in near.depth_columns()]
        for pair in range(2):
            corner = jnp.zeros(TILE, jnp.float32)
            if corners:
                corner = masked(level < corner_d, near.corner(pair, g))
            sides, laps = [], []
            for q, d_all in zip(near.columns(pair, g), depths):
                here = level < d_all[0]
                q = masked(here, q)
                sides.append(q)
                if pair in with_laplacian:
                    e, w, n, s = near.neighbours(q, corner)
                    count = sum(jnp.where(level < d, 1.0, 0.0) for d in d_all[1:])
                    laps.append(masked(here, ((e + w) + n) + s - count * q))
            self.ring[pair] = near.join(*sides)
            self.corner[pair] = near.join(corner, corner)
            if laps:
                self.lap[pair] = near.join(*laps)

    def edge(self, pair, j):
        return self.ring[pair] if 0 <= j < ROWS else self.corner[pair]


def prefix(x, sub):
    for by in (1, 2, 4):
        x = x + jnp.where(sub >= by, turn(x, by, 0), 0.0)
    return x


def laplace_row(near, dep, level, wet, q, edges, pair, j):
    count = (
        jnp.where(level < dep.tile(j, 1), 1.0, 0.0) + jnp.where(level < dep.tile(j, 2), 1.0, 0.0)
    ) + (jnp.where(wet[j + 1], 1.0, 0.0) + jnp.where(wet[j - 1], 1.0, 0.0))
    laps, sides = [], []
    for f in range(2):
        e, w = near.sideways(q[j][f], edges.edge(pair, j), f, min(max(j, 0), ROWS - 1))
        sides.append((e, w))
        total = (e + w) + (q[j + 1][f] + q[j - 1][f])
        laps.append(masked(wet[j], total - count * q[j][f]))
    return laps, sides, count


def momentum_levels(
    near, dep, lat_total, windows, corners, t, s, u, v, u_next, v_next, sum_x, sum_y, sum_u, sum_v
):
    sub = sublanes()
    zero = jnp.zeros(TILE, jnp.float32)
    for first, last in windows:
        for r in range(first, last + 1):
            for ref in (sum_x, sum_y):
                ref[GROUP * r : GROUP * (r + 1), :] = zero
            for ref in (sum_u, sum_v):
                ref[r] = zero
    first_row = (place()[0] * ROWS).astype(jnp.float32)

    def body(g, carry):
        start = GROUP * ROWS * g
        level = (GROUP * g + sub).astype(jnp.float32)
        edges = Edges(near, g, level, (1,), corners)
        edge_load = turn(edges.ring[0], 64) - edges.ring[0]
        for first, last in windows:
            wet, q, lap, dens, count = {}, {}, {}, {}, {}
            for j in range(first - 2, last + 3):
                wet[j] = level < dep.tile(j, 0)
                q[j] = [masked(wet[j], near.level_row(ref, i, g, j)) for i, ref in ((2, u), (3, v))]
                if first - 1 <= j <= last + 1:
                    dens[j] = masked(wet[j], near.level_row(s, 1, g, j) - near.level_row(t, 0, g, j))
                if j >= first:
                    lap[j - 1], _, count[j - 1] = laplace_row(near, dep, level, wet, q, edges, 1, j - 1)
                r = j - 2
                if r < first:
                    continue
                mixes = []
                for f in range(2):
                    e, w = near.sideways(lap[r][f], edges.lap[1], f, r)
                    mixes.append((e + w) + (lap[r + 1][f] + lap[r - 1][f]) - count[r] * lap[r][f])
                e, w = near.sideways(dens[r], edge_load, 0, r)
                final = GROUP * r + GROUP - 1
                grad_x = prefix(e - w, sub) + row_of(sum_x, final)
                grad_y = prefix(dens[r + 1] - dens[r - 1], sub) + row_of(sum_y, final)
                sum_x[GROUP * r : GROUP * (r + 1), :] = grad_x
                sum_y[GROUP * r : GROUP * (r + 1), :] = grad_y
                turning = TIME_STEP * CORIOLIS * (2.0 * (first_row + (r + 0.5)) / lat_total - 1.0)
                pull = TIME_STEP * 0.5 * SALT_INDEX
                mix = TIME_STEP * MIX_MOMENTUM
                new_u = masked(
                    wet[r], q[r][0] + ((turning * q[r][1] - pull * grad_x) - mix * mixes[0])
                )
                new_v = masked(
                    wet[r], q[r][1] - ((turning * q[r][0] + pull * grad_y) + mix * mixes[1])
                )
                u_next[pl.ds(start + r, GROUP, stride=ROWS), :] = new_u
                v_next[pl.ds(start + r, GROUP, stride=ROWS), :] = new_v
                sum_u[r] += new_u
                sum_v[r] += new_v
        return carry

    lax.fori_loop(0, GROUPS, body, 0)


def write_sums(windows, sum_u, sum_v, block):
    for first, last in windows:
        for r in range(first, last + 1):
            half, row = divmod(r, GROUP)
            block[half, row : row + 1, :] = jnp.sum(sum_u[r], axis=0, keepdims=True)
            block[2 + half, row : row + 1, :] = jnp.sum(sum_v[r], axis=0, keepdims=True)


INNER = ((2, ROWS - 3),)
OUTER = ((0, 1), (ROWS - 2, ROWS - 1))


def inner_kernel(
    lat_total, t, s, u, v, depth, own, side_0, side_1, u_next, v_next, sums, inner,
    sum_x, sum_y, sum_u, sum_v,
):
    near, dep = Around(own, side_0, side_1), Depths(inner)
    dep.build_inner(near, depth)
    momentum_levels(
        near, dep, lat_total, INNER, False, t, s, u, v, u_next, v_next, sum_x, sum_y, sum_u, sum_v
    )
    sums[...] = jnp.zeros(sums.shape, jnp.float32)
    write_sums(INNER, sum_u, sum_v, sums)


def outer_kernel(
    lat_total, t, s, u, v, depth, prior, own, side_0, side_1, swap_0, swap_1, u_inner, v_inner, sums, inner,
    u_next, v_next, block, strip_0, strip_1, outer, sum_x, sum_y, sum_u, sum_v, total,
):
    near, dep = Around(own, side_0, side_1, swap_0, swap_1), Depths(inner, outer)
    dep.build_outer(near)
    u_next[...] = u_inner[...]
    v_next[...] = v_inner[...]
    total[...] = sums[...]
    momentum_levels(
        near, dep, lat_total, OUTER, True, t, s, u, v, u_next, v_next, sum_x, sum_y, sum_u, sum_v
    )
    write_sums(OUTER, sum_u, sum_v, total)
    quarter = lanes() // 32
    for half in range(2):
        rows = slice(GROUP * half, GROUP * (half + 1))
        planes = [depth[rows, :], prior[rows, :], total[half], total[2 + half]]
        for plane, x in enumerate(planes):
            block[2 * plane + half] = x
        strips = []
        for first in (96, 0):
            strip = jnp.zeros(TILE, jnp.float32)
            for plane, x in enumerate(planes):
                strip = jnp.where(quarter == plane, turn(x, 32 * plane - first), strip)
            strips.append(strip)
        strip_0[half] = jnp.where(near.lon_even, strips[0], strips[1])
        strip_1[half] = jnp.where(near.lon_even, strips[1], strips[0])


def tracer_kernel(
    part, t, s, u, v, own, side_0, side_1, swap_0, swap_1, inner, outer, t_next, s_next
):
    near, dep = Around(own, side_0, side_1, swap_0, swap_1), Depths(inner, outer)
    sub = sublanes()

    def body(g, carry):
        start = GROUP * ROWS * g - PART * part
        level = (GROUP * g + sub).astype(jnp.float32)
        edges = Edges(near, g, level, (0,), True)
        wet, q, sides, lap, flow, count = {}, {}, {}, {}, {}, {}
        for j in range(-2, ROWS + 2):
            wet[j] = level < dep.tile(j, 0)
            q[j] = [masked(wet[j], near.level_row(ref, i, g, j)) for i, ref in ((0, t), (1, s))]
            if -1 <= j <= ROWS:
                flow[j] = [masked(wet[j], near.level_row(ref, i, g, j)) for i, ref in ((2, u), (3, v))]
            if j >= 0:
                lap[j - 1], sides[j - 1], count[j - 1] = laplace_row(
                    near, dep, level, wet, q, edges, 0, j - 1
                )
            r = j - 2
            if r < 0:
                continue
            e, w = near.sideways(flow[r][0], edges.ring[1], 0, r)
            u_e = masked(level < dep.tile(r, 1), flow[r][0] + e)
            u_w = masked(level < dep.tile(r, 2), flow[r][0] + w)
            v_n = masked(wet[r + 1], flow[r][1] + flow[r + 1][1])
            v_s = masked(wet[r - 1], flow[r][1] + flow[r - 1][1])
            for f, out in ((0, t_next), (1, s_next)):
                e, w = near.sideways(lap[r][f], edges.lap[0], f, r)
                mix = (e + w) + (lap[r + 1][f] + lap[r - 1][f]) - count[r] * lap[r][f]
                mid = q[r][f]
                e, w = sides[r][f]
                advected = (u_e * (mid + e) - u_w * (mid + w)) + (
                    v_n * (mid + q[r + 1][f]) - v_s * (mid + q[r - 1][f])
                )
                out[pl.ds(start + r, GROUP, stride=ROWS), :] = masked(
                    wet[r],
                    mid - (0.25 * TIME_STEP * advected + TIME_STEP * MIX_TRACER * mix),
                )
        return carry

    lax.fori_loop(2 * part, 2 * part + 2, body, 0)


def store_kernel(levels, u_next, v_next, *refs):
    pieces, (t_out, s_out, u_out, v_out, stored, sems, sems_flow) = refs[:-7], refs[-7:]
    stored[...] = jnp.zeros(TILE, jnp.float32)
    copies = []
    for i, (src, dst) in enumerate(((u_next, u_out), (v_next, v_out))):
        copies.append(
            pltpu.make_async_copy(src.at[pl.ds(0, levels * ROWS), :], dst, sems_flow.at[i])
        )
    for part in range(PARTS):
        size = min(PART, levels * ROWS - PART * part)
        for i, dst in enumerate((t_out, s_out)):
            copies.append(
                pltpu.make_async_copy(
                    pieces[2 * part + i].at[pl.ds(0, size), :],
                    dst.at[pl.ds(PART * part, size), :],
                    sems.at[2 * part + i],
                )
            )
    for copy in copies:
        copy.start()
    for copy in copies:
        copy.wait()


STEPS = 5 * ROWS // GROUP


class Plane:
    def __init__(self, own, rim):
        self.own, self.rim = own, rim

    def map(self, other, fn):
        if isinstance(other, Plane):
            return Plane(
                [fn(a, b) for a, b in zip(self.own, other.own)],
                [fn(a, b) for a, b in zip(self.rim, other.rim)],
            )
        return Plane([fn(a, other) for a in self.own], [fn(a, other) for a in self.rim])

    def __add__(self, other):
        return self.map(other, lambda a, b: a + b)

    def __sub__(self, other):
        return self.map(other, lambda a, b: a - b)

    def __mul__(self, other):
        return self.map(other, lambda a, b: a * b)

    def low(self, other):
        return self.map(other, jnp.minimum)

    def side(self, by, lane):
        at = lanes() == lane
        pairs = [(turn(a, by), turn(b, by)) for a, b in zip(self.own, self.rim)]
        return Plane([jnp.where(at, b, a) for a, b in pairs], [jnp.where(at, a, b) for a, b in pairs])

    def east(self):
        return self.side(-1, COLS - 1)

    def west(self):
        return self.side(1, 0)

    def north(self):
        return Plane(*[x[1:] + [turn(x[0], -1, 0)] for x in (self.own, self.rim)])

    def south(self):
        return Plane(*[[turn(x[-1], 1, 0)] + x[:-1] for x in (self.own, self.rim)])


def solve_kernel(levels, own, core, chip_0, chip_1, passed, stored, out, own_buf, rim_buf):
    del stored
    lat, _ = place()
    lat_even, lon_even = evens()
    chip_even = lat // 2 % 2 == 0
    lane = lanes()

    def tile(b, index):
        if b == 0:
            return own[index]
        if abs(b) == 2:
            to_first = chip_even if b > 0 else jnp.logical_not(chip_even)
            return jnp.where(to_first, chip_0[index], chip_1[index])
        on_chip = lat_even if b > 0 else jnp.logical_not(lat_even)
        return jnp.where(on_chip, core[index], passed[index])

    def gather(plane):
        for b in range(-2, 3):
            inside = (lat + b >= 0) & (lat + b < lax.axis_size("lat"))
            for half in range(2):
                at = ROWS * (b + 2) + GROUP * half
                mid = tile(b, 2 * plane + half)
                first, second = tile(b, BLOCK + half), tile(b, BLOCK + STRIP + half)
                east = turn(jnp.where(lon_even, first, second), -32 * plane)
                west = turn(jnp.where(lon_even, second, first), 96 - 32 * plane)
                rim = jnp.where(lane < 32, east, jnp.where(lane >= 96, west, 0.0))
                if b != 0:
                    mid, rim = jnp.where(inside, mid, 0.0), jnp.where(inside, rim, 0.0)
                own_buf[at : at + GROUP, :] = mid
                rim_buf[at : at + GROUP, :] = rim
        return Plane(
            *[[buf[pl.ds(t, GROUP, stride=STEPS), :] for t in range(STEPS)] for buf in (own_buf, rim_buf)]
        )

    depth, prior, zonal, northward = [gather(plane) for plane in range(4)]

    ocean = depth.map(0.0, lambda a, b: jnp.where(a > b, 1.0, 0.0))
    depth_east, depth_north = depth.low(depth.east()), depth.low(depth.north())
    zonal_flow = zonal.map(depth_east, lambda a, b: masked(b > 0.0, a))
    north_flow = northward.map(depth_north, lambda a, b: masked(b > 0.0, a))
    divergence = (zonal_flow - zonal_flow.west()) + (north_flow - north_flow.south())
    right_side = prior * SURFACE_TERM - divergence * TRANSPORT_SCALE
    east_face, north_face = depth_east * (1.0 / levels), depth_north * (1.0 / levels)
    west_face, south_face = east_face.west(), north_face.south()
    diagonal = (((east_face + west_face) + north_face) + south_face) + SURFACE_TERM
    inverse = diagonal.map(1.0, lambda a, b: b / a)
    right_side, east_face, west_face, north_face, south_face = [
        x * inverse for x in (right_side, east_face, west_face, north_face, south_face)
    ]
    height, change = prior, None
    scales, carries = chebyshev_weights(ITERATIONS)
    for scale, carry in zip(scales, carries):
        spread = (east_face * height.east() + west_face * height.west()) + (
            north_face * height.north() + south_face * height.south()
        )
        residual = (right_side - height) + spread
        step = residual * scale
        change = step if change is None else step + change * carry
        height = height + change
    height = height * ocean
    for t in range(STEPS):
        own_buf[pl.ds(t, GROUP, stride=STEPS), :] = height.own[t]
    out[...] = own_buf[2 * ROWS : 3 * ROWS, :]


def join_kernel(count, *refs):
    at = 0
    for ref in refs[:count]:
        refs[-1][at : at + ref.shape[0]] = ref[...]
        at += ref.shape[0]


def pass_kernel(chip_0, chip_1, *refs):
    lat, _ = place()
    refs[-1][...] = jnp.where((lat % 2 == 0) == (lat // 2 % 2 == 0), chip_0[...], chip_1[...])


def swap(value, axis, partner):
    count = lax.axis_size(axis)
    return lax.ppermute(value, axis, [(i, partner(i) % count) for i in range(count)])


def even_first(i):
    return i + 1 if i % 2 == 0 else i - 1


def odd_first(i):
    return i - 1 if i % 2 == 0 else i + 1


def chip_even_first(i):
    return i + 2 if i // 2 % 2 == 0 else i - 2


def chip_odd_first(i):
    return i - 2 if i // 2 % 2 == 0 else i + 2


def shape(*dims):
    return jax.ShapeDtypeStruct(dims, jnp.float32)


VMEM = pl.BlockSpec(memory_space=pltpu.VMEM)
ANY = pl.BlockSpec(memory_space=pl.ANY)
HBM = pl.BlockSpec(memory_space=pltpu.HBM)


def call(kernel, outs, scratch, *args, ins=None, out_specs=None):
    return pl.pallas_call(
        kernel,
        out_shape=outs,
        in_specs=ins or [VMEM] * len(args),
        out_specs=out_specs or jax.tree.map(lambda _: VMEM, outs),
        scratch_shapes=scratch,
        compiler_params=pltpu.CompilerParams(vmem_limit_bytes=32 * 2**20),
        cost_estimate=pl.CostEstimate(flops=0, bytes_accessed=4 * 2**20, transcendentals=0),
    )(*args)


def per_device(
    heat_anomaly,
    saltiness_anomaly,
    zonal_current_array,
    meridional_current_array,
    sea_height_prior,
    ocean_layer_number,
):
    levels, rows, cols = heat_anomaly.shape
    lat_total = rows * lax.axis_size("lat")
    fields = [
        x.reshape(levels * rows, cols)
        for x in (heat_anomaly, saltiness_anomaly, zonal_current_array, meridional_current_array)
    ]
    padded, plane = shape(PADDED, cols), shape(rows, cols)

    def tiles(n):
        return shape(n, *TILE)

    *kept, own, to_0, to_1, depth, prior = call(
        functools.partial(load_kernel, levels),
        (padded,) * 4 + (tiles(PACKS + 1), tiles(SIDE), tiles(SIDE), plane, plane),
        [
            pltpu.VMEM((rows, cols), jnp.int32),
            pltpu.SemaphoreType.DMA((4 * LOADS,)),
            pltpu.SemaphoreType.DMA((2,)),
        ],
        *[
            pltpu.with_memory_space_constraint(x, pltpu.HBM)
            for x in (*fields, ocean_layer_number, sea_height_prior)
        ],
        ins=[HBM] * 6,
    )
    sides = (own, swap(to_0, "lon", even_first), swap(to_1, "lon", odd_first))
    rows_0, rows_1 = call(rows_kernel, (tiles(HALO + 2),) * 2, [], *kept, depth)
    to_0, to_1 = call(corner_kernel, (tiles(ROWS_OUT),) * 2, [], rows_0, rows_1, *sides)
    swaps = (swap(to_0, "lat", even_first), swap(to_1, "lat", odd_first))

    scratch = [pltpu.VMEM((GROUP * ROWS, COLS), jnp.float32)] * 2
    scratch += [pltpu.VMEM((ROWS, *TILE), jnp.float32)] * 2
    u_inner, v_inner, sums, inner = call(
        functools.partial(inner_kernel, lat_total),
        (padded, padded, tiles(4), tiles(3 * ROWS)),
        scratch,
        *kept,
        depth,
        *sides,
    )
    u_next, v_next, block, strip_0, strip_1, outer = call(
        functools.partial(outer_kernel, lat_total),
        (padded, padded, tiles(BLOCK), tiles(STRIP), tiles(STRIP), tiles(12)),
        scratch + [pltpu.VMEM((4, *TILE), jnp.float32)],
        *kept,
        depth,
        prior,
        *sides,
        *swaps,
        u_inner,
        v_inner,
        sums,
        inner,
    )
    pieces = []
    for part in range(PARTS):
        pieces += call(
            functools.partial(tracer_kernel, part),
            (shape(PART, cols),) * 2,
            [],
            *kept,
            *sides,
            *swaps,
            inner,
            outer,
        )

    strips = [swap(strip_0, "lon", even_first), swap(strip_1, "lon", odd_first)]
    made = pieces[:4]
    block = call(
        functools.partial(join_kernel, 3),
        tiles(BLOCK + 2 * STRIP),
        [],
        block,
        *strips,
        *made,
        ins=[VMEM] * 3 + [ANY] * len(made),
    )
    chip_0, chip_1 = swap(block, "lat", chip_even_first), swap(block, "lat", chip_odd_first)
    core = swap(block, "lat", even_first)
    made = pieces[4:]
    passed = call(
        pass_kernel,
        tiles(BLOCK + 2 * STRIP),
        [],
        chip_0,
        chip_1,
        *made,
        ins=[VMEM] * 2 + [ANY] * len(made),
    )
    passed = swap(passed, "lat", even_first)
    *results, stored = call(
        functools.partial(store_kernel, levels),
        (shape(levels * rows, cols),) * 4 + (shape(*TILE),),
        [pltpu.SemaphoreType.DMA((2 * PARTS,)), pltpu.SemaphoreType.DMA((2,))],
        u_next,
        v_next,
        *pieces,
        out_specs=(HBM,) * 4 + (VMEM,),
    )
    height = call(
        functools.partial(solve_kernel, levels),
        plane,
        [pltpu.VMEM((5 * ROWS, COLS), jnp.float32)] * 2,
        block,
        core,
        chip_0,
        chip_1,
        passed,
        stored,
        ins=[VMEM] * 5 + [ANY],
    )
    return *[x.reshape(levels, rows, cols) for x in results], height


def solution(mesh):
    cells, plane = P(None, "lat", "lon"), P("lat", "lon")
    return jax.shard_map(
        per_device,
        mesh=mesh,
        in_specs=(cells,) * 4 + (plane,) * 2,
        out_specs=(cells,) * 4 + (plane,),
        check_vma=False,
    )
```

```python
import functools

import jax
import jax.numpy as jnp
from jax import lax
from jax.experimental import pallas as pl
from jax.experimental.pallas import tpu as pltpu
from jax.sharding import PartitionSpec as P

ITERATIONS = 32

TIME_STEP = 0.1
MIX_TRACER = 0.05
MIX_MOMENTUM = 0.05
HEAT_INDEX = 0.2
SALT_INDEX = 0.2
CORIOLIS = 2.0
SURFACE_TERM = 0.0005
TRANSPORT_SCALE = 0.05

ROWS = 16
COLS = 128
GROUP = 8
GROUPS = 8
TILE = (GROUP, COLS)
PADDED = GROUPS * GROUP * ROWS
PARTS = 4
PART = PADDED // PARTS
LOADS = 4
HALO = 2 * 4 * GROUPS
PACKS = 2 * GROUPS
SIDE = GROUPS + 1
ROWS_OUT = HALO + 4
BLOCK = 8
STRIP = 2


def chebyshev_weights(total_steps):
    low_bound = SURFACE_TERM / (SURFACE_TERM + 4.0)
    high_bound = 2.0 - low_bound
    spread_ratio = (high_bound - low_bound) / (high_bound + low_bound)
    middle = 0.5 * (high_bound + low_bound)
    weights = [1.0]
    for number in range(1, total_steps):
        if number == 1:
            weights.append(2.0 / (2.0 - spread_ratio * spread_ratio))
        else:
            weights.append(1.0 / (1.0 - spread_ratio * spread_ratio * weights[-1] / 4.0))
    return [weight / middle for weight in weights], [weight - 1.0 for weight in weights]


def lanes():
    return lax.broadcasted_iota(jnp.int32, TILE, 1)


def sublanes():
    return lax.broadcasted_iota(jnp.int32, TILE, 0)


def turn(value, by, axis=1):
    size = value.shape[axis]
    by = by % size
    return value if by == 0 else pltpu.roll(value, by, axis)


def row_of(ref, row):
    return jnp.broadcast_to(ref[pl.ds(row, 1), :], TILE)


def masked(mask, value):
    return jnp.where(mask, value, 0.0)


def place():
    return lax.axis_index("lat"), lax.axis_index("lon")


def evens():
    lat, lon = place()
    return lat % 2 == 0, lon % 2 == 0


def load_kernel(
    levels, t, s, u, v, depth_in, prior_in, t_out, s_out, u_out, v_out, own, side_0, side_1, depth_out,
    prior, depth, sems, sems_plane,
):
    _, lon_even = evens()
    fields, kept = (t, s, u, v), (t_out, s_out, u_out, v_out)
    planes = [
        pltpu.make_async_copy(src, dst, sems_plane.at[i])
        for i, (src, dst) in enumerate(((depth_in, depth), (prior_in, prior)))
    ]
    copies = []
    for part in range(LOADS):
        first = PADDED // LOADS * part
        span = pl.ds(first, min(PADDED // LOADS, levels * ROWS - first))
        for field in range(4):
            copies.append(
                pltpu.make_async_copy(
                    fields[field].at[span, :], kept[field].at[span, :], sems.at[4 * part + field]
                )
            )
    for copy in planes + copies:
        copy.start()
    for copy in planes:
        copy.wait()
    for half in range(2):
        rows = slice(GROUP * half, GROUP * (half + 1))
        depth_out[rows, :] = depth[rows, :].astype(jnp.float32)
    lane = lanes()
    slot, low = lane // 4, (lane & 3) < 2
    pack = jnp.zeros(TILE, jnp.float32)
    for r in range(ROWS):
        x = row_of(depth_out, r)
        for f in range(2):
            pack = jnp.where(slot == 16 * f + r, turn(x, 64 * f + 4 * r + 2), pack)
    own[PACKS] = pack
    side_0[GROUPS] = pack
    side_1[GROUPS] = pack

    def body(g, carry):
        packs = []
        for pair in range(2):
            pack = jnp.zeros(TILE, jnp.float32)
            for f in range(2):
                for r in range(ROWS):
                    x = kept[2 * pair + f][pl.ds(GROUP * ROWS * g + r, GROUP, stride=ROWS), :]
                    pack = jnp.where(slot == 16 * f + r, turn(x, 64 * f + 4 * r + 2), pack)
            own[pair * GROUPS + g] = pack
            packs.append(pack)
        to_east = jnp.where(low, packs[0], turn(packs[1], 2))
        to_west = jnp.where(low, turn(packs[1], -2), packs[0])
        side_0[g] = jnp.where(lon_even, to_east, to_west)
        side_1[g] = jnp.where(lon_even, to_west, to_east)
        return carry

    for part in range(LOADS):
        for copy in copies[4 * part : 4 * part + 4]:
            copy.wait()
        lax.fori_loop(GROUPS // LOADS * part, GROUPS // LOADS * (part + 1), body, 0)


def rows_kernel(t, s, u, v, depth, swap_0, swap_1):
    lat_even, _ = evens()
    fields = (t, s, u, v)
    outer = jnp.where(lat_even, ROWS - 2, 0)

    def body(g, carry):
        for field in range(4):
            for r in range(2):
                for swap, row in ((swap_0, outer), (swap_1, ROWS - 2 - outer)):
                    swap[(r * 4 + field) * GROUPS + g] = fields[field][
                        pl.ds(GROUP * ROWS * g + row + r, GROUP, stride=ROWS), :
                    ]
        return carry

    lax.fori_loop(0, GROUPS, body, 0)
    for half in range(2):
        x = depth[GROUP * half : GROUP * (half + 1), :]
        swap_0[HALO + half] = x
        swap_1[HALO + half] = x


class Around:
    def __init__(self, own, side_0, side_1, swap_0=None, swap_1=None):
        lat, _ = place()
        self.lat_even, self.lon_even = evens()
        self.first, self.final = lat == 0, lat == lax.axis_size("lat") - 1
        lane = lanes()
        self.lane, self.column, self.row = lane, lane & 3, (lane // 4) & 15
        self.low, self.column_2 = self.column < 2, self.column == 2
        self.own, self.sides, self.swaps = own, (side_0, side_1), (swap_0, swap_1)

    def beside(self, tile):
        a, b = self.sides[0][tile], self.sides[1][tile]
        return jnp.where(self.lon_even, a, b), jnp.where(self.lon_even, b, a)

    def beyond(self, north, index):
        a, b = self.swaps if north else self.swaps[::-1]
        return jnp.where(self.lat_even, a[index], b[index])

    def columns(self, pair, g):
        east, west = self.beside(g)
        if pair == 1:
            east, west = turn(east, 2), turn(west, -2)
        own = self.own[pair * GROUPS + g]
        return jnp.where(self.low, west, own), jnp.where(self.low, own, east)

    def depth_columns(self):
        east, west = self.beside(GROUPS)
        own = self.own[PACKS]
        return jnp.where(self.low, west, own), jnp.where(self.low, own, east)

    def corner(self, pair, g):
        at = 4 * (g + GROUPS * pair)
        south = pltpu.roll(self.beyond(False, HALO + 2), (COLS - at) % COLS, 1)
        north = pltpu.roll(self.beyond(True, HALO + 2), (COLS + 60 - at) % COLS, 1)
        return jnp.where(self.row == 0, south, north)

    def corner_depth(self):
        south = jnp.where(self.first, 0.0, self.beyond(False, HALO + 3))
        north = jnp.where(self.final, 0.0, self.beyond(True, HALO + 3))
        return jnp.where(self.row == 0, south, north)

    def row_depth(self, j):
        if j < 0:
            x, outside = self.beyond(False, HALO + 1)[GROUP + j : GROUP + j + 1, :], self.first
        else:
            x, outside = self.beyond(True, HALO)[j - ROWS : j - ROWS + 1, :], self.final
        return jnp.where(outside, 0.0, jnp.broadcast_to(x, TILE))

    def level_row(self, ref, field, g, j):
        if 0 <= j < ROWS:
            return ref[pl.ds(GROUP * ROWS * g + j, GROUP, stride=ROWS), :]
        return self.beyond(j >= ROWS, ((j - ROWS if j >= ROWS else j + 2) * 4 + field) * GROUPS + g)

    def neighbours(self, q, corner):
        north = jnp.where(self.row == ROWS - 1, corner, turn(q, -4))
        south = jnp.where(self.row == 0, corner, turn(q, 4))
        return turn(q, -1), turn(q, 1), north, south

    def join(self, west, east):
        return jnp.where(self.column_2, east, turn(west, 2))

    def sideways(self, q, edge, f, r):
        edge = turn(edge, 127 - (64 * f + 4 * r + 2))
        east = jnp.where(self.lane == COLS - 1, edge, turn(q, -1))
        west = jnp.where(self.lane == 0, edge, turn(q, 1))
        return east, west


def corner_kernel(rows_0, rows_1, own, side_0, side_1, swap_0, swap_1):
    near = Around(own, side_0, side_1)
    slot = near.row
    for swap, rows, upper in (
        (swap_0, rows_0, near.lat_even),
        (swap_1, rows_1, jnp.logical_not(near.lat_even)),
    ):
        swap[: HALO + 2] = rows[...]
        from_row = jnp.where(upper, 4 * (ROWS - 1), 0)
        tile = jnp.zeros(TILE, jnp.float32)
        for pair in range(2):
            for g in range(GROUPS):
                west, east = near.columns(pair, g)
                at = g + GROUPS * pair
                moved = pltpu.roll(jnp.where(near.low, west, east), (4 * at + COLS - from_row) % COLS, 1)
                tile = jnp.where(slot == at, moved, tile)
        swap[HALO + 2] = tile
        west, east = near.depth_columns()
        shift = jnp.where(upper, COLS - 60, 60)
        swap[HALO + 3] = pltpu.roll(jnp.where(near.low, west, east), shift, 1)


class Depths:
    def __init__(self, inner, outer=None):
        self.inner, self.outer = inner, outer

    def tile(self, j, which):
        if 0 <= j < ROWS:
            return self.inner[3 * j + which]
        return self.outer[3 * (j + 2 if j < 0 else j - ROWS + 2) + which]

    def build_inner(self, near, depth):
        ring = near.join(*near.depth_columns())
        for j in range(ROWS):
            d = row_of(depth, j)
            self.inner[3 * j] = d
            self.inner[3 * j + 1], self.inner[3 * j + 2] = near.sideways(d, ring, 0, j)

    def build_outer(self, near):
        corner = near.corner_depth()
        ring = near.join(corner, corner)
        for j in (-2, -1, ROWS, ROWS + 1):
            at = 3 * (j + 2 if j < 0 else j - ROWS + 2)
            d = near.row_depth(j)
            self.outer[at] = d
            d_e, d_w = near.sideways(d, ring, 0, 0 if j < 0 else ROWS - 1)
            self.outer[at + 1], self.outer[at + 2] = d_e, d_w


class Edges:
    def __init__(self, near, g, level, with_laplacian, corners):
        self.ring, self.corner, self.lap = {}, {}, {}
        corner_d = near.corner_depth() if corners else jnp.zeros(TILE, jnp.float32)
        depths = [(d, *near.neighbours(d, corner_d)) for d in near.depth_columns()]
        for pair in range(2):
            corner = jnp.zeros(TILE, jnp.float32)
            if corners:
                corner = masked(level < corner_d, near.corner(pair, g))
            sides, laps = [], []
            for q, d_all in zip(near.columns(pair, g), depths):
                here = level < d_all[0]
                q = masked(here, q)
                sides.append(q)
                if pair in with_laplacian:
                    e, w, n, s = near.neighbours(q, corner)
                    count = sum(jnp.where(level < d, 1.0, 0.0) for d in d_all[1:])
                    laps.append(masked(here, ((e + w) + n) + s - count * q))
            self.ring[pair] = near.join(*sides)
            self.corner[pair] = near.join(corner, corner)
            if laps:
                self.lap[pair] = near.join(*laps)

    def edge(self, pair, j):
        return self.ring[pair] if 0 <= j < ROWS else self.corner[pair]


def prefix(x, sub):
    for by in (1, 2, 4):
        x = x + jnp.where(sub >= by, turn(x, by, 0), 0.0)
    return x


def wet_sides(dep, level, wet, j):
    return (
        jnp.where(level < dep.tile(j, 1), 1.0, 0.0) + jnp.where(level < dep.tile(j, 2), 1.0, 0.0)
    ) + (jnp.where(wet[j + 1], 1.0, 0.0) + jnp.where(wet[j - 1], 1.0, 0.0))


def laplace_row(near, dep, level, wet, q, edges, pair, j):
    count = wet_sides(dep, level, wet, j)
    laps, sides = [], []
    for f in range(2):
        e, w = near.sideways(q[j][f], edges.edge(pair, j), f, min(max(j, 0), ROWS - 1))
        sides.append((e, w))
        total = (e + w) + (q[j + 1][f] + q[j - 1][f])
        laps.append(masked(wet[j], total - count * q[j][f]))
    return laps, sides, count


def momentum_levels(
    near, dep, lat_total, windows, corners, t, s, u, v, write, kept, sum_x, sum_y, sum_u, sum_v
):
    sub = sublanes()
    zero = jnp.zeros(TILE, jnp.float32)
    for first, last in windows:
        for r in range(first, last + 1):
            for ref in (sum_x, sum_y):
                ref[GROUP * r : GROUP * (r + 1), :] = zero
            for ref in (sum_u, sum_v):
                ref[r] = zero
    first_row = (place()[0] * ROWS).astype(jnp.float32)

    def body(g, carry):
        level = (GROUP * g + sub).astype(jnp.float32)
        edges = Edges(near, g, level, (1,), corners)
        edge_load = turn(edges.ring[0], 64) - edges.ring[0]
        for first, last in windows:
            wet, q, lap, dens, count = {}, {}, {}, {}, {}
            for j in range(first - 2, last + 3):
                if not corners or j not in (3, ROWS - 4):
                    wet[j] = level < dep.tile(j, 0)
                    q[j] = [masked(wet[j], near.level_row(ref, i, g, j)) for i, ref in ((2, u), (3, v))]
                if first - 1 <= j <= last + 1:
                    dens[j] = masked(wet[j], near.level_row(s, 1, g, j) - near.level_row(t, 0, g, j))
                i = j - 1
                if j >= first:
                    if corners and i in KEPT:
                        lap[i] = [kept[KEPT.index(i) * 2 + f, g] for f in range(2)]
                        if first <= i <= last:
                            count[i] = wet_sides(dep, level, wet, i)
                    else:
                        lap[i], _, count[i] = laplace_row(near, dep, level, wet, q, edges, 1, i)
                        if not corners and i in KEPT:
                            for f in range(2):
                                kept[KEPT.index(i) * 2 + f, g] = lap[i][f]
                r = j - 2
                if r < first:
                    continue
                mixes = []
                for f in range(2):
                    e, w = near.sideways(lap[r][f], edges.lap[1], f, r)
                    mixes.append((e + w) + (lap[r + 1][f] + lap[r - 1][f]) - count[r] * lap[r][f])
                e, w = near.sideways(dens[r], edge_load, 0, r)
                final = GROUP * r + GROUP - 1
                grad_x = prefix(e - w, sub) + row_of(sum_x, final)
                grad_y = prefix(dens[r + 1] - dens[r - 1], sub) + row_of(sum_y, final)
                sum_x[GROUP * r : GROUP * (r + 1), :] = grad_x
                sum_y[GROUP * r : GROUP * (r + 1), :] = grad_y
                turning = TIME_STEP * CORIOLIS * (2.0 * (first_row + (r + 0.5)) / lat_total - 1.0)
                pull = TIME_STEP * 0.5 * SALT_INDEX
                mix = TIME_STEP * MIX_MOMENTUM
                new_u = masked(
                    wet[r], q[r][0] + ((turning * q[r][1] - pull * grad_x) - mix * mixes[0])
                )
                new_v = masked(
                    wet[r], q[r][1] - ((turning * q[r][0] + pull * grad_y) + mix * mixes[1])
                )
                write(g, r, new_u, new_v)
                sum_u[r] += new_u
                sum_v[r] += new_v
        return carry

    lax.fori_loop(0, GROUPS, body, 0)


def write_sums(windows, sum_u, sum_v, block):
    for first, last in windows:
        for r in range(first, last + 1):
            half, row = divmod(r, GROUP)
            block[half, row : row + 1, :] = jnp.sum(sum_u[r], axis=0, keepdims=True)
            block[2 + half, row : row + 1, :] = jnp.sum(sum_v[r], axis=0, keepdims=True)


INNER = ((2, ROWS - 3),)
OUTER = ((0, 1), (ROWS - 2, ROWS - 1))
OUTER_ROWS = (0, 1, ROWS - 2, ROWS - 1)
KEPT = (1, 2, ROWS - 3, ROWS - 2)


def inner_kernel(
    lat_total, t, s, u, v, depth, own, side_0, side_1, u_next, v_next, sums, inner, kept,
    sum_x, sum_y, sum_u, sum_v,
):
    near, dep = Around(own, side_0, side_1), Depths(inner)
    dep.build_inner(near, depth)

    def write(g, r, new_u, new_v):
        rows = pl.ds(GROUP * ROWS * g + r, GROUP, stride=ROWS)
        u_next[rows, :] = new_u
        v_next[rows, :] = new_v

    momentum_levels(
        near, dep, lat_total, INNER, False, t, s, u, v, write, kept, sum_x, sum_y, sum_u, sum_v
    )
    sums[...] = jnp.zeros(sums.shape, jnp.float32)
    write_sums(INNER, sum_u, sum_v, sums)


def outer_kernel(
    lat_total, t, s, u, v, depth, prior, own, side_0, side_1, swap_0, swap_1, sums, inner, kept,
    u_outer, v_outer, block, strip_0, strip_1, outer, sum_x, sum_y, sum_u, sum_v, total,
):
    near, dep = Around(own, side_0, side_1, swap_0, swap_1), Depths(inner, outer)
    dep.build_outer(near)
    total[...] = sums[...]

    def write(g, r, new_u, new_v):
        u_outer[OUTER_ROWS.index(r), g] = new_u
        v_outer[OUTER_ROWS.index(r), g] = new_v

    momentum_levels(
        near, dep, lat_total, OUTER, True, t, s, u, v, write, kept, sum_x, sum_y, sum_u, sum_v
    )
    write_sums(OUTER, sum_u, sum_v, total)
    quarter = lanes() // 32
    for half in range(2):
        rows = slice(GROUP * half, GROUP * (half + 1))
        planes = [depth[rows, :], prior[rows, :], total[half], total[2 + half]]
        for plane, x in enumerate(planes):
            block[2 * plane + half] = x
        strips = []
        for first in (96, 0):
            strip = jnp.zeros(TILE, jnp.float32)
            for plane, x in enumerate(planes):
                strip = jnp.where(quarter == plane, turn(x, 32 * plane - first), strip)
            strips.append(strip)
        strip_0[half] = jnp.where(near.lon_even, strips[0], strips[1])
        strip_1[half] = jnp.where(near.lon_even, strips[1], strips[0])


def merge_kernel(u_inner, v_inner, u_outer, v_outer, u_next, v_next):
    for inner, outer, out in ((u_inner, u_outer, u_next), (v_inner, v_outer, v_next)):
        out[...] = inner[...]
        for g in range(GROUPS):
            for i, r in enumerate(OUTER_ROWS):
                out[pl.ds(GROUP * ROWS * g + r, GROUP, stride=ROWS), :] = outer[i, g]


def tracer_kernel(
    part, t, s, u, v, own, side_0, side_1, swap_0, swap_1, inner, outer, t_next, s_next
):
    near, dep = Around(own, side_0, side_1, swap_0, swap_1), Depths(inner, outer)
    sub = sublanes()

    def body(g, carry):
        start = GROUP * ROWS * g - PART * part
        level = (GROUP * g + sub).astype(jnp.float32)
        edges = Edges(near, g, level, (0,), True)
        wet, q, sides, lap, flow, count = {}, {}, {}, {}, {}, {}
        for j in range(-2, ROWS + 2):
            wet[j] = level < dep.tile(j, 0)
            q[j] = [masked(wet[j], near.level_row(ref, i, g, j)) for i, ref in ((0, t), (1, s))]
            if -1 <= j <= ROWS:
                flow[j] = [masked(wet[j], near.level_row(ref, i, g, j)) for i, ref in ((2, u), (3, v))]
            if j >= 0:
                lap[j - 1], sides[j - 1], count[j - 1] = laplace_row(
                    near, dep, level, wet, q, edges, 0, j - 1
                )
            r = j - 2
            if r < 0:
                continue
            e, w = near.sideways(flow[r][0], edges.ring[1], 0, r)
            u_e = masked(level < dep.tile(r, 1), flow[r][0] + e)
            u_w = masked(level < dep.tile(r, 2), flow[r][0] + w)
            v_n = masked(wet[r + 1], flow[r][1] + flow[r + 1][1])
            v_s = masked(wet[r - 1], flow[r][1] + flow[r - 1][1])
            for f, out in ((0, t_next), (1, s_next)):
                e, w = near.sideways(lap[r][f], edges.lap[0], f, r)
                mix = (e + w) + (lap[r + 1][f] + lap[r - 1][f]) - count[r] * lap[r][f]
                mid = q[r][f]
                e, w = sides[r][f]
                advected = (u_e * (mid + e) - u_w * (mid + w)) + (
                    v_n * (mid + q[r + 1][f]) - v_s * (mid + q[r - 1][f])
                )
                out[pl.ds(start + r, GROUP, stride=ROWS), :] = masked(
                    wet[r],
                    mid - (0.25 * TIME_STEP * advected + TIME_STEP * MIX_TRACER * mix),
                )
        return carry

    lax.fori_loop(2 * part, 2 * part + 2, body, 0)


def store_kernel(levels, u_next, v_next, *refs):
    pieces, (t_out, s_out, u_out, v_out, stored, sems, sems_flow) = refs[:-7], refs[-7:]
    stored[...] = jnp.zeros(TILE, jnp.float32)
    copies = []
    for i, (src, dst) in enumerate(((u_next, u_out), (v_next, v_out))):
        copies.append(
            pltpu.make_async_copy(src.at[pl.ds(0, levels * ROWS), :], dst, sems_flow.at[i])
        )
    for part in range(PARTS):
        size = min(PART, levels * ROWS - PART * part)
        for i, dst in enumerate((t_out, s_out)):
            copies.append(
                pltpu.make_async_copy(
                    pieces[2 * part + i].at[pl.ds(0, size), :],
                    dst.at[pl.ds(PART * part, size), :],
                    sems.at[2 * part + i],
                )
            )
    for copy in copies:
        copy.start()
    for copy in copies:
        copy.wait()


STEPS = 5 * ROWS // GROUP


class Plane:
    def __init__(self, own, rim):
        self.own, self.rim = own, rim

    def map(self, other, fn):
        if isinstance(other, Plane):
            return Plane(
                [fn(a, b) for a, b in zip(self.own, other.own)],
                [fn(a, b) for a, b in zip(self.rim, other.rim)],
            )
        return Plane([fn(a, other) for a in self.own], [fn(a, other) for a in self.rim])

    def __add__(self, other):
        return self.map(other, lambda a, b: a + b)

    def __sub__(self, other):
        return self.map(other, lambda a, b: a - b)

    def __mul__(self, other):
        return self.map(other, lambda a, b: a * b)

    def low(self, other):
        return self.map(other, jnp.minimum)

    def side(self, by, lane):
        at = lanes() == lane
        pairs = [(turn(a, by), turn(b, by)) for a, b in zip(self.own, self.rim)]
        return Plane([jnp.where(at, b, a) for a, b in pairs], [jnp.where(at, a, b) for a, b in pairs])

    def east(self):
        return self.side(-1, COLS - 1)

    def west(self):
        return self.side(1, 0)

    def north(self):
        return Plane(*[x[1:] + [turn(x[0], -1, 0)] for x in (self.own, self.rim)])

    def south(self):
        return Plane(*[[turn(x[-1], 1, 0)] + x[:-1] for x in (self.own, self.rim)])


def solve_kernel(levels, own, core, chip_0, chip_1, passed, stored, out, own_buf, rim_buf, terms, weights):
    del stored
    lat, _ = place()
    lat_even, lon_even = evens()
    chip_even = lat // 2 % 2 == 0
    lane = lanes()

    def tile(b, index):
        if b == 0:
            return own[index]
        if abs(b) == 2:
            to_first = chip_even if b > 0 else jnp.logical_not(chip_even)
            return jnp.where(to_first, chip_0[index], chip_1[index])
        on_chip = lat_even if b > 0 else jnp.logical_not(lat_even)
        return jnp.where(on_chip, core[index], passed[index])

    def gather(plane):
        for b in range(-2, 3):
            inside = (lat + b >= 0) & (lat + b < lax.axis_size("lat"))
            for half in range(2):
                at = ROWS * (b + 2) + GROUP * half
                mid = tile(b, 2 * plane + half)
                first, second = tile(b, BLOCK + half), tile(b, BLOCK + STRIP + half)
                east = turn(jnp.where(lon_even, first, second), -32 * plane)
                west = turn(jnp.where(lon_even, second, first), 96 - 32 * plane)
                rim = jnp.where(lane < 32, east, jnp.where(lane >= 96, west, 0.0))
                if b != 0:
                    mid, rim = jnp.where(inside, mid, 0.0), jnp.where(inside, rim, 0.0)
                own_buf[at : at + GROUP, :] = mid
                rim_buf[at : at + GROUP, :] = rim
        return Plane(
            *[[buf[pl.ds(t, GROUP, stride=STEPS), :] for t in range(STEPS)] for buf in (own_buf, rim_buf)]
        )

    depth, prior, zonal, northward = [gather(plane) for plane in range(4)]

    ocean = depth.map(0.0, lambda a, b: jnp.where(a > b, 1.0, 0.0))
    depth_east, depth_north = depth.low(depth.east()), depth.low(depth.north())
    zonal_flow = zonal.map(depth_east, lambda a, b: masked(b > 0.0, a))
    north_flow = northward.map(depth_north, lambda a, b: masked(b > 0.0, a))
    divergence = (zonal_flow - zonal_flow.west()) + (north_flow - north_flow.south())
    right_side = prior * SURFACE_TERM - divergence * TRANSPORT_SCALE
    east_face, north_face = depth_east * (1.0 / levels), depth_north * (1.0 / levels)
    west_face, south_face = east_face.west(), north_face.south()
    diagonal = (((east_face + west_face) + north_face) + south_face) + SURFACE_TERM
    root = diagonal.map(0.0, lambda a, b: jnp.sqrt(a))
    inverse = root.map(1.0, lambda a, b: b / a)
    scaled_side = right_side * inverse
    east_face = east_face * inverse * inverse.east()
    north_face = north_face * inverse * inverse.north()
    for step, (scale, carry) in enumerate(zip(*chebyshev_weights(ITERATIONS))):
        weights[step : step + 1, :] = jnp.full((1, COLS), scale, jnp.float32)
        weights[ITERATIONS + step : ITERATIONS + step + 1, :] = jnp.full((1, COLS), carry, jnp.float32)
    for i, plane in enumerate((scaled_side, east_face, north_face)):
        for t in range(STEPS):
            terms[2 * i, t] = plane.own[t]
            terms[2 * i + 1, t] = plane.rim[t]

    def body(step, state):
        height, change = [Plane(list(x[:STEPS]), list(x[STEPS:])) for x in state]
        side, east, north = [
            Plane([terms[2 * i, t] for t in range(STEPS)], [terms[2 * i + 1, t] for t in range(STEPS)])
            for i in range(3)
        ]
        spread = (east * height.east() + (east * height).west()) + (
            north * height.north() + (north * height).south()
        )
        residual = (side - height) + spread
        change = residual * row_of(weights, step) + change * row_of(weights, ITERATIONS + step)
        height = height + change
        return tuple(tuple(x.own + x.rim) for x in (height, change))

    start = prior * root
    nothing = (jnp.zeros(TILE, jnp.float32),) * (2 * STEPS)
    height, _ = lax.fori_loop(0, ITERATIONS, body, (tuple(start.own + start.rim), nothing))
    height = Plane(list(height[:STEPS]), list(height[STEPS:])) * inverse
    height = height * ocean
    for t in range(STEPS):
        own_buf[pl.ds(t, GROUP, stride=STEPS), :] = height.own[t]
    out[...] = own_buf[2 * ROWS : 3 * ROWS, :]


def join_kernel(count, *refs):
    at = 0
    for ref in refs[:count]:
        refs[-1][at : at + ref.shape[0]] = ref[...]
        at += ref.shape[0]


def pass_kernel(chip_0, chip_1, *refs):
    lat, _ = place()
    refs[-1][...] = jnp.where((lat % 2 == 0) == (lat // 2 % 2 == 0), chip_0[...], chip_1[...])


def swap(value, axis, partner):
    count = lax.axis_size(axis)
    return lax.ppermute(value, axis, [(i, partner(i) % count) for i in range(count)])


def even_first(i):
    return i + 1 if i % 2 == 0 else i - 1


def odd_first(i):
    return i - 1 if i % 2 == 0 else i + 1


def chip_even_first(i):
    return i + 2 if i // 2 % 2 == 0 else i - 2


def chip_odd_first(i):
    return i - 2 if i // 2 % 2 == 0 else i + 2


def shape(*dims):
    return jax.ShapeDtypeStruct(dims, jnp.float32)


VMEM = pl.BlockSpec(memory_space=pltpu.VMEM)
ANY = pl.BlockSpec(memory_space=pl.ANY)
HBM = pl.BlockSpec(memory_space=pltpu.HBM)


def call(kernel, outs, scratch, *args, ins=None, out_specs=None):
    return pl.pallas_call(
        kernel,
        out_shape=outs,
        in_specs=ins or [VMEM] * len(args),
        out_specs=out_specs or jax.tree.map(lambda _: VMEM, outs),
        scratch_shapes=scratch,
        compiler_params=pltpu.CompilerParams(vmem_limit_bytes=32 * 2**20),
        cost_estimate=pl.CostEstimate(flops=0, bytes_accessed=4 * 2**20, transcendentals=0),
    )(*args)


def per_device(
    heat_anomaly,
    saltiness_anomaly,
    zonal_current_array,
    meridional_current_array,
    sea_height_prior,
    ocean_layer_number,
):
    levels, rows, cols = heat_anomaly.shape
    lat_total = rows * lax.axis_size("lat")
    fields = [
        x.reshape(levels * rows, cols)
        for x in (heat_anomaly, saltiness_anomaly, zonal_current_array, meridional_current_array)
    ]
    padded, plane = shape(PADDED, cols), shape(rows, cols)

    def tiles(n):
        return shape(n, *TILE)

    *kept, own, to_0, to_1, depth, prior = call(
        functools.partial(load_kernel, levels),
        (padded,) * 4 + (tiles(PACKS + 1), tiles(SIDE), tiles(SIDE), plane, plane),
        [
            pltpu.VMEM((rows, cols), jnp.int32),
            pltpu.SemaphoreType.DMA((4 * LOADS,)),
            pltpu.SemaphoreType.DMA((2,)),
        ],
        *[
            pltpu.with_memory_space_constraint(x, pltpu.HBM)
            for x in (*fields, ocean_layer_number, sea_height_prior)
        ],
        ins=[HBM] * 6,
    )
    sides = (own, swap(to_0, "lon", even_first), swap(to_1, "lon", odd_first))
    rows_0, rows_1 = call(rows_kernel, (tiles(HALO + 2),) * 2, [], *kept, depth)
    to_0, to_1 = call(corner_kernel, (tiles(ROWS_OUT),) * 2, [], rows_0, rows_1, *sides)
    swaps = (swap(to_0, "lat", even_first), swap(to_1, "lat", odd_first))

    scratch = [pltpu.VMEM((GROUP * ROWS, COLS), jnp.float32)] * 2
    scratch += [pltpu.VMEM((ROWS, *TILE), jnp.float32)] * 2
    u_inner, v_inner, sums, inner, kept_laps = call(
        functools.partial(inner_kernel, lat_total),
        (padded, padded, tiles(4), tiles(3 * ROWS), shape(2 * len(KEPT), GROUPS, *TILE)),
        scratch,
        *kept,
        depth,
        *sides,
    )
    some_rows = shape(len(OUTER_ROWS), GROUPS, *TILE)
    u_outer, v_outer, block, strip_0, strip_1, outer = call(
        functools.partial(outer_kernel, lat_total),
        (some_rows, some_rows, tiles(BLOCK), tiles(STRIP), tiles(STRIP), tiles(12)),
        scratch + [pltpu.VMEM((4, *TILE), jnp.float32)],
        *kept,
        depth,
        prior,
        *sides,
        *swaps,
        sums,
        inner,
        kept_laps,
    )
    u_next, v_next = call(merge_kernel, (padded, padded), [], u_inner, v_inner, u_outer, v_outer)
    pieces = []
    for part in range(PARTS):
        pieces += call(
            functools.partial(tracer_kernel, part),
            (shape(PART, cols),) * 2,
            [],
            *kept,
            *sides,
            *swaps,
            inner,
            outer,
        )

    strips = [swap(strip_0, "lon", even_first), swap(strip_1, "lon", odd_first)]
    made = pieces[:4]
    block = call(
        functools.partial(join_kernel, 3),
        tiles(BLOCK + 2 * STRIP),
        [],
        block,
        *strips,
        *made,
        ins=[VMEM] * 3 + [ANY] * len(made),
    )
    chip_0, chip_1 = swap(block, "lat", chip_even_first), swap(block, "lat", chip_odd_first)
    core = swap(block, "lat", even_first)
    made = [*pieces[4:], u_next, v_next]
    passed = call(
        pass_kernel,
        tiles(BLOCK + 2 * STRIP),
        [],
        chip_0,
        chip_1,
        *made,
        ins=[VMEM] * 2 + [ANY] * len(made),
    )
    passed = swap(passed, "lat", even_first)
    *results, stored = call(
        functools.partial(store_kernel, levels),
        (shape(levels * rows, cols),) * 4 + (shape(*TILE),),
        [pltpu.SemaphoreType.DMA((2 * PARTS,)), pltpu.SemaphoreType.DMA((2,))],
        u_next,
        v_next,
        *pieces,
        out_specs=(HBM,) * 4 + (VMEM,),
    )
    height = call(
        functools.partial(solve_kernel, levels),
        plane,
        [pltpu.VMEM((5 * ROWS, COLS), jnp.float32)] * 2
        + [
            pltpu.VMEM((6, STEPS, *TILE), jnp.float32),
            pltpu.VMEM((2 * ITERATIONS, COLS), jnp.float32),
        ],
        block,
        core,
        chip_0,
        chip_1,
        passed,
        stored,
        ins=[VMEM] * 5 + [ANY],
    )
    return *[x.reshape(levels, rows, cols) for x in results], height


def solution(mesh):
    cells, plane = P(None, "lat", "lon"), P("lat", "lon")
    return jax.shard_map(
        per_device,
        mesh=mesh,
        in_specs=(cells,) * 4 + (plane,) * 2,
        out_specs=(cells,) * 4 + (plane,),
        check_vma=False,
    )
```

```python
import functools

import jax
import jax.numpy as jnp
from jax import lax
from jax.experimental import pallas as pl
from jax.experimental.pallas import tpu as pltpu
from jax.sharding import PartitionSpec as P

ITERATIONS = 32

TIME_STEP = 0.1
MIX_TRACER = 0.05
MIX_MOMENTUM = 0.05
HEAT_INDEX = 0.2
SALT_INDEX = 0.2
CORIOLIS = 2.0
SURFACE_TERM = 0.0005
TRANSPORT_SCALE = 0.05

ROWS = 16
COLS = 128
GROUP = 8
GROUPS = 8
TILE = (GROUP, COLS)
PADDED = GROUPS * GROUP * ROWS
PARTS = 4
PART = PADDED // PARTS
LOADS = 4
HALO = 2 * 4 * GROUPS
PACKS = 2 * GROUPS
SIDE = GROUPS + 1
CORNER = 2
BLOCK = 8
STRIP = 2


def chebyshev_weights(total_steps):
    low_bound = SURFACE_TERM / (SURFACE_TERM + 4.0)
    high_bound = 2.0 - low_bound
    spread_ratio = (high_bound - low_bound) / (high_bound + low_bound)
    middle = 0.5 * (high_bound + low_bound)
    weights = [1.0]
    for number in range(1, total_steps):
        if number == 1:
            weights.append(2.0 / (2.0 - spread_ratio * spread_ratio))
        else:
            weights.append(1.0 / (1.0 - spread_ratio * spread_ratio * weights[-1] / 4.0))
    return [weight / middle for weight in weights], [weight - 1.0 for weight in weights]


def lanes():
    return lax.broadcasted_iota(jnp.int32, TILE, 1)


def sublanes():
    return lax.broadcasted_iota(jnp.int32, TILE, 0)


def turn(value, by, axis=1):
    size = value.shape[axis]
    by = by % size
    return value if by == 0 else pltpu.roll(value, by, axis)


def row_of(ref, row):
    return jnp.broadcast_to(ref[pl.ds(row, 1), :], TILE)


def masked(mask, value):
    return jnp.where(mask, value, 0.0)


def place():
    return lax.axis_index("lat"), lax.axis_index("lon")


def evens():
    lat, lon = place()
    return lat % 2 == 0, lon % 2 == 0


def load_kernel(
    levels, t, s, u, v, depth_in, prior_in, t_out, s_out, u_out, v_out, own, side_0, side_1, depth_out,
    prior, depth, sems, sems_plane,
):
    _, lon_even = evens()
    fields, kept = (t, s, u, v), (t_out, s_out, u_out, v_out)
    planes = [
        pltpu.make_async_copy(src, dst, sems_plane.at[i])
        for i, (src, dst) in enumerate(((depth_in, depth), (prior_in, prior)))
    ]
    copies = []
    for part in range(LOADS):
        first = PADDED // LOADS * part
        span = pl.ds(first, min(PADDED // LOADS, levels * ROWS - first))
        for field in range(4):
            copies.append(
                pltpu.make_async_copy(
                    fields[field].at[span, :], kept[field].at[span, :], sems.at[4 * part + field]
                )
            )
    for copy in planes + copies:
        copy.start()
    for copy in planes:
        copy.wait()
    for half in range(2):
        rows = slice(GROUP * half, GROUP * (half + 1))
        depth_out[rows, :] = depth[rows, :].astype(jnp.float32)
    lane = lanes()
    slot, low = lane // 4, (lane & 3) < 2
    pack = jnp.zeros(TILE, jnp.float32)
    for r in range(ROWS):
        x = row_of(depth_out, r)
        for f in range(2):
            pack = jnp.where(slot == 16 * f + r, turn(x, 64 * f + 4 * r + 2), pack)
    own[PACKS] = pack
    side_0[GROUPS] = pack
    side_1[GROUPS] = pack

    def body(g, carry):
        packs = []
        for pair in range(2):
            pack = jnp.zeros(TILE, jnp.float32)
            for f in range(2):
                for r in range(ROWS):
                    x = kept[2 * pair + f][pl.ds(GROUP * ROWS * g + r, GROUP, stride=ROWS), :]
                    pack = jnp.where(slot == 16 * f + r, turn(x, 64 * f + 4 * r + 2), pack)
            own[pair * GROUPS + g] = pack
            packs.append(pack)
        to_east = jnp.where(low, packs[0], turn(packs[1], 2))
        to_west = jnp.where(low, turn(packs[1], -2), packs[0])
        side_0[g] = jnp.where(lon_even, to_east, to_west)
        side_1[g] = jnp.where(lon_even, to_west, to_east)
        return carry

    for part in range(LOADS):
        for copy in copies[4 * part : 4 * part + 4]:
            copy.wait()
        for g in range(GROUPS // LOADS * part, GROUPS // LOADS * (part + 1)):
            body(g, 0)


def rows_kernel(t, s, u, v, depth, swap_0, swap_1):
    lat_even, _ = evens()
    fields = (t, s, u, v)
    outer = jnp.where(lat_even, ROWS - 2, 0)

    def body(g, carry):
        for field in range(4):
            for r in range(2):
                for swap, row in ((swap_0, outer), (swap_1, ROWS - 2 - outer)):
                    swap[(r * 4 + field) * GROUPS + g] = fields[field][
                        pl.ds(GROUP * ROWS * g + row + r, GROUP, stride=ROWS), :
                    ]
        return carry

    lax.fori_loop(0, GROUPS, body, 0)
    for half in range(2):
        x = depth[GROUP * half : GROUP * (half + 1), :]
        swap_0[HALO + half] = x
        swap_1[HALO + half] = x


class Around:
    def __init__(self, own, side_0, side_1, swap_0=None, swap_1=None, corner_0=None, corner_1=None):
        lat, _ = place()
        self.lat_even, self.lon_even = evens()
        self.first, self.final = lat == 0, lat == lax.axis_size("lat") - 1
        lane = lanes()
        self.lane, self.column, self.row = lane, lane & 3, (lane // 4) & 15
        self.low, self.column_2 = self.column < 2, self.column == 2
        self.own, self.sides, self.swaps = own, (side_0, side_1), (swap_0, swap_1)
        self.corners = corner_0, corner_1

    def beside(self, tile):
        a, b = self.sides[0][tile], self.sides[1][tile]
        return jnp.where(self.lon_even, a, b), jnp.where(self.lon_even, b, a)

    def beyond(self, north, index):
        a, b = self.swaps if north else self.swaps[::-1]
        return jnp.where(self.lat_even, a[index], b[index])

    def cornered(self, north, index):
        a, b = self.corners if north else self.corners[::-1]
        return jnp.where(self.lat_even, a[index], b[index])

    def columns(self, pair, g):
        east, west = self.beside(g)
        if pair == 1:
            east, west = turn(east, 2), turn(west, -2)
        own = self.own[pair * GROUPS + g]
        return jnp.where(self.low, west, own), jnp.where(self.low, own, east)

    def depth_columns(self):
        east, west = self.beside(GROUPS)
        own = self.own[PACKS]
        return jnp.where(self.low, west, own), jnp.where(self.low, own, east)

    def corner(self, pair, g):
        at = 4 * (g + GROUPS * pair)
        south = pltpu.roll(self.cornered(False, 0), (COLS - at) % COLS, 1)
        north = pltpu.roll(self.cornered(True, 0), (COLS + 60 - at) % COLS, 1)
        return jnp.where(self.row == 0, south, north)

    def corner_depth(self):
        south = jnp.where(self.first, 0.0, self.cornered(False, 1))
        north = jnp.where(self.final, 0.0, self.cornered(True, 1))
        return jnp.where(self.row == 0, south, north)

    def row_depth(self, j):
        if j < 0:
            x, outside = self.beyond(False, HALO + 1)[GROUP + j : GROUP + j + 1, :], self.first
        else:
            x, outside = self.beyond(True, HALO)[j - ROWS : j - ROWS + 1, :], self.final
        return jnp.where(outside, 0.0, jnp.broadcast_to(x, TILE))

    def level_row(self, ref, field, g, j):
        if 0 <= j < ROWS:
            return ref[pl.ds(GROUP * ROWS * g + j, GROUP, stride=ROWS), :]
        return self.beyond(j >= ROWS, ((j - ROWS if j >= ROWS else j + 2) * 4 + field) * GROUPS + g)

    def neighbours(self, q, corner):
        north = jnp.where(self.row == ROWS - 1, corner, turn(q, -4))
        south = jnp.where(self.row == 0, corner, turn(q, 4))
        return turn(q, -1), turn(q, 1), north, south

    def join(self, west, east):
        return jnp.where(self.column_2, east, turn(west, 2))

    def sideways(self, q, edge, f, r):
        edge = turn(edge, 127 - (64 * f + 4 * r + 2))
        east = jnp.where(self.lane == COLS - 1, edge, turn(q, -1))
        west = jnp.where(self.lane == 0, edge, turn(q, 1))
        return east, west


def corner_kernel(own, side_0, side_1, corner_0, corner_1):
    near = Around(own, side_0, side_1)
    slot = near.row
    for corner, upper in ((corner_0, near.lat_even), (corner_1, jnp.logical_not(near.lat_even))):
        from_row = jnp.where(upper, 4 * (ROWS - 1), 0)
        tile = jnp.zeros(TILE, jnp.float32)
        for pair in range(2):
            for g in range(GROUPS):
                west, east = near.columns(pair, g)
                at = g + GROUPS * pair
                moved = pltpu.roll(jnp.where(near.low, west, east), (4 * at + COLS - from_row) % COLS, 1)
                tile = jnp.where(slot == at, moved, tile)
        corner[0] = tile
        west, east = near.depth_columns()
        shift = jnp.where(upper, COLS - 60, 60)
        corner[1] = pltpu.roll(jnp.where(near.low, west, east), shift, 1)


class Depths:
    def __init__(self, inner, outer=None):
        self.inner, self.outer = inner, outer

    def tile(self, j, which):
        if 0 <= j < ROWS:
            return self.inner[3 * j + which]
        return self.outer[3 * (j + 2 if j < 0 else j - ROWS + 2) + which]

    def build_inner(self, near, depth):
        ring = near.join(*near.depth_columns())
        for j in range(ROWS):
            d = row_of(depth, j)
            self.inner[3 * j] = d
            self.inner[3 * j + 1], self.inner[3 * j + 2] = near.sideways(d, ring, 0, j)

    def build_outer(self, near):
        corner = near.corner_depth()
        ring = near.join(corner, corner)
        for j in (-2, -1, ROWS, ROWS + 1):
            at = 3 * (j + 2 if j < 0 else j - ROWS + 2)
            d = near.row_depth(j)
            self.outer[at] = d
            d_e, d_w = near.sideways(d, ring, 0, 0 if j < 0 else ROWS - 1)
            self.outer[at + 1], self.outer[at + 2] = d_e, d_w


class Edges:
    def __init__(self, near, g, level, with_laplacian, corners):
        self.ring, self.corner, self.lap = {}, {}, {}
        corner_d = near.corner_depth() if corners else jnp.zeros(TILE, jnp.float32)
        depths = [(d, *near.neighbours(d, corner_d)) for d in near.depth_columns()]
        for pair in range(2):
            corner = jnp.zeros(TILE, jnp.float32)
            if corners:
                corner = masked(level < corner_d, near.corner(pair, g))
            sides, laps = [], []
            for q, d_all in zip(near.columns(pair, g), depths):
                here = level < d_all[0]
                q = masked(here, q)
                sides.append(q)
                if pair in with_laplacian:
                    e, w, n, s = near.neighbours(q, corner)
                    count = sum(jnp.where(level < d, 1.0, 0.0) for d in d_all[1:])
                    laps.append(masked(here, ((e + w) + n) + s - count * q))
            self.ring[pair] = near.join(*sides)
            self.corner[pair] = near.join(corner, corner)
            if laps:
                self.lap[pair] = near.join(*laps)

    def edge(self, pair, j):
        return self.ring[pair] if 0 <= j < ROWS else self.corner[pair]


def prefix(x, sub):
    for by in (1, 2, 4):
        x = x + jnp.where(sub >= by, turn(x, by, 0), 0.0)
    return x


def wet_sides(dep, level, wet, j):
    return (
        jnp.where(level < dep.tile(j, 1), 1.0, 0.0) + jnp.where(level < dep.tile(j, 2), 1.0, 0.0)
    ) + (jnp.where(wet[j + 1], 1.0, 0.0) + jnp.where(wet[j - 1], 1.0, 0.0))


def laplace_row(near, dep, level, wet, q, edges, pair, j):
    count = wet_sides(dep, level, wet, j)
    laps, sides = [], []
    for f in range(2):
        e, w = near.sideways(q[j][f], edges.edge(pair, j), f, min(max(j, 0), ROWS - 1))
        sides.append((e, w))
        total = (e + w) + (q[j + 1][f] + q[j - 1][f])
        laps.append(masked(wet[j], total - count * q[j][f]))
    return laps, sides, count


def momentum_levels(
    near, dep, lat_total, windows, corners, t, s, u, v, write, kept, sum_x, sum_y, sum_u, sum_v
):
    sub = sublanes()
    zero = jnp.zeros(TILE, jnp.float32)
    for first, last in windows:
        for r in range(first, last + 1):
            for ref in (sum_x, sum_y):
                ref[GROUP * r : GROUP * (r + 1), :] = zero
            for ref in (sum_u, sum_v):
                ref[r] = zero
    first_row = (place()[0] * ROWS).astype(jnp.float32)

    def body(g, carry):
        level = (GROUP * g + sub).astype(jnp.float32)
        edges = Edges(near, g, level, (1,), corners)
        edge_load = turn(edges.ring[0], 64) - edges.ring[0]
        for first, last in windows:
            wet, q, lap, dens, count = {}, {}, {}, {}, {}
            for j in range(first - 2, last + 3):
                if not corners or j not in (3, ROWS - 4):
                    wet[j] = level < dep.tile(j, 0)
                    q[j] = [masked(wet[j], near.level_row(ref, i, g, j)) for i, ref in ((2, u), (3, v))]
                if first - 1 <= j <= last + 1:
                    dens[j] = masked(wet[j], near.level_row(s, 1, g, j) - near.level_row(t, 0, g, j))
                i = j - 1
                if j >= first:
                    if corners and i in KEPT:
                        lap[i] = [kept[KEPT.index(i) * 2 + f, g] for f in range(2)]
                        if first <= i <= last:
                            count[i] = wet_sides(dep, level, wet, i)
                    else:
                        lap[i], _, count[i] = laplace_row(near, dep, level, wet, q, edges, 1, i)
                        if not corners and i in KEPT:
                            for f in range(2):
                                kept[KEPT.index(i) * 2 + f, g] = lap[i][f]
                r = j - 2
                if r < first:
                    continue
                mixes = []
                for f in range(2):
                    e, w = near.sideways(lap[r][f], edges.lap[1], f, r)
                    mixes.append((e + w) + (lap[r + 1][f] + lap[r - 1][f]) - count[r] * lap[r][f])
                e, w = near.sideways(dens[r], edge_load, 0, r)
                final = GROUP * r + GROUP - 1
                grad_x = prefix(e - w, sub) + row_of(sum_x, final)
                grad_y = prefix(dens[r + 1] - dens[r - 1], sub) + row_of(sum_y, final)
                sum_x[GROUP * r : GROUP * (r + 1), :] = grad_x
                sum_y[GROUP * r : GROUP * (r + 1), :] = grad_y
                turning = TIME_STEP * CORIOLIS * (2.0 * (first_row + (r + 0.5)) / lat_total - 1.0)
                pull = TIME_STEP * 0.5 * SALT_INDEX
                mix = TIME_STEP * MIX_MOMENTUM
                new_u = masked(
                    wet[r], q[r][0] + ((turning * q[r][1] - pull * grad_x) - mix * mixes[0])
                )
                new_v = masked(
                    wet[r], q[r][1] - ((turning * q[r][0] + pull * grad_y) + mix * mixes[1])
                )
                write(g, r, new_u, new_v)
                sum_u[r] += new_u
                sum_v[r] += new_v
        return carry

    lax.fori_loop(0, GROUPS, body, 0, unroll=4 if corners else 2)


def write_sums(windows, sum_u, sum_v, block):
    for first, last in windows:
        for r in range(first, last + 1):
            half, row = divmod(r, GROUP)
            block[half, row : row + 1, :] = jnp.sum(sum_u[r], axis=0, keepdims=True)
            block[2 + half, row : row + 1, :] = jnp.sum(sum_v[r], axis=0, keepdims=True)


INNER = ((2, ROWS - 3),)
OUTER = ((0, 1), (ROWS - 2, ROWS - 1))
OUTER_ROWS = (0, 1, ROWS - 2, ROWS - 1)
KEPT = (1, 2, ROWS - 3, ROWS - 2)


def inner_kernel(
    lat_total, t, s, u, v, depth, own, side_0, side_1, u_next, v_next, sums, inner, kept,
    sum_x, sum_y, sum_u, sum_v,
):
    near, dep = Around(own, side_0, side_1), Depths(inner)
    dep.build_inner(near, depth)

    def write(g, r, new_u, new_v):
        rows = pl.ds(GROUP * ROWS * g + r, GROUP, stride=ROWS)
        u_next[rows, :] = new_u
        v_next[rows, :] = new_v

    momentum_levels(
        near, dep, lat_total, INNER, False, t, s, u, v, write, kept, sum_x, sum_y, sum_u, sum_v
    )
    sums[...] = jnp.zeros(sums.shape, jnp.float32)
    write_sums(INNER, sum_u, sum_v, sums)


def outer_kernel(
    lat_total, t, s, u, v, depth, prior, own, side_0, side_1, swap_0, swap_1, corner_0, corner_1,
    sums, inner, kept, u_outer, v_outer, block, strip_0, strip_1, outer, sum_x, sum_y, sum_u, sum_v, total,
):
    near = Around(own, side_0, side_1, swap_0, swap_1, corner_0, corner_1)
    dep = Depths(inner, outer)
    dep.build_outer(near)
    total[...] = sums[...]

    def write(g, r, new_u, new_v):
        u_outer[OUTER_ROWS.index(r), g] = new_u
        v_outer[OUTER_ROWS.index(r), g] = new_v

    momentum_levels(
        near, dep, lat_total, OUTER, True, t, s, u, v, write, kept, sum_x, sum_y, sum_u, sum_v
    )
    write_sums(OUTER, sum_u, sum_v, total)
    quarter = lanes() // 32
    for half in range(2):
        rows = slice(GROUP * half, GROUP * (half + 1))
        planes = [depth[rows, :], prior[rows, :], total[half], total[2 + half]]
        for plane, x in enumerate(planes):
            block[2 * plane + half] = x
        strips = []
        for first in (96, 0):
            strip = jnp.zeros(TILE, jnp.float32)
            for plane, x in enumerate(planes):
                strip = jnp.where(quarter == plane, turn(x, 32 * plane - first), strip)
            strips.append(strip)
        strip_0[half] = jnp.where(near.lon_even, strips[0], strips[1])
        strip_1[half] = jnp.where(near.lon_even, strips[1], strips[0])


def merge_kernel(u_inner, v_inner, u_outer, v_outer, u_next, v_next):
    for inner, outer, out in ((u_inner, u_outer, u_next), (v_inner, v_outer, v_next)):
        out[...] = inner[...]
        for g in range(GROUPS):
            for i, r in enumerate(OUTER_ROWS):
                out[pl.ds(GROUP * ROWS * g + r, GROUP, stride=ROWS), :] = outer[i, g]


def tracer_kernel(
    part, t, s, u, v, own, side_0, side_1, swap_0, swap_1, corner_0, corner_1, inner, outer, t_next, s_next
):
    near = Around(own, side_0, side_1, swap_0, swap_1, corner_0, corner_1)
    dep = Depths(inner, outer)
    sub = sublanes()

    def body(g, carry):
        start = GROUP * ROWS * g - PART * part
        level = (GROUP * g + sub).astype(jnp.float32)
        edges = Edges(near, g, level, (0,), True)
        wet, q, sides, lap, flow, count = {}, {}, {}, {}, {}, {}
        for j in range(-2, ROWS + 2):
            wet[j] = level < dep.tile(j, 0)
            q[j] = [masked(wet[j], near.level_row(ref, i, g, j)) for i, ref in ((0, t), (1, s))]
            if -1 <= j <= ROWS:
                flow[j] = [masked(wet[j], near.level_row(ref, i, g, j)) for i, ref in ((2, u), (3, v))]
            if j >= 0:
                lap[j - 1], sides[j - 1], count[j - 1] = laplace_row(
                    near, dep, level, wet, q, edges, 0, j - 1
                )
            r = j - 2
            if r < 0:
                continue
            e, w = near.sideways(flow[r][0], edges.ring[1], 0, r)
            u_e = masked(level < dep.tile(r, 1), flow[r][0] + e)
            u_w = masked(level < dep.tile(r, 2), flow[r][0] + w)
            v_n = masked(wet[r + 1], flow[r][1] + flow[r + 1][1])
            v_s = masked(wet[r - 1], flow[r][1] + flow[r - 1][1])
            for f, out in ((0, t_next), (1, s_next)):
                e, w = near.sideways(lap[r][f], edges.lap[0], f, r)
                mix = (e + w) + (lap[r + 1][f] + lap[r - 1][f]) - count[r] * lap[r][f]
                mid = q[r][f]
                e, w = sides[r][f]
                advected = (u_e * (mid + e) - u_w * (mid + w)) + (
                    v_n * (mid + q[r + 1][f]) - v_s * (mid + q[r - 1][f])
                )
                out[pl.ds(start + r, GROUP, stride=ROWS), :] = masked(
                    wet[r],
                    mid - (0.25 * TIME_STEP * advected + TIME_STEP * MIX_TRACER * mix),
                )
        return carry

    lax.fori_loop(2 * part, 2 * part + 2, body, 0)


def store_kernel(levels, u_next, v_next, *refs):
    pieces, (t_out, s_out, u_out, v_out, stored, sems, sems_flow) = refs[:-7], refs[-7:]
    stored[...] = jnp.zeros(TILE, jnp.float32)
    copies = []
    for i, (src, dst) in enumerate(((u_next, u_out), (v_next, v_out))):
        copies.append(
            pltpu.make_async_copy(src.at[pl.ds(0, levels * ROWS), :], dst, sems_flow.at[i])
        )
    for part in range(PARTS):
        size = min(PART, levels * ROWS - PART * part)
        for i, dst in enumerate((t_out, s_out)):
            copies.append(
                pltpu.make_async_copy(
                    pieces[2 * part + i].at[pl.ds(0, size), :],
                    dst.at[pl.ds(PART * part, size), :],
                    sems.at[2 * part + i],
                )
            )
    for copy in copies:
        copy.start()
    for copy in copies:
        copy.wait()


STEPS = 5 * ROWS // GROUP


class Plane:
    def __init__(self, own, rim):
        self.own, self.rim = own, rim

    def map(self, other, fn):
        if isinstance(other, Plane):
            return Plane(
                [fn(a, b) for a, b in zip(self.own, other.own)],
                [fn(a, b) for a, b in zip(self.rim, other.rim)],
            )
        return Plane([fn(a, other) for a in self.own], [fn(a, other) for a in self.rim])

    def __add__(self, other):
        return self.map(other, lambda a, b: a + b)

    def __sub__(self, other):
        return self.map(other, lambda a, b: a - b)

    def __mul__(self, other):
        return self.map(other, lambda a, b: a * b)

    def low(self, other):
        return self.map(other, jnp.minimum)

    def side(self, by, lane):
        at = lanes() == lane
        pairs = [(turn(a, by), turn(b, by)) for a, b in zip(self.own, self.rim)]
        return Plane([jnp.where(at, b, a) for a, b in pairs], [jnp.where(at, a, b) for a, b in pairs])

    def east(self):
        return self.side(-1, COLS - 1)

    def west(self):
        return self.side(1, 0)

    def north(self):
        return Plane(*[x[1:] + [turn(x[0], -1, 0)] for x in (self.own, self.rim)])

    def south(self):
        return Plane(*[[turn(x[-1], 1, 0)] + x[:-1] for x in (self.own, self.rim)])


def solve_kernel(levels, own, core, chip_0, chip_1, passed, stored, out, own_buf, rim_buf):
    del stored
    lat, _ = place()
    lat_even, lon_even = evens()
    chip_even = lat // 2 % 2 == 0
    lane = lanes()

    def tile(b, index):
        if b == 0:
            return own[index]
        if abs(b) == 2:
            to_first = chip_even if b > 0 else jnp.logical_not(chip_even)
            return jnp.where(to_first, chip_0[index], chip_1[index])
        on_chip = lat_even if b > 0 else jnp.logical_not(lat_even)
        return jnp.where(on_chip, core[index], passed[index])

    def gather(plane):
        for b in range(-2, 3):
            inside = (lat + b >= 0) & (lat + b < lax.axis_size("lat"))
            for half in range(2):
                at = ROWS * (b + 2) + GROUP * half
                mid = tile(b, 2 * plane + half)
                first, second = tile(b, BLOCK + half), tile(b, BLOCK + STRIP + half)
                east = turn(jnp.where(lon_even, first, second), -32 * plane)
                west = turn(jnp.where(lon_even, second, first), 96 - 32 * plane)
                rim = jnp.where(lane < 32, east, jnp.where(lane >= 96, west, 0.0))
                if b != 0:
                    mid, rim = jnp.where(inside, mid, 0.0), jnp.where(inside, rim, 0.0)
                own_buf[at : at + GROUP, :] = mid
                rim_buf[at : at + GROUP, :] = rim
        return Plane(
            *[[buf[pl.ds(t, GROUP, stride=STEPS), :] for t in range(STEPS)] for buf in (own_buf, rim_buf)]
        )

    depth, prior, zonal, northward = [gather(plane) for plane in range(4)]

    ocean = depth.map(0.0, lambda a, b: jnp.where(a > b, 1.0, 0.0))
    depth_east, depth_north = depth.low(depth.east()), depth.low(depth.north())
    zonal_flow = zonal.map(depth_east, lambda a, b: masked(b > 0.0, a))
    north_flow = northward.map(depth_north, lambda a, b: masked(b > 0.0, a))
    divergence = (zonal_flow - zonal_flow.west()) + (north_flow - north_flow.south())
    right_side = prior * SURFACE_TERM - divergence * TRANSPORT_SCALE
    east_face, north_face = depth_east * (1.0 / levels), depth_north * (1.0 / levels)
    west_face, south_face = east_face.west(), north_face.south()
    diagonal = (((east_face + west_face) + north_face) + south_face) + SURFACE_TERM
    inverse = diagonal.map(1.0, lambda a, b: b / a)
    right_side, east_face, west_face, north_face, south_face = [
        x * inverse for x in (right_side, east_face, west_face, north_face, south_face)
    ]
    height, change = prior, None
    scales, carries = chebyshev_weights(ITERATIONS)
    for scale, carry in zip(scales, carries):
        spread = (east_face * height.east() + west_face * height.west()) + (
            north_face * height.north() + south_face * height.south()
        )
        residual = (right_side - height) + spread
        step = residual * scale
        change = step if change is None else step + change * carry
        height = height + change
    height = height * ocean
    for t in range(STEPS):
        own_buf[pl.ds(t, GROUP, stride=STEPS), :] = height.own[t]
    out[...] = own_buf[2 * ROWS : 3 * ROWS, :]


def join_kernel(count, *refs):
    at = 0
    for ref in refs[:count]:
        refs[-1][at : at + ref.shape[0]] = ref[...]
        at += ref.shape[0]


def pass_kernel(chip_0, chip_1, *refs):
    lat, _ = place()
    refs[-1][...] = jnp.where((lat % 2 == 0) == (lat // 2 % 2 == 0), chip_0[...], chip_1[...])


def swap(value, axis, partner):
    count = lax.axis_size(axis)
    return lax.ppermute(value, axis, [(i, partner(i) % count) for i in range(count)])


def even_first(i):
    return i + 1 if i % 2 == 0 else i - 1


def odd_first(i):
    return i - 1 if i % 2 == 0 else i + 1


def chip_even_first(i):
    return i + 2 if i // 2 % 2 == 0 else i - 2


def chip_odd_first(i):
    return i - 2 if i // 2 % 2 == 0 else i + 2


def shape(*dims):
    return jax.ShapeDtypeStruct(dims, jnp.float32)


VMEM = pl.BlockSpec(memory_space=pltpu.VMEM)
ANY = pl.BlockSpec(memory_space=pl.ANY)
HBM = pl.BlockSpec(memory_space=pltpu.HBM)


def call(kernel, outs, scratch, *args, ins=None, out_specs=None):
    return pl.pallas_call(
        kernel,
        out_shape=outs,
        in_specs=ins or [VMEM] * len(args),
        out_specs=out_specs or jax.tree.map(lambda _: VMEM, outs),
        scratch_shapes=scratch,
        compiler_params=pltpu.CompilerParams(vmem_limit_bytes=32 * 2**20),
        cost_estimate=pl.CostEstimate(flops=0, bytes_accessed=4 * 2**20, transcendentals=0),
    )(*args)


def per_device(
    heat_anomaly,
    saltiness_anomaly,
    zonal_current_array,
    meridional_current_array,
    sea_height_prior,
    ocean_layer_number,
):
    levels, rows, cols = heat_anomaly.shape
    lat_total = rows * lax.axis_size("lat")
    fields = [
        x.reshape(levels * rows, cols)
        for x in (heat_anomaly, saltiness_anomaly, zonal_current_array, meridional_current_array)
    ]
    padded, plane = shape(PADDED, cols), shape(rows, cols)

    def tiles(n):
        return shape(n, *TILE)

    *kept, own, to_0, to_1, depth, prior = call(
        functools.partial(load_kernel, levels),
        (padded,) * 4 + (tiles(PACKS + 1), tiles(SIDE), tiles(SIDE), plane, plane),
        [
            pltpu.VMEM((rows, cols), jnp.int32),
            pltpu.SemaphoreType.DMA((4 * LOADS,)),
            pltpu.SemaphoreType.DMA((2,)),
        ],
        *[
            pltpu.with_memory_space_constraint(x, pltpu.HBM)
            for x in (*fields, ocean_layer_number, sea_height_prior)
        ],
        ins=[HBM] * 6,
    )
    sides = (own, swap(to_0, "lon", even_first), swap(to_1, "lon", odd_first))
    rows_0, rows_1 = call(rows_kernel, (tiles(HALO + 2),) * 2, [], *kept, depth)
    swaps = (swap(rows_0, "lat", even_first), swap(rows_1, "lat", odd_first))
    to_0, to_1 = call(corner_kernel, (tiles(CORNER),) * 2, [], *sides)
    swaps += (swap(to_0, "lat", even_first), swap(to_1, "lat", odd_first))

    scratch = [pltpu.VMEM((GROUP * ROWS, COLS), jnp.float32)] * 2
    scratch += [pltpu.VMEM((ROWS, *TILE), jnp.float32)] * 2
    u_inner, v_inner, sums, inner, kept_laps = call(
        functools.partial(inner_kernel, lat_total),
        (padded, padded, tiles(4), tiles(3 * ROWS), shape(2 * len(KEPT), GROUPS, *TILE)),
        scratch,
        *kept,
        depth,
        *sides,
    )
    some_rows = shape(len(OUTER_ROWS), GROUPS, *TILE)
    u_outer, v_outer, block, strip_0, strip_1, outer = call(
        functools.partial(outer_kernel, lat_total),
        (some_rows, some_rows, tiles(BLOCK), tiles(STRIP), tiles(STRIP), tiles(12)),
        scratch + [pltpu.VMEM((4, *TILE), jnp.float32)],
        *kept,
        depth,
        prior,
        *sides,
        *swaps,
        sums,
        inner,
        kept_laps,
    )
    u_next, v_next = call(merge_kernel, (padded, padded), [], u_inner, v_inner, u_outer, v_outer)
    pieces = []
    for part in range(PARTS):
        pieces += call(
            functools.partial(tracer_kernel, part),
            (shape(PART, cols),) * 2,
            [],
            *kept,
            *sides,
            *swaps,
            inner,
            outer,
        )

    strips = [swap(strip_0, "lon", even_first), swap(strip_1, "lon", odd_first)]
    made = pieces[:4]
    block = call(
        functools.partial(join_kernel, 3),
        tiles(BLOCK + 2 * STRIP),
        [],
        block,
        *strips,
        *made,
        ins=[VMEM] * 3 + [ANY] * len(made),
    )
    chip_0, chip_1 = swap(block, "lat", chip_even_first), swap(block, "lat", chip_odd_first)
    core = swap(block, "lat", even_first)
    made = [*pieces[4:], u_next, v_next]
    passed = call(
        pass_kernel,
        tiles(BLOCK + 2 * STRIP),
        [],
        chip_0,
        chip_1,
        *made,
        ins=[VMEM] * 2 + [ANY] * len(made),
    )
    passed = swap(passed, "lat", even_first)
    *results, stored = call(
        functools.partial(store_kernel, levels),
        (shape(levels * rows, cols),) * 4 + (shape(*TILE),),
        [pltpu.SemaphoreType.DMA((2 * PARTS,)), pltpu.SemaphoreType.DMA((2,))],
        u_next,
        v_next,
        *pieces,
        out_specs=(HBM,) * 4 + (VMEM,),
    )
    height = call(
        functools.partial(solve_kernel, levels),
        plane,
        [pltpu.VMEM((5 * ROWS, COLS), jnp.float32)] * 2,
        block,
        core,
        chip_0,
        chip_1,
        passed,
        stored,
        ins=[VMEM] * 5 + [ANY],
    )
    return *[x.reshape(levels, rows, cols) for x in results], height


def solution(mesh):
    cells, plane = P(None, "lat", "lon"), P("lat", "lon")
    return jax.shard_map(
        per_device,
        mesh=mesh,
        in_specs=(cells,) * 4 + (plane,) * 2,
        out_specs=(cells,) * 4 + (plane,),
        check_vma=False,
    )
```

```python
import functools

import jax
import jax.numpy as jnp
from jax import lax
from jax.experimental import pallas as pl
from jax.experimental.pallas import tpu as pltpu
from jax.sharding import PartitionSpec as P

ITERATIONS = 32

TIME_STEP = 0.1
MIX_TRACER = 0.05
MIX_MOMENTUM = 0.05
HEAT_INDEX = 0.2
SALT_INDEX = 0.2
CORIOLIS = 2.0
SURFACE_TERM = 0.0005
TRANSPORT_SCALE = 0.05

ROWS = 16
COLS = 128
GROUP = 8
GROUPS = 8
TILE = (GROUP, COLS)
PADDED = GROUPS * GROUP * ROWS
PARTS = 4
PART = PADDED // PARTS
LOADS = 4
HALO = 2 * 4 * GROUPS
PACKS = 2 * GROUPS
SIDE = GROUPS + 1
CORNER = 2
BLOCK = 8
STRIP = 2


def chebyshev_weights(total_steps):
    low_bound = SURFACE_TERM / (SURFACE_TERM + 4.0)
    high_bound = 2.0 - low_bound
    spread_ratio = (high_bound - low_bound) / (high_bound + low_bound)
    middle = 0.5 * (high_bound + low_bound)
    weights = [1.0]
    for number in range(1, total_steps):
        if number == 1:
            weights.append(2.0 / (2.0 - spread_ratio * spread_ratio))
        else:
            weights.append(1.0 / (1.0 - spread_ratio * spread_ratio * weights[-1] / 4.0))
    return [weight / middle for weight in weights], [weight - 1.0 for weight in weights]


def lanes():
    return lax.broadcasted_iota(jnp.int32, TILE, 1)


def sublanes():
    return lax.broadcasted_iota(jnp.int32, TILE, 0)


def turn(value, by, axis=1):
    size = value.shape[axis]
    by = by % size
    return value if by == 0 else pltpu.roll(value, by, axis)


def row_of(ref, row):
    return jnp.broadcast_to(ref[pl.ds(row, 1), :], TILE)


def masked(mask, value):
    return jnp.where(mask, value, 0.0)


def place():
    return lax.axis_index("lat"), lax.axis_index("lon")


def evens():
    lat, lon = place()
    return lat % 2 == 0, lon % 2 == 0


def load_kernel(
    levels, t, s, u, v, depth_in, prior_in, t_out, s_out, u_out, v_out, own, side_0, side_1, depth_out,
    prior, depth, t_buf, s_buf, u_buf, v_buf, sems, sems_plane,
):
    _, lon_even = evens()
    fields, outs, kept = (t, s, u, v), (t_out, s_out, u_out, v_out), (t_buf, s_buf, u_buf, v_buf)
    planes = [
        pltpu.make_async_copy(src, dst, sems_plane.at[i])
        for i, (src, dst) in enumerate(((depth_in, depth), (prior_in, prior)))
    ]
    copies = []
    for part in range(LOADS):
        first = PADDED // LOADS * part
        span = pl.ds(first, min(PADDED // LOADS, levels * ROWS - first))
        for field in range(4):
            copies.append(
                pltpu.make_async_copy(
                    fields[field].at[span, :], kept[field].at[span, :], sems.at[4 * part + field]
                )
            )
    for copy in planes + copies:
        copy.start()
    for copy in planes:
        copy.wait()
    for half in range(2):
        rows = slice(GROUP * half, GROUP * (half + 1))
        depth_out[rows, :] = depth[rows, :].astype(jnp.float32)
    lane = lanes()
    slot, low = lane // 4, (lane & 3) < 2
    pack = jnp.zeros(TILE, jnp.float32)
    for r in range(ROWS):
        x = row_of(depth_out, r)
        for f in range(2):
            pack = jnp.where(slot == 16 * f + r, turn(x, 64 * f + 4 * r + 2), pack)
    own[PACKS] = pack
    side_0[GROUPS] = pack
    side_1[GROUPS] = pack

    def body(g, carry):
        packs = []
        for pair in range(2):
            pack = jnp.zeros(TILE, jnp.float32)
            for f in range(2):
                for r in range(ROWS):
                    x = kept[2 * pair + f][pl.ds(GROUP * ROWS * g + r, GROUP, stride=ROWS), :]
                    outs[2 * pair + f][GROUPS * r + g] = x
                    pack = jnp.where(slot == 16 * f + r, turn(x, 64 * f + 4 * r + 2), pack)
            own[pair * GROUPS + g] = pack
            packs.append(pack)
        to_east = jnp.where(low, packs[0], turn(packs[1], 2))
        to_west = jnp.where(low, turn(packs[1], -2), packs[0])
        side_0[g] = jnp.where(lon_even, to_east, to_west)
        side_1[g] = jnp.where(lon_even, to_west, to_east)
        return carry

    for part in range(LOADS):
        for copy in copies[4 * part : 4 * part + 4]:
            copy.wait()
        for g in range(GROUPS // LOADS * part, GROUPS // LOADS * (part + 1)):
            body(g, 0)


def rows_kernel(t, s, u, v, depth, swap_0, swap_1):
    lat_even, _ = evens()
    fields = (t, s, u, v)
    outer = jnp.where(lat_even, ROWS - 2, 0)

    def body(g, carry):
        for field in range(4):
            for r in range(2):
                for swap, row in ((swap_0, outer), (swap_1, ROWS - 2 - outer)):
                    swap[(r * 4 + field) * GROUPS + g] = fields[field][GROUPS * (row + r) + g]
        return carry

    lax.fori_loop(0, GROUPS, body, 0)
    for half in range(2):
        x = depth[GROUP * half : GROUP * (half + 1), :]
        swap_0[HALO + half] = x
        swap_1[HALO + half] = x


class Around:
    def __init__(self, own, side_0, side_1, swap_0=None, swap_1=None, corner_0=None, corner_1=None):
        lat, _ = place()
        self.lat_even, self.lon_even = evens()
        self.first, self.final = lat == 0, lat == lax.axis_size("lat") - 1
        lane = lanes()
        self.lane, self.column, self.row = lane, lane & 3, (lane // 4) & 15
        self.low, self.column_2 = self.column < 2, self.column == 2
        self.own, self.sides, self.swaps = own, (side_0, side_1), (swap_0, swap_1)
        self.corners = corner_0, corner_1

    def beside(self, tile):
        a, b = self.sides[0][tile], self.sides[1][tile]
        return jnp.where(self.lon_even, a, b), jnp.where(self.lon_even, b, a)

    def beyond(self, north, index):
        a, b = self.swaps if north else self.swaps[::-1]
        return jnp.where(self.lat_even, a[index], b[index])

    def cornered(self, north, index):
        a, b = self.corners if north else self.corners[::-1]
        return jnp.where(self.lat_even, a[index], b[index])

    def columns(self, pair, g):
        east, west = self.beside(g)
        if pair == 1:
            east, west = turn(east, 2), turn(west, -2)
        own = self.own[pair * GROUPS + g]
        return jnp.where(self.low, west, own), jnp.where(self.low, own, east)

    def depth_columns(self):
        east, west = self.beside(GROUPS)
        own = self.own[PACKS]
        return jnp.where(self.low, west, own), jnp.where(self.low, own, east)

    def corner(self, pair, g):
        at = 4 * (g + GROUPS * pair)
        south = pltpu.roll(self.cornered(False, 0), (COLS - at) % COLS, 1)
        north = pltpu.roll(self.cornered(True, 0), (COLS + 60 - at) % COLS, 1)
        return jnp.where(self.row == 0, south, north)

    def corner_depth(self):
        south = jnp.where(self.first, 0.0, self.cornered(False, 1))
        north = jnp.where(self.final, 0.0, self.cornered(True, 1))
        return jnp.where(self.row == 0, south, north)

    def row_depth(self, j):
        if j < 0:
            x, outside = self.beyond(False, HALO + 1)[GROUP + j : GROUP + j + 1, :], self.first
        else:
            x, outside = self.beyond(True, HALO)[j - ROWS : j - ROWS + 1, :], self.final
        return jnp.where(outside, 0.0, jnp.broadcast_to(x, TILE))

    def level_row(self, ref, field, g, j):
        if 0 <= j < ROWS:
            return ref[GROUPS * j + g]
        return self.beyond(j >= ROWS, ((j - ROWS if j >= ROWS else j + 2) * 4 + field) * GROUPS + g)

    def neighbours(self, q, corner):
        north = jnp.where(self.row == ROWS - 1, corner, turn(q, -4))
        south = jnp.where(self.row == 0, corner, turn(q, 4))
        return turn(q, -1), turn(q, 1), north, south

    def join(self, west, east):
        return jnp.where(self.column_2, east, turn(west, 2))

    def sideways(self, q, edge, f, r):
        edge = turn(edge, 127 - (64 * f + 4 * r + 2))
        east = jnp.where(self.lane == COLS - 1, edge, turn(q, -1))
        west = jnp.where(self.lane == 0, edge, turn(q, 1))
        return east, west


def corner_kernel(own, side_0, side_1, corner_0, corner_1):
    near = Around(own, side_0, side_1)
    slot = near.row
    for corner, upper in ((corner_0, near.lat_even), (corner_1, jnp.logical_not(near.lat_even))):
        from_row = jnp.where(upper, 4 * (ROWS - 1), 0)
        tile = jnp.zeros(TILE, jnp.float32)
        for pair in range(2):
            for g in range(GROUPS):
                west, east = near.columns(pair, g)
                at = g + GROUPS * pair
                moved = pltpu.roll(jnp.where(near.low, west, east), (4 * at + COLS - from_row) % COLS, 1)
                tile = jnp.where(slot == at, moved, tile)
        corner[0] = tile
        west, east = near.depth_columns()
        shift = jnp.where(upper, COLS - 60, 60)
        corner[1] = pltpu.roll(jnp.where(near.low, west, east), shift, 1)


class Depths:
    def __init__(self, inner, outer=None):
        self.inner, self.outer = inner, outer

    def tile(self, j, which):
        if 0 <= j < ROWS:
            return self.inner[3 * j + which]
        return self.outer[3 * (j + 2 if j < 0 else j - ROWS + 2) + which]

    def build_inner(self, near, depth):
        ring = near.join(*near.depth_columns())
        for j in range(ROWS):
            d = row_of(depth, j)
            self.inner[3 * j] = d
            self.inner[3 * j + 1], self.inner[3 * j + 2] = near.sideways(d, ring, 0, j)

    def build_outer(self, near):
        corner = near.corner_depth()
        ring = near.join(corner, corner)
        for j in (-2, -1, ROWS, ROWS + 1):
            at = 3 * (j + 2 if j < 0 else j - ROWS + 2)
            d = near.row_depth(j)
            self.outer[at] = d
            d_e, d_w = near.sideways(d, ring, 0, 0 if j < 0 else ROWS - 1)
            self.outer[at + 1], self.outer[at + 2] = d_e, d_w


class Edges:
    def __init__(self, near, g, level, with_laplacian, corners):
        self.ring, self.corner, self.lap = {}, {}, {}
        corner_d = near.corner_depth() if corners else jnp.zeros(TILE, jnp.float32)
        depths = [(d, *near.neighbours(d, corner_d)) for d in near.depth_columns()]
        for pair in range(2):
            corner = jnp.zeros(TILE, jnp.float32)
            if corners:
                corner = masked(level < corner_d, near.corner(pair, g))
            sides, laps = [], []
            for q, d_all in zip(near.columns(pair, g), depths):
                here = level < d_all[0]
                q = masked(here, q)
                sides.append(q)
                if pair in with_laplacian:
                    e, w, n, s = near.neighbours(q, corner)
                    count = sum(jnp.where(level < d, 1.0, 0.0) for d in d_all[1:])
                    laps.append(masked(here, ((e + w) + n) + s - count * q))
            self.ring[pair] = near.join(*sides)
            self.corner[pair] = near.join(corner, corner)
            if laps:
                self.lap[pair] = near.join(*laps)

    def edge(self, pair, j):
        return self.ring[pair] if 0 <= j < ROWS else self.corner[pair]


def prefix(x, sub):
    for by in (1, 2, 4):
        x = x + jnp.where(sub >= by, turn(x, by, 0), 0.0)
    return x


def wet_sides(dep, level, wet, j):
    return (
        jnp.where(level < dep.tile(j, 1), 1.0, 0.0) + jnp.where(level < dep.tile(j, 2), 1.0, 0.0)
    ) + (jnp.where(wet[j + 1], 1.0, 0.0) + jnp.where(wet[j - 1], 1.0, 0.0))


def laplace_row(near, dep, level, wet, q, edges, pair, j):
    count = wet_sides(dep, level, wet, j)
    laps, sides = [], []
    for f in range(2):
        e, w = near.sideways(q[j][f], edges.edge(pair, j), f, min(max(j, 0), ROWS - 1))
        sides.append((e, w))
        total = (e + w) + (q[j + 1][f] + q[j - 1][f])
        laps.append(masked(wet[j], total - count * q[j][f]))
    return laps, sides, count


def momentum_levels(
    near, dep, lat_total, windows, corners, t, s, u, v, write, kept, sum_x, sum_y, sum_u, sum_v
):
    sub = sublanes()
    zero = jnp.zeros(TILE, jnp.float32)
    for first, last in windows:
        for r in range(first, last + 1):
            for ref in (sum_x, sum_y):
                ref[GROUP * r : GROUP * (r + 1), :] = zero
            for ref in (sum_u, sum_v):
                ref[r] = zero
    first_row = (place()[0] * ROWS).astype(jnp.float32)

    def body(g, carry):
        level = (GROUP * g + sub).astype(jnp.float32)
        edges = Edges(near, g, level, (1,), corners)
        edge_load = turn(edges.ring[0], 64) - edges.ring[0]
        for first, last in windows:
            wet, q, lap, dens, count = {}, {}, {}, {}, {}
            for j in range(first - 2, last + 3):
                if not corners or j not in (3, ROWS - 4):
                    wet[j] = level < dep.tile(j, 0)
                    q[j] = [masked(wet[j], near.level_row(ref, i, g, j)) for i, ref in ((2, u), (3, v))]
                if first - 1 <= j <= last + 1:
                    dens[j] = masked(wet[j], near.level_row(s, 1, g, j) - near.level_row(t, 0, g, j))
                i = j - 1
                if j >= first:
                    if corners and i in KEPT:
                        lap[i] = [kept[KEPT.index(i) * 2 + f, g] for f in range(2)]
                        if first <= i <= last:
                            count[i] = wet_sides(dep, level, wet, i)
                    else:
                        lap[i], _, count[i] = laplace_row(near, dep, level, wet, q, edges, 1, i)
                        if not corners and i in KEPT:
                            for f in range(2):
                                kept[KEPT.index(i) * 2 + f, g] = lap[i][f]
                r = j - 2
                if r < first:
                    continue
                mixes = []
                for f in range(2):
                    e, w = near.sideways(lap[r][f], edges.lap[1], f, r)
                    mixes.append((e + w) + (lap[r + 1][f] + lap[r - 1][f]) - count[r] * lap[r][f])
                e, w = near.sideways(dens[r], edge_load, 0, r)
                final = GROUP * r + GROUP - 1
                grad_x = prefix(e - w, sub) + row_of(sum_x, final)
                grad_y = prefix(dens[r + 1] - dens[r - 1], sub) + row_of(sum_y, final)
                sum_x[GROUP * r : GROUP * (r + 1), :] = grad_x
                sum_y[GROUP * r : GROUP * (r + 1), :] = grad_y
                turning = TIME_STEP * CORIOLIS * (2.0 * (first_row + (r + 0.5)) / lat_total - 1.0)
                pull = TIME_STEP * 0.5 * SALT_INDEX
                mix = TIME_STEP * MIX_MOMENTUM
                new_u = masked(
                    wet[r], q[r][0] + ((turning * q[r][1] - pull * grad_x) - mix * mixes[0])
                )
                new_v = masked(
                    wet[r], q[r][1] - ((turning * q[r][0] + pull * grad_y) + mix * mixes[1])
                )
                write(g, r, new_u, new_v)
                sum_u[r] += new_u
                sum_v[r] += new_v
        return carry

    lax.fori_loop(0, GROUPS, body, 0, unroll=GROUPS if corners else 1)


def write_sums(windows, sum_u, sum_v, block):
    for first, last in windows:
        for r in range(first, last + 1):
            half, row = divmod(r, GROUP)
            block[half, row : row + 1, :] = jnp.sum(sum_u[r], axis=0, keepdims=True)
            block[2 + half, row : row + 1, :] = jnp.sum(sum_v[r], axis=0, keepdims=True)


INNER = ((2, ROWS - 3),)
OUTER = ((0, 1), (ROWS - 2, ROWS - 1))
OUTER_ROWS = (0, 1, ROWS - 2, ROWS - 1)
KEPT = (1, 2, ROWS - 3, ROWS - 2)


def inner_kernel(
    lat_total, t, s, u, v, depth, own, side_0, side_1, u_next, v_next, sums, inner, kept,
    sum_x, sum_y, sum_u, sum_v,
):
    near, dep = Around(own, side_0, side_1), Depths(inner)
    dep.build_inner(near, depth)

    def write(g, r, new_u, new_v):
        u_next[GROUPS * r + g] = new_u
        v_next[GROUPS * r + g] = new_v

    momentum_levels(
        near, dep, lat_total, INNER, False, t, s, u, v, write, kept, sum_x, sum_y, sum_u, sum_v
    )
    sums[...] = jnp.zeros(sums.shape, jnp.float32)
    write_sums(INNER, sum_u, sum_v, sums)


def outer_kernel(
    lat_total, t, s, u, v, depth, prior, own, side_0, side_1, swap_0, swap_1, corner_0, corner_1,
    sums, inner, kept, u_outer, v_outer, block, strip_0, strip_1, outer, sum_x, sum_y, sum_u, sum_v, total,
):
    near = Around(own, side_0, side_1, swap_0, swap_1, corner_0, corner_1)
    dep = Depths(inner, outer)
    dep.build_outer(near)
    total[...] = sums[...]

    def write(g, r, new_u, new_v):
        u_outer[OUTER_ROWS.index(r), g] = new_u
        v_outer[OUTER_ROWS.index(r), g] = new_v

    momentum_levels(
        near, dep, lat_total, OUTER, True, t, s, u, v, write, kept, sum_x, sum_y, sum_u, sum_v
    )
    write_sums(OUTER, sum_u, sum_v, total)
    quarter = lanes() // 32
    for half in range(2):
        rows = slice(GROUP * half, GROUP * (half + 1))
        planes = [depth[rows, :], prior[rows, :], total[half], total[2 + half]]
        for plane, x in enumerate(planes):
            block[2 * plane + half] = x
        strips = []
        for first in (96, 0):
            strip = jnp.zeros(TILE, jnp.float32)
            for plane, x in enumerate(planes):
                strip = jnp.where(quarter == plane, turn(x, 32 * plane - first), strip)
            strips.append(strip)
        strip_0[half] = jnp.where(near.lon_even, strips[0], strips[1])
        strip_1[half] = jnp.where(near.lon_even, strips[1], strips[0])


def merge_kernel(u_inner, v_inner, u_outer, v_outer, u_next, v_next, parting):
    for inner, outer, out in ((u_inner, u_outer, u_next), (v_inner, v_outer, v_next)):
        for g in range(GROUPS):
            for r in range(ROWS):
                tile = outer[OUTER_ROWS.index(r), g] if r in OUTER_ROWS else inner[GROUPS * r + g]
                out[pl.ds(GROUP * ROWS * g + r, GROUP, stride=ROWS), :] = tile
    source = lax.broadcasted_iota(jnp.int32, parting.shape, 0)
    target = lax.broadcasted_iota(jnp.int32, parting.shape, 1)
    rim = source - COLS
    column = jnp.where(
        source < COLS, source + 32, jnp.where(rim < 32, rim + 160, jnp.where(rim >= 96, rim - 96, -1))
    )
    wanted = jnp.where(target < COLS, 2 * target, 2 * (target - COLS) + 1)
    parting[...] = jnp.where(column == wanted, 1.0, 0.0).astype(jnp.bfloat16)


def tracer_kernel(
    part, t, s, u, v, own, side_0, side_1, swap_0, swap_1, corner_0, corner_1, inner, outer, t_next, s_next
):
    near = Around(own, side_0, side_1, swap_0, swap_1, corner_0, corner_1)
    dep = Depths(inner, outer)
    sub = sublanes()

    def body(g, carry):
        start = GROUP * ROWS * g - PART * part
        level = (GROUP * g + sub).astype(jnp.float32)
        edges = Edges(near, g, level, (0,), True)
        wet, q, sides, lap, flow, count = {}, {}, {}, {}, {}, {}
        for j in range(-2, ROWS + 2):
            wet[j] = level < dep.tile(j, 0)
            q[j] = [masked(wet[j], near.level_row(ref, i, g, j)) for i, ref in ((0, t), (1, s))]
            if -1 <= j <= ROWS:
                flow[j] = [masked(wet[j], near.level_row(ref, i, g, j)) for i, ref in ((2, u), (3, v))]
            if j >= 0:
                lap[j - 1], sides[j - 1], count[j - 1] = laplace_row(
                    near, dep, level, wet, q, edges, 0, j - 1
                )
            r = j - 2
            if r < 0:
                continue
            e, w = near.sideways(flow[r][0], edges.ring[1], 0, r)
            u_e = masked(level < dep.tile(r, 1), flow[r][0] + e)
            u_w = masked(level < dep.tile(r, 2), flow[r][0] + w)
            v_n = masked(wet[r + 1], flow[r][1] + flow[r + 1][1])
            v_s = masked(wet[r - 1], flow[r][1] + flow[r - 1][1])
            for f, out in ((0, t_next), (1, s_next)):
                e, w = near.sideways(lap[r][f], edges.lap[0], f, r)
                mix = (e + w) + (lap[r + 1][f] + lap[r - 1][f]) - count[r] * lap[r][f]
                mid = q[r][f]
                e, w = sides[r][f]
                advected = (u_e * (mid + e) - u_w * (mid + w)) + (
                    v_n * (mid + q[r + 1][f]) - v_s * (mid + q[r - 1][f])
                )
                out[pl.ds(start + r, GROUP, stride=ROWS), :] = masked(
                    wet[r],
                    mid - (0.25 * TIME_STEP * advected + TIME_STEP * MIX_TRACER * mix),
                )
        return carry

    lax.fori_loop(2 * part, 2 * part + 2, body, 0)


def store_kernel(levels, u_next, v_next, *refs):
    pieces, (t_out, s_out, u_out, v_out, stored, sems, sems_flow) = refs[:-7], refs[-7:]
    stored[...] = jnp.zeros(TILE, jnp.float32)
    copies = []
    for i, (src, dst) in enumerate(((u_next, u_out), (v_next, v_out))):
        copies.append(
            pltpu.make_async_copy(src.at[pl.ds(0, levels * ROWS), :], dst, sems_flow.at[i])
        )
    for part in range(PARTS):
        size = min(PART, levels * ROWS - PART * part)
        for i, dst in enumerate((t_out, s_out)):
            copies.append(
                pltpu.make_async_copy(
                    pieces[2 * part + i].at[pl.ds(0, size), :],
                    dst.at[pl.ds(PART * part, size), :],
                    sems.at[2 * part + i],
                )
            )
    for copy in copies:
        copy.start()
    for copy in copies:
        copy.wait()


STEPS = 5 * ROWS // GROUP


class Plane:
    def __init__(self, even, odd):
        self.even, self.odd = even, odd

    def map(self, other, fn):
        if isinstance(other, Plane):
            return Plane(
                [fn(a, b) for a, b in zip(self.even, other.even)],
                [fn(a, b) for a, b in zip(self.odd, other.odd)],
            )
        return Plane([fn(a, other) for a in self.even], [fn(a, other) for a in self.odd])

    def __add__(self, other):
        return self.map(other, lambda a, b: a + b)

    def __sub__(self, other):
        return self.map(other, lambda a, b: a - b)

    def __mul__(self, other):
        return self.map(other, lambda a, b: a * b)

    def low(self, other):
        return self.map(other, jnp.minimum)

    def east(self):
        return Plane(self.odd, [turn(x, -1) for x in self.even])

    def west(self):
        return Plane([turn(x, 1) for x in self.odd], self.even)

    def north(self):
        return Plane(*[x[1:] + [turn(x[0], -1, 0)] for x in (self.even, self.odd)])

    def south(self):
        return Plane(*[[turn(x[-1], 1, 0)] + x[:-1] for x in (self.even, self.odd)])


def one_hot(x, matrix, side, terms):
    total = None
    for _ in range(terms):
        term = x.astype(jnp.bfloat16)
        x = x - term.astype(jnp.float32)
        product = lax.dot_general(
            term, matrix, (((1,), (side,)), ((), ())), preferred_element_type=jnp.float32
        )
        total = product if total is None else total + product
    return total


def solve_kernel(levels, own, core, chip_0, chip_1, passed, parting, stored, out, own_buf, rim_buf):
    del stored
    lat, _ = place()
    lat_even, lon_even = evens()
    chip_even = lat // 2 % 2 == 0
    lane = lanes()

    def tile(b, index):
        if b == 0:
            return own[index]
        if abs(b) == 2:
            to_first = chip_even if b > 0 else jnp.logical_not(chip_even)
            return jnp.where(to_first, chip_0[index], chip_1[index])
        on_chip = lat_even if b > 0 else jnp.logical_not(lat_even)
        return jnp.where(on_chip, core[index], passed[index])

    def gather(plane):
        for b in range(-2, 3):
            inside = (lat + b >= 0) & (lat + b < lax.axis_size("lat"))
            for half in range(2):
                at = ROWS * (b + 2) + GROUP * half
                mid = tile(b, 2 * plane + half)
                first, second = tile(b, BLOCK + half), tile(b, BLOCK + STRIP + half)
                east = turn(jnp.where(lon_even, first, second), -32 * plane)
                west = turn(jnp.where(lon_even, second, first), 96 - 32 * plane)
                rim = jnp.where(lane < 32, east, jnp.where(lane >= 96, west, 0.0))
                if b != 0:
                    mid, rim = jnp.where(inside, mid, 0.0), jnp.where(inside, rim, 0.0)
                own_buf[at : at + GROUP, :] = mid
                rim_buf[at : at + GROUP, :] = rim
        both = one_hot(
            jnp.concatenate([own_buf[...], rim_buf[...]], axis=1), parting[...], 0, 1 if plane == 0 else 3
        )
        own_buf[...], rim_buf[...] = both[:, :COLS], both[:, COLS:]
        return Plane(
            *[[buf[pl.ds(t, GROUP, stride=STEPS), :] for t in range(STEPS)] for buf in (own_buf, rim_buf)]
        )

    depth, prior, zonal, northward = [gather(plane) for plane in range(4)]

    ocean = depth.map(0.0, lambda a, b: jnp.where(a > b, 1.0, 0.0))
    depth_east, depth_north = depth.low(depth.east()), depth.low(depth.north())
    zonal_flow = zonal.map(depth_east, lambda a, b: masked(b > 0.0, a))
    north_flow = northward.map(depth_north, lambda a, b: masked(b > 0.0, a))
    divergence = (zonal_flow - zonal_flow.west()) + (north_flow - north_flow.south())
    right_side = prior * SURFACE_TERM - divergence * TRANSPORT_SCALE
    east_face, north_face = depth_east * (1.0 / levels), depth_north * (1.0 / levels)
    west_face, south_face = east_face.west(), north_face.south()
    diagonal = (((east_face + west_face) + north_face) + south_face) + SURFACE_TERM
    inverse = diagonal.map(1.0, lambda a, b: b / a)
    right_side, east_face, west_face, north_face, south_face = [
        x * inverse for x in (right_side, east_face, west_face, north_face, south_face)
    ]
    height, change = prior, None
    scales, carries = chebyshev_weights(ITERATIONS)
    for scale, carry in zip(scales, carries):
        spread = (east_face * height.east() + west_face * height.west()) + (
            north_face * height.north() + south_face * height.south()
        )
        residual = (right_side - height) + spread
        step = residual * scale
        change = step if change is None else step + change * carry
        height = height + change
    height = height * ocean
    for t in range(STEPS):
        own_buf[pl.ds(t, GROUP, stride=STEPS), :] = height.even[t]
        rim_buf[pl.ds(t, GROUP, stride=STEPS), :] = height.odd[t]
    rows = slice(2 * ROWS, 3 * ROWS)
    out[...] = one_hot(
        jnp.concatenate([own_buf[rows, :], rim_buf[rows, :]], axis=1), parting[:COLS, :], 1, 3
    )


def join_kernel(count, *refs):
    at = 0
    for ref in refs[:count]:
        refs[-1][at : at + ref.shape[0]] = ref[...]
        at += ref.shape[0]


def pass_kernel(chip_0, chip_1, *refs):
    lat, _ = place()
    refs[-1][...] = jnp.where((lat % 2 == 0) == (lat // 2 % 2 == 0), chip_0[...], chip_1[...])


def swap(value, axis, partner):
    count = lax.axis_size(axis)
    return lax.ppermute(value, axis, [(i, partner(i) % count) for i in range(count)])


def even_first(i):
    return i + 1 if i % 2 == 0 else i - 1


def odd_first(i):
    return i - 1 if i % 2 == 0 else i + 1


def chip_even_first(i):
    return i + 2 if i // 2 % 2 == 0 else i - 2


def chip_odd_first(i):
    return i - 2 if i // 2 % 2 == 0 else i + 2


def shape(*dims):
    return jax.ShapeDtypeStruct(dims, jnp.float32)


VMEM = pl.BlockSpec(memory_space=pltpu.VMEM)
ANY = pl.BlockSpec(memory_space=pl.ANY)
HBM = pl.BlockSpec(memory_space=pltpu.HBM)


def call(kernel, outs, scratch, *args, ins=None, out_specs=None):
    return pl.pallas_call(
        kernel,
        out_shape=outs,
        in_specs=ins or [VMEM] * len(args),
        out_specs=out_specs or jax.tree.map(lambda _: VMEM, outs),
        scratch_shapes=scratch,
        compiler_params=pltpu.CompilerParams(vmem_limit_bytes=32 * 2**20),
        cost_estimate=pl.CostEstimate(flops=0, bytes_accessed=4 * 2**20, transcendentals=0),
    )(*args)


def per_device(
    heat_anomaly,
    saltiness_anomaly,
    zonal_current_array,
    meridional_current_array,
    sea_height_prior,
    ocean_layer_number,
):
    levels, rows, cols = heat_anomaly.shape
    lat_total = rows * lax.axis_size("lat")
    fields = [
        x.reshape(levels * rows, cols)
        for x in (heat_anomaly, saltiness_anomaly, zonal_current_array, meridional_current_array)
    ]
    padded, plane = shape(PADDED, cols), shape(rows, cols)

    def tiles(n):
        return shape(n, *TILE)

    by_rows = tiles(ROWS * GROUPS)

    *kept, own, to_0, to_1, depth, prior = call(
        functools.partial(load_kernel, levels),
        (by_rows,) * 4 + (tiles(PACKS + 1), tiles(SIDE), tiles(SIDE), plane, plane),
        [
            pltpu.VMEM((rows, cols), jnp.int32),
            *[pltpu.VMEM((PADDED, cols), jnp.float32)] * 4,
            pltpu.SemaphoreType.DMA((4 * LOADS,)),
            pltpu.SemaphoreType.DMA((2,)),
        ],
        *[
            pltpu.with_memory_space_constraint(x, pltpu.HBM)
            for x in (*fields, ocean_layer_number, sea_height_prior)
        ],
        ins=[HBM] * 6,
    )
    sides = (own, swap(to_0, "lon", even_first), swap(to_1, "lon", odd_first))
    rows_0, rows_1 = call(rows_kernel, (tiles(HALO + 2),) * 2, [], *kept, depth)
    swaps = (swap(rows_0, "lat", even_first), swap(rows_1, "lat", odd_first))
    to_0, to_1 = call(corner_kernel, (tiles(CORNER),) * 2, [], *sides)
    swaps += (swap(to_0, "lat", even_first), swap(to_1, "lat", odd_first))

    scratch = [pltpu.VMEM((GROUP * ROWS, COLS), jnp.float32)] * 2
    scratch += [pltpu.VMEM((ROWS, *TILE), jnp.float32)] * 2
    u_inner, v_inner, sums, inner, kept_laps = call(
        functools.partial(inner_kernel, lat_total),
        (by_rows, by_rows, tiles(4), tiles(3 * ROWS), shape(2 * len(KEPT), GROUPS, *TILE)),
        scratch,
        *kept,
        depth,
        *sides,
    )
    some_rows = shape(len(OUTER_ROWS), GROUPS, *TILE)
    u_outer, v_outer, block, strip_0, strip_1, outer = call(
        functools.partial(outer_kernel, lat_total),
        (some_rows, some_rows, tiles(BLOCK), tiles(STRIP), tiles(STRIP), tiles(12)),
        scratch + [pltpu.VMEM((4, *TILE), jnp.float32)],
        *kept,
        depth,
        prior,
        *sides,
        *swaps,
        sums,
        inner,
        kept_laps,
    )
    matrix = jax.ShapeDtypeStruct((2 * COLS, 2 * COLS), jnp.bfloat16)
    u_next, v_next, parting = call(
        merge_kernel, (padded, padded, matrix), [], u_inner, v_inner, u_outer, v_outer
    )
    pieces = []
    for part in range(PARTS):
        pieces += call(
            functools.partial(tracer_kernel, part),
            (shape(PART, cols),) * 2,
            [],
            *kept,
            *sides,
            *swaps,
            inner,
            outer,
        )

    strips = [swap(strip_0, "lon", even_first), swap(strip_1, "lon", odd_first)]
    made = pieces[:4]
    block = call(
        functools.partial(join_kernel, 3),
        tiles(BLOCK + 2 * STRIP),
        [],
        block,
        *strips,
        *made,
        ins=[VMEM] * 3 + [ANY] * len(made),
    )
    chip_0, chip_1 = swap(block, "lat", chip_even_first), swap(block, "lat", chip_odd_first)
    core = swap(block, "lat", even_first)
    made = [*pieces[4:], u_next, v_next]
    passed = call(
        pass_kernel,
        tiles(BLOCK + 2 * STRIP),
        [],
        chip_0,
        chip_1,
        *made,
        ins=[VMEM] * 2 + [ANY] * len(made),
    )
    passed = swap(passed, "lat", even_first)
    *results, stored = call(
        functools.partial(store_kernel, levels),
        (shape(levels * rows, cols),) * 4 + (shape(*TILE),),
        [pltpu.SemaphoreType.DMA((2 * PARTS,)), pltpu.SemaphoreType.DMA((2,))],
        u_next,
        v_next,
        *pieces,
        out_specs=(HBM,) * 4 + (VMEM,),
    )
    height = call(
        functools.partial(solve_kernel, levels),
        plane,
        [pltpu.VMEM((5 * ROWS, COLS), jnp.float32)] * 2,
        block,
        core,
        chip_0,
        chip_1,
        passed,
        parting,
        stored,
        ins=[VMEM] * 6 + [ANY],
    )
    return *[x.reshape(levels, rows, cols) for x in results], height


def solution(mesh):
    cells, plane = P(None, "lat", "lon"), P("lat", "lon")
    return jax.shard_map(
        per_device,
        mesh=mesh,
        in_specs=(cells,) * 4 + (plane,) * 2,
        out_specs=(cells,) * 4 + (plane,),
        check_vma=False,
    )
```

```python
import functools

import jax
import jax.numpy as jnp
from jax import lax
from jax.experimental import pallas as pl
from jax.experimental.pallas import tpu as pltpu
from jax.sharding import PartitionSpec as P

ITERATIONS = 32

TIME_STEP = 0.1
MIX_TRACER = 0.05
MIX_MOMENTUM = 0.05
HEAT_INDEX = 0.2
SALT_INDEX = 0.2
CORIOLIS = 2.0
SURFACE_TERM = 0.0005
TRANSPORT_SCALE = 0.05

ROWS = 16
COLS = 128
GROUP = 8
GROUPS = 8
TILE = (GROUP, COLS)
PADDED = GROUPS * GROUP * ROWS
PARTS = 4
PART = PADDED // PARTS
LOADS = 4
HALO = 2 * 4 * GROUPS
PACKS = 2 * GROUPS
SIDE = GROUPS + 1
CORNER = 2
BLOCK = 8
STRIP = 2


def chebyshev_weights(total_steps):
    low_bound = SURFACE_TERM / (SURFACE_TERM + 4.0)
    high_bound = 2.0 - low_bound
    spread_ratio = (high_bound - low_bound) / (high_bound + low_bound)
    middle = 0.5 * (high_bound + low_bound)
    weights = [1.0]
    for number in range(1, total_steps):
        if number == 1:
            weights.append(2.0 / (2.0 - spread_ratio * spread_ratio))
        else:
            weights.append(1.0 / (1.0 - spread_ratio * spread_ratio * weights[-1] / 4.0))
    return [weight / middle for weight in weights], [weight - 1.0 for weight in weights]


def lanes():
    return lax.broadcasted_iota(jnp.int32, TILE, 1)


def sublanes():
    return lax.broadcasted_iota(jnp.int32, TILE, 0)


def turn(value, by, axis=1):
    size = value.shape[axis]
    by = by % size
    return value if by == 0 else pltpu.roll(value, by, axis)


def row_of(ref, row):
    return jnp.broadcast_to(ref[pl.ds(row, 1), :], TILE)


def masked(mask, value):
    return jnp.where(mask, value, 0.0)


def place():
    return lax.axis_index("lat"), lax.axis_index("lon")


def evens():
    lat, lon = place()
    return lat % 2 == 0, lon % 2 == 0


def load_kernel(
    levels, t, s, u, v, depth_in, prior_in, t_out, s_out, u_out, v_out, own, side_0, side_1, depth_out,
    prior, depth, t_buf, s_buf, u_buf, v_buf, sems, sems_plane,
):
    _, lon_even = evens()
    fields, outs, kept = (t, s, u, v), (t_out, s_out, u_out, v_out), (t_buf, s_buf, u_buf, v_buf)
    planes = [
        pltpu.make_async_copy(src, dst, sems_plane.at[i])
        for i, (src, dst) in enumerate(((depth_in, depth), (prior_in, prior)))
    ]
    copies = []
    for part in range(LOADS):
        first = PADDED // LOADS * part
        span = pl.ds(first, min(PADDED // LOADS, levels * ROWS - first))
        for field in range(4):
            copies.append(
                pltpu.make_async_copy(
                    fields[field].at[span, :], kept[field].at[span, :], sems.at[4 * part + field]
                )
            )
    for copy in planes + copies:
        copy.start()
    for copy in planes:
        copy.wait()
    for half in range(2):
        rows = slice(GROUP * half, GROUP * (half + 1))
        depth_out[rows, :] = depth[rows, :].astype(jnp.float32)
    lane = lanes()
    slot, low = lane // 4, (lane & 3) < 2
    pack = jnp.zeros(TILE, jnp.float32)
    for r in range(ROWS):
        x = row_of(depth_out, r)
        for f in range(2):
            pack = jnp.where(slot == 16 * f + r, turn(x, 64 * f + 4 * r + 2), pack)
    own[PACKS] = pack
    side_0[GROUPS] = pack
    side_1[GROUPS] = pack

    def body(g, carry):
        packs = []
        for pair in range(2):
            pack = jnp.zeros(TILE, jnp.float32)
            for f in range(2):
                for r in range(ROWS):
                    x = kept[2 * pair + f][pl.ds(GROUP * ROWS * g + r, GROUP, stride=ROWS), :]
                    outs[2 * pair + f][GROUPS * r + g] = x
                    pack = jnp.where(slot == 16 * f + r, turn(x, 64 * f + 4 * r + 2), pack)
            own[pair * GROUPS + g] = pack
            packs.append(pack)
        to_east = jnp.where(low, packs[0], turn(packs[1], 2))
        to_west = jnp.where(low, turn(packs[1], -2), packs[0])
        side_0[g] = jnp.where(lon_even, to_east, to_west)
        side_1[g] = jnp.where(lon_even, to_west, to_east)
        return carry

    for part in range(LOADS):
        for copy in copies[4 * part : 4 * part + 4]:
            copy.wait()
        for g in range(GROUPS // LOADS * part, GROUPS // LOADS * (part + 1)):
            body(g, 0)


def rows_kernel(t, s, u, v, depth, swap_0, swap_1):
    lat_even, _ = evens()
    fields = (t, s, u, v)
    outer = jnp.where(lat_even, ROWS - 2, 0)

    def body(g, carry):
        for field in range(4):
            for r in range(2):
                for swap, row in ((swap_0, outer), (swap_1, ROWS - 2 - outer)):
                    swap[(r * 4 + field) * GROUPS + g] = fields[field][GROUPS * (row + r) + g]
        return carry

    lax.fori_loop(0, GROUPS, body, 0)
    for half in range(2):
        x = depth[GROUP * half : GROUP * (half + 1), :]
        swap_0[HALO + half] = x
        swap_1[HALO + half] = x


class Around:
    def __init__(self, own, side_0, side_1, swap_0=None, swap_1=None, corner_0=None, corner_1=None):
        lat, _ = place()
        self.lat_even, self.lon_even = evens()
        self.first, self.final = lat == 0, lat == lax.axis_size("lat") - 1
        lane = lanes()
        self.lane, self.column, self.row = lane, lane & 3, (lane // 4) & 15
        self.low, self.column_2 = self.column < 2, self.column == 2
        self.own, self.sides, self.swaps = own, (side_0, side_1), (swap_0, swap_1)
        self.corners = corner_0, corner_1

    def beside(self, tile):
        a, b = self.sides[0][tile], self.sides[1][tile]
        return jnp.where(self.lon_even, a, b), jnp.where(self.lon_even, b, a)

    def beyond(self, north, index):
        a, b = self.swaps if north else self.swaps[::-1]
        return jnp.where(self.lat_even, a[index], b[index])

    def cornered(self, north, index):
        a, b = self.corners if north else self.corners[::-1]
        return jnp.where(self.lat_even, a[index], b[index])

    def columns(self, pair, g):
        east, west = self.beside(g)
        if pair == 1:
            east, west = turn(east, 2), turn(west, -2)
        own = self.own[pair * GROUPS + g]
        return jnp.where(self.low, west, own), jnp.where(self.low, own, east)

    def depth_columns(self):
        east, west = self.beside(GROUPS)
        own = self.own[PACKS]
        return jnp.where(self.low, west, own), jnp.where(self.low, own, east)

    def corner(self, pair, g):
        at = 4 * (g + GROUPS * pair)
        south = pltpu.roll(self.cornered(False, 0), (COLS - at) % COLS, 1)
        north = pltpu.roll(self.cornered(True, 0), (COLS + 60 - at) % COLS, 1)
        return jnp.where(self.row == 0, south, north)

    def corner_depth(self):
        south = jnp.where(self.first, 0.0, self.cornered(False, 1))
        north = jnp.where(self.final, 0.0, self.cornered(True, 1))
        return jnp.where(self.row == 0, south, north)

    def row_depth(self, j):
        if j < 0:
            x, outside = self.beyond(False, HALO + 1)[GROUP + j : GROUP + j + 1, :], self.first
        else:
            x, outside = self.beyond(True, HALO)[j - ROWS : j - ROWS + 1, :], self.final
        return jnp.where(outside, 0.0, jnp.broadcast_to(x, TILE))

    def level_row(self, ref, field, g, j):
        if 0 <= j < ROWS:
            return ref[GROUPS * j + g]
        return self.beyond(j >= ROWS, ((j - ROWS if j >= ROWS else j + 2) * 4 + field) * GROUPS + g)

    def neighbours(self, q, corner):
        north = jnp.where(self.row == ROWS - 1, corner, turn(q, -4))
        south = jnp.where(self.row == 0, corner, turn(q, 4))
        return turn(q, -1), turn(q, 1), north, south

    def join(self, west, east):
        return jnp.where(self.column_2, east, turn(west, 2))

    def sideways(self, q, edge, f, r):
        edge = turn(edge, 127 - (64 * f + 4 * r + 2))
        east = jnp.where(self.lane == COLS - 1, edge, turn(q, -1))
        west = jnp.where(self.lane == 0, edge, turn(q, 1))
        return east, west


def corner_kernel(own, side_0, side_1, corner_0, corner_1):
    near = Around(own, side_0, side_1)
    slot = near.row
    for corner, upper in ((corner_0, near.lat_even), (corner_1, jnp.logical_not(near.lat_even))):
        from_row = jnp.where(upper, 4 * (ROWS - 1), 0)
        tile = jnp.zeros(TILE, jnp.float32)
        for pair in range(2):
            for g in range(GROUPS):
                west, east = near.columns(pair, g)
                at = g + GROUPS * pair
                moved = pltpu.roll(jnp.where(near.low, west, east), (4 * at + COLS - from_row) % COLS, 1)
                tile = jnp.where(slot == at, moved, tile)
        corner[0] = tile
        west, east = near.depth_columns()
        shift = jnp.where(upper, COLS - 60, 60)
        corner[1] = pltpu.roll(jnp.where(near.low, west, east), shift, 1)


class Depths:
    def __init__(self, inner, outer=None):
        self.inner, self.outer = inner, outer

    def tile(self, j, which):
        if 0 <= j < ROWS:
            return self.inner[3 * j + which]
        return self.outer[3 * (j + 2 if j < 0 else j - ROWS + 2) + which]

    def build_inner(self, near, depth):
        ring = near.join(*near.depth_columns())
        for j in range(ROWS):
            d = row_of(depth, j)
            self.inner[3 * j] = d
            self.inner[3 * j + 1], self.inner[3 * j + 2] = near.sideways(d, ring, 0, j)

    def build_outer(self, near):
        corner = near.corner_depth()
        ring = near.join(corner, corner)
        for j in (-2, -1, ROWS, ROWS + 1):
            at = 3 * (j + 2 if j < 0 else j - ROWS + 2)
            d = near.row_depth(j)
            self.outer[at] = d
            d_e, d_w = near.sideways(d, ring, 0, 0 if j < 0 else ROWS - 1)
            self.outer[at + 1], self.outer[at + 2] = d_e, d_w


class Edges:
    def __init__(self, near, g, level, with_laplacian, corners):
        self.ring, self.corner, self.lap = {}, {}, {}
        corner_d = near.corner_depth() if corners else jnp.zeros(TILE, jnp.float32)
        depths = [(d, *near.neighbours(d, corner_d)) for d in near.depth_columns()]
        for pair in range(2):
            corner = jnp.zeros(TILE, jnp.float32)
            if corners:
                corner = masked(level < corner_d, near.corner(pair, g))
            sides, laps = [], []
            for q, d_all in zip(near.columns(pair, g), depths):
                here = level < d_all[0]
                q = masked(here, q)
                sides.append(q)
                if pair in with_laplacian:
                    e, w, n, s = near.neighbours(q, corner)
                    count = sum(jnp.where(level < d, 1.0, 0.0) for d in d_all[1:])
                    laps.append(masked(here, ((e + w) + n) + s - count * q))
            self.ring[pair] = near.join(*sides)
            self.corner[pair] = near.join(corner, corner)
            if laps:
                self.lap[pair] = near.join(*laps)

    def edge(self, pair, j):
        return self.ring[pair] if 0 <= j < ROWS else self.corner[pair]


def prefix(x, sub):
    for by in (1, 2, 4):
        x = x + jnp.where(sub >= by, turn(x, by, 0), 0.0)
    return x


def wet_sides(dep, level, wet, j):
    return (
        jnp.where(level < dep.tile(j, 1), 1.0, 0.0) + jnp.where(level < dep.tile(j, 2), 1.0, 0.0)
    ) + (jnp.where(wet[j + 1], 1.0, 0.0) + jnp.where(wet[j - 1], 1.0, 0.0))


def laplace_row(near, dep, level, wet, q, edges, pair, j):
    count = wet_sides(dep, level, wet, j)
    laps, sides = [], []
    for f in range(2):
        e, w = near.sideways(q[j][f], edges.edge(pair, j), f, min(max(j, 0), ROWS - 1))
        sides.append((e, w))
        total = (e + w) + (q[j + 1][f] + q[j - 1][f])
        laps.append(masked(wet[j], total - count * q[j][f]))
    return laps, sides, count


def momentum_levels(
    near, dep, lat_total, windows, corners, t, s, u, v, write, kept, sum_x, sum_y, sum_u, sum_v
):
    sub = sublanes()
    zero = jnp.zeros(TILE, jnp.float32)
    for first, last in windows:
        for r in range(first, last + 1):
            for ref in (sum_x, sum_y):
                ref[GROUP * r : GROUP * (r + 1), :] = zero
            for ref in (sum_u, sum_v):
                ref[r] = zero
    first_row = (place()[0] * ROWS).astype(jnp.float32)

    def body(g, carry):
        level = (GROUP * g + sub).astype(jnp.float32)
        edges = Edges(near, g, level, (1,), corners)
        edge_load = turn(edges.ring[0], 64) - edges.ring[0]
        for first, last in windows:
            wet, q, lap, dens, count = {}, {}, {}, {}, {}
            for j in range(first - 2, last + 3):
                if not corners or j not in (3, ROWS - 4):
                    wet[j] = level < dep.tile(j, 0)
                    q[j] = [masked(wet[j], near.level_row(ref, i, g, j)) for i, ref in ((2, u), (3, v))]
                if first - 1 <= j <= last + 1:
                    dens[j] = masked(wet[j], near.level_row(s, 1, g, j) - near.level_row(t, 0, g, j))
                i = j - 1
                if j >= first:
                    if corners and i in KEPT:
                        lap[i] = [kept[KEPT.index(i) * 2 + f, g] for f in range(2)]
                        if first <= i <= last:
                            count[i] = wet_sides(dep, level, wet, i)
                    else:
                        lap[i], _, count[i] = laplace_row(near, dep, level, wet, q, edges, 1, i)
                        if not corners and i in KEPT:
                            for f in range(2):
                                kept[KEPT.index(i) * 2 + f, g] = lap[i][f]
                r = j - 2
                if r < first:
                    continue
                mixes = []
                for f in range(2):
                    e, w = near.sideways(lap[r][f], edges.lap[1], f, r)
                    mixes.append((e + w) + (lap[r + 1][f] + lap[r - 1][f]) - count[r] * lap[r][f])
                e, w = near.sideways(dens[r], edge_load, 0, r)
                final = GROUP * r + GROUP - 1
                grad_x = prefix(e - w, sub) + row_of(sum_x, final)
                grad_y = prefix(dens[r + 1] - dens[r - 1], sub) + row_of(sum_y, final)
                sum_x[GROUP * r : GROUP * (r + 1), :] = grad_x
                sum_y[GROUP * r : GROUP * (r + 1), :] = grad_y
                turning = TIME_STEP * CORIOLIS * (2.0 * (first_row + (r + 0.5)) / lat_total - 1.0)
                pull = TIME_STEP * 0.5 * SALT_INDEX
                mix = TIME_STEP * MIX_MOMENTUM
                new_u = masked(
                    wet[r], q[r][0] + ((turning * q[r][1] - pull * grad_x) - mix * mixes[0])
                )
                new_v = masked(
                    wet[r], q[r][1] - ((turning * q[r][0] + pull * grad_y) + mix * mixes[1])
                )
                write(g, r, new_u, new_v)
                sum_u[r] += new_u
                sum_v[r] += new_v
        return carry

    lax.fori_loop(0, GROUPS, body, 0, unroll=4 if corners else 1)


def write_sums(windows, sum_u, sum_v, block):
    for first, last in windows:
        for r in range(first, last + 1):
            half, row = divmod(r, GROUP)
            block[half, row : row + 1, :] = jnp.sum(sum_u[r], axis=0, keepdims=True)
            block[2 + half, row : row + 1, :] = jnp.sum(sum_v[r], axis=0, keepdims=True)


INNER = ((2, ROWS - 3),)
OUTER = ((0, 1), (ROWS - 2, ROWS - 1))
OUTER_ROWS = (0, 1, ROWS - 2, ROWS - 1)
KEPT = (1, 2, ROWS - 3, ROWS - 2)


def inner_kernel(
    lat_total, t, s, u, v, depth, own, side_0, side_1, u_next, v_next, sums, inner, kept,
    sum_x, sum_y, sum_u, sum_v,
):
    near, dep = Around(own, side_0, side_1), Depths(inner)
    dep.build_inner(near, depth)

    def write(g, r, new_u, new_v):
        u_next[GROUPS * r + g] = new_u
        v_next[GROUPS * r + g] = new_v

    momentum_levels(
        near, dep, lat_total, INNER, False, t, s, u, v, write, kept, sum_x, sum_y, sum_u, sum_v
    )
    sums[...] = jnp.zeros(sums.shape, jnp.float32)
    write_sums(INNER, sum_u, sum_v, sums)


def outer_kernel(
    lat_total, t, s, u, v, depth, prior, own, side_0, side_1, swap_0, swap_1, corner_0, corner_1,
    sums, inner, kept, u_outer, v_outer, block, strip_0, strip_1, outer, sum_x, sum_y, sum_u, sum_v, total,
):
    near = Around(own, side_0, side_1, swap_0, swap_1, corner_0, corner_1)
    dep = Depths(inner, outer)
    dep.build_outer(near)
    total[...] = sums[...]

    def write(g, r, new_u, new_v):
        u_outer[OUTER_ROWS.index(r), g] = new_u
        v_outer[OUTER_ROWS.index(r), g] = new_v

    momentum_levels(
        near, dep, lat_total, OUTER, True, t, s, u, v, write, kept, sum_x, sum_y, sum_u, sum_v
    )
    write_sums(OUTER, sum_u, sum_v, total)
    quarter = lanes() // 32
    for half in range(2):
        rows = slice(GROUP * half, GROUP * (half + 1))
        planes = [depth[rows, :], prior[rows, :], total[half], total[2 + half]]
        for plane, x in enumerate(planes):
            block[2 * plane + half] = x
        strips = []
        for first in (96, 0):
            strip = jnp.zeros(TILE, jnp.float32)
            for plane, x in enumerate(planes):
                strip = jnp.where(quarter == plane, turn(x, 32 * plane - first), strip)
            strips.append(strip)
        strip_0[half] = jnp.where(near.lon_even, strips[0], strips[1])
        strip_1[half] = jnp.where(near.lon_even, strips[1], strips[0])


def merge_kernel(u_inner, v_inner, u_outer, v_outer, u_next, v_next, parting):
    for inner, outer, out in ((u_inner, u_outer, u_next), (v_inner, v_outer, v_next)):
        for g in range(GROUPS):
            for r in range(ROWS):
                tile = outer[OUTER_ROWS.index(r), g] if r in OUTER_ROWS else inner[GROUPS * r + g]
                out[pl.ds(GROUP * ROWS * g + r, GROUP, stride=ROWS), :] = tile
    source = lax.broadcasted_iota(jnp.int32, parting.shape, 0)
    target = lax.broadcasted_iota(jnp.int32, parting.shape, 1)
    rim = source - COLS
    column = jnp.where(
        source < COLS, source + 32, jnp.where(rim < 32, rim + 160, jnp.where(rim >= 96, rim - 96, -1))
    )
    wanted = jnp.where(target < COLS, 2 * target, 2 * (target - COLS) + 1)
    parting[...] = jnp.where(column == wanted, 1.0, 0.0).astype(jnp.bfloat16)


def tracer_kernel(
    part, t, s, u, v, own, side_0, side_1, swap_0, swap_1, corner_0, corner_1, inner, outer, t_next, s_next
):
    near = Around(own, side_0, side_1, swap_0, swap_1, corner_0, corner_1)
    dep = Depths(inner, outer)
    sub = sublanes()

    def body(g, carry):
        start = GROUP * ROWS * g - PART * part
        level = (GROUP * g + sub).astype(jnp.float32)
        edges = Edges(near, g, level, (0,), True)
        wet, q, sides, lap, flow, count = {}, {}, {}, {}, {}, {}
        for j in range(-2, ROWS + 2):
            wet[j] = level < dep.tile(j, 0)
            q[j] = [masked(wet[j], near.level_row(ref, i, g, j)) for i, ref in ((0, t), (1, s))]
            if -1 <= j <= ROWS:
                flow[j] = [masked(wet[j], near.level_row(ref, i, g, j)) for i, ref in ((2, u), (3, v))]
            if j >= 0:
                lap[j - 1], sides[j - 1], count[j - 1] = laplace_row(
                    near, dep, level, wet, q, edges, 0, j - 1
                )
            r = j - 2
            if r < 0:
                continue
            e, w = near.sideways(flow[r][0], edges.ring[1], 0, r)
            u_e = masked(level < dep.tile(r, 1), flow[r][0] + e)
            u_w = masked(level < dep.tile(r, 2), flow[r][0] + w)
            v_n = masked(wet[r + 1], flow[r][1] + flow[r + 1][1])
            v_s = masked(wet[r - 1], flow[r][1] + flow[r - 1][1])
            for f, out in ((0, t_next), (1, s_next)):
                e, w = near.sideways(lap[r][f], edges.lap[0], f, r)
                mix = (e + w) + (lap[r + 1][f] + lap[r - 1][f]) - count[r] * lap[r][f]
                mid = q[r][f]
                e, w = sides[r][f]
                advected = (u_e * (mid + e) - u_w * (mid + w)) + (
                    v_n * (mid + q[r + 1][f]) - v_s * (mid + q[r - 1][f])
                )
                out[pl.ds(start + r, GROUP, stride=ROWS), :] = masked(
                    wet[r],
                    mid - (0.25 * TIME_STEP * advected + TIME_STEP * MIX_TRACER * mix),
                )
        return carry

    lax.fori_loop(2 * part, 2 * part + 2, body, 0)


def store_kernel(levels, u_next, v_next, *refs):
    pieces, (t_out, s_out, u_out, v_out, stored, sems, sems_flow) = refs[:-7], refs[-7:]
    stored[...] = jnp.zeros(TILE, jnp.float32)
    copies = []
    for i, (src, dst) in enumerate(((u_next, u_out), (v_next, v_out))):
        copies.append(
            pltpu.make_async_copy(src.at[pl.ds(0, levels * ROWS), :], dst, sems_flow.at[i])
        )
    for part in range(PARTS):
        size = min(PART, levels * ROWS - PART * part)
        for i, dst in enumerate((t_out, s_out)):
            copies.append(
                pltpu.make_async_copy(
                    pieces[2 * part + i].at[pl.ds(0, size), :],
                    dst.at[pl.ds(PART * part, size), :],
                    sems.at[2 * part + i],
                )
            )
    for copy in copies:
        copy.start()
    for copy in copies:
        copy.wait()


STEPS = 5 * ROWS // GROUP


class Plane:
    def __init__(self, even, odd):
        self.even, self.odd = even, odd

    def map(self, other, fn):
        if isinstance(other, Plane):
            return Plane(
                [fn(a, b) for a, b in zip(self.even, other.even)],
                [fn(a, b) for a, b in zip(self.odd, other.odd)],
            )
        return Plane([fn(a, other) for a in self.even], [fn(a, other) for a in self.odd])

    def __add__(self, other):
        return self.map(other, lambda a, b: a + b)

    def __sub__(self, other):
        return self.map(other, lambda a, b: a - b)

    def __mul__(self, other):
        return self.map(other, lambda a, b: a * b)

    def low(self, other):
        return self.map(other, jnp.minimum)

    def east(self):
        return Plane(self.odd, [turn(x, -1) for x in self.even])

    def west(self):
        return Plane([turn(x, 1) for x in self.odd], self.even)

    def north(self):
        return Plane(*[x[1:] + [turn(x[0], -1, 0)] for x in (self.even, self.odd)])

    def south(self):
        return Plane(*[[turn(x[-1], 1, 0)] + x[:-1] for x in (self.even, self.odd)])


def one_hot(x, matrix, side, terms):
    total = None
    for _ in range(terms):
        term = x.astype(jnp.bfloat16)
        x = x - term.astype(jnp.float32)
        product = lax.dot_general(
            term, matrix, (((1,), (side,)), ((), ())), preferred_element_type=jnp.float32
        )
        total = product if total is None else total + product
    return total


def solve_kernel(levels, own, core, chip_0, chip_1, passed, parting, stored, out, own_buf, rim_buf):
    del stored
    lat, _ = place()
    lat_even, lon_even = evens()
    chip_even = lat // 2 % 2 == 0
    lane = lanes()

    def tile(b, index):
        if b == 0:
            return own[index]
        if abs(b) == 2:
            to_first = chip_even if b > 0 else jnp.logical_not(chip_even)
            return jnp.where(to_first, chip_0[index], chip_1[index])
        on_chip = lat_even if b > 0 else jnp.logical_not(lat_even)
        return jnp.where(on_chip, core[index], passed[index])

    def gather(plane):
        for b in range(-2, 3):
            inside = (lat + b >= 0) & (lat + b < lax.axis_size("lat"))
            for half in range(2):
                at = ROWS * (b + 2) + GROUP * half
                mid = tile(b, 2 * plane + half)
                first, second = tile(b, BLOCK + half), tile(b, BLOCK + STRIP + half)
                east = turn(jnp.where(lon_even, first, second), -32 * plane)
                west = turn(jnp.where(lon_even, second, first), 96 - 32 * plane)
                rim = jnp.where(lane < 32, east, jnp.where(lane >= 96, west, 0.0))
                if b != 0:
                    mid, rim = jnp.where(inside, mid, 0.0), jnp.where(inside, rim, 0.0)
                own_buf[at : at + GROUP, :] = mid
                rim_buf[at : at + GROUP, :] = rim
        both = one_hot(
            jnp.concatenate([own_buf[...], rim_buf[...]], axis=1), parting[...], 0, 1 if plane == 0 else 3
        )
        own_buf[...], rim_buf[...] = both[:, :COLS], both[:, COLS:]
        return Plane(
            *[[buf[pl.ds(t, GROUP, stride=STEPS), :] for t in range(STEPS)] for buf in (own_buf, rim_buf)]
        )

    depth, prior, zonal, northward = [gather(plane) for plane in range(4)]

    ocean = depth.map(0.0, lambda a, b: jnp.where(a > b, 1.0, 0.0))
    depth_east, depth_north = depth.low(depth.east()), depth.low(depth.north())
    zonal_flow = zonal.map(depth_east, lambda a, b: masked(b > 0.0, a))
    north_flow = northward.map(depth_north, lambda a, b: masked(b > 0.0, a))
    divergence = (zonal_flow - zonal_flow.west()) + (north_flow - north_flow.south())
    right_side = prior * SURFACE_TERM - divergence * TRANSPORT_SCALE
    east_face, north_face = depth_east * (1.0 / levels), depth_north * (1.0 / levels)
    west_face, south_face = east_face.west(), north_face.south()
    diagonal = (((east_face + west_face) + north_face) + south_face) + SURFACE_TERM
    inverse = diagonal.map(1.0, lambda a, b: b / a)
    right_side, east_face, west_face, north_face, south_face = [
        x * inverse for x in (right_side, east_face, west_face, north_face, south_face)
    ]
    height, change = prior, None
    scales, carries = chebyshev_weights(ITERATIONS)
    for scale, carry in zip(scales, carries):
        spread = (east_face * height.east() + west_face * height.west()) + (
            north_face * height.north() + south_face * height.south()
        )
        residual = (right_side - height) + spread
        step = residual * scale
        change = step if change is None else step + change * carry
        height = height + change
    height = height * ocean
    for t in range(STEPS):
        own_buf[pl.ds(t, GROUP, stride=STEPS), :] = height.even[t]
        rim_buf[pl.ds(t, GROUP, stride=STEPS), :] = height.odd[t]
    rows = slice(2 * ROWS, 3 * ROWS)
    out[...] = one_hot(
        jnp.concatenate([own_buf[rows, :], rim_buf[rows, :]], axis=1), parting[:COLS, :], 1, 3
    )


def join_kernel(count, *refs):
    at = 0
    for ref in refs[:count]:
        refs[-1][at : at + ref.shape[0]] = ref[...]
        at += ref.shape[0]


def pass_kernel(chip_0, chip_1, *refs):
    lat, _ = place()
    refs[-1][...] = jnp.where((lat % 2 == 0) == (lat // 2 % 2 == 0), chip_0[...], chip_1[...])


def swap(value, axis, partner):
    count = lax.axis_size(axis)
    return lax.ppermute(value, axis, [(i, partner(i) % count) for i in range(count)])


def even_first(i):
    return i + 1 if i % 2 == 0 else i - 1


def odd_first(i):
    return i - 1 if i % 2 == 0 else i + 1


def chip_even_first(i):
    return i + 2 if i // 2 % 2 == 0 else i - 2


def chip_odd_first(i):
    return i - 2 if i // 2 % 2 == 0 else i + 2


def shape(*dims):
    return jax.ShapeDtypeStruct(dims, jnp.float32)


VMEM = pl.BlockSpec(memory_space=pltpu.VMEM)
ANY = pl.BlockSpec(memory_space=pl.ANY)
HBM = pl.BlockSpec(memory_space=pltpu.HBM)


def call(kernel, outs, scratch, *args, ins=None, out_specs=None):
    return pl.pallas_call(
        kernel,
        out_shape=outs,
        in_specs=ins or [VMEM] * len(args),
        out_specs=out_specs or jax.tree.map(lambda _: VMEM, outs),
        scratch_shapes=scratch,
        compiler_params=pltpu.CompilerParams(vmem_limit_bytes=32 * 2**20),
        cost_estimate=pl.CostEstimate(flops=0, bytes_accessed=4 * 2**20, transcendentals=0),
    )(*args)


def per_device(
    heat_anomaly,
    saltiness_anomaly,
    zonal_current_array,
    meridional_current_array,
    sea_height_prior,
    ocean_layer_number,
):
    levels, rows, cols = heat_anomaly.shape
    lat_total = rows * lax.axis_size("lat")
    fields = [
        x.reshape(levels * rows, cols)
        for x in (heat_anomaly, saltiness_anomaly, zonal_current_array, meridional_current_array)
    ]
    padded, plane = shape(PADDED, cols), shape(rows, cols)

    def tiles(n):
        return shape(n, *TILE)

    by_rows = tiles(ROWS * GROUPS)

    *kept, own, to_0, to_1, depth, prior = call(
        functools.partial(load_kernel, levels),
        (by_rows,) * 4 + (tiles(PACKS + 1), tiles(SIDE), tiles(SIDE), plane, plane),
        [
            pltpu.VMEM((rows, cols), jnp.int32),
            *[pltpu.VMEM((PADDED, cols), jnp.float32)] * 4,
            pltpu.SemaphoreType.DMA((4 * LOADS,)),
            pltpu.SemaphoreType.DMA((2,)),
        ],
        *[
            pltpu.with_memory_space_constraint(x, pltpu.HBM)
            for x in (*fields, ocean_layer_number, sea_height_prior)
        ],
        ins=[HBM] * 6,
    )
    sides = (own, swap(to_0, "lon", even_first), swap(to_1, "lon", odd_first))
    rows_0, rows_1 = call(rows_kernel, (tiles(HALO + 2),) * 2, [], *kept, depth)
    swaps = (swap(rows_0, "lat", even_first), swap(rows_1, "lat", odd_first))
    to_0, to_1 = call(corner_kernel, (tiles(CORNER),) * 2, [], *sides)
    swaps += (swap(to_0, "lat", even_first), swap(to_1, "lat", odd_first))

    scratch = [pltpu.VMEM((GROUP * ROWS, COLS), jnp.float32)] * 2
    scratch += [pltpu.VMEM((ROWS, *TILE), jnp.float32)] * 2
    u_inner, v_inner, sums, inner, kept_laps = call(
        functools.partial(inner_kernel, lat_total),
        (by_rows, by_rows, tiles(4), tiles(3 * ROWS), shape(2 * len(KEPT), GROUPS, *TILE)),
        scratch,
        *kept,
        depth,
        *sides,
    )
    some_rows = shape(len(OUTER_ROWS), GROUPS, *TILE)
    u_outer, v_outer, block, strip_0, strip_1, outer = call(
        functools.partial(outer_kernel, lat_total),
        (some_rows, some_rows, tiles(BLOCK), tiles(STRIP), tiles(STRIP), tiles(12)),
        scratch + [pltpu.VMEM((4, *TILE), jnp.float32)],
        *kept,
        depth,
        prior,
        *sides,
        *swaps,
        sums,
        inner,
        kept_laps,
    )
    matrix = jax.ShapeDtypeStruct((2 * COLS, 2 * COLS), jnp.bfloat16)
    u_next, v_next, parting = call(
        merge_kernel, (padded, padded, matrix), [], u_inner, v_inner, u_outer, v_outer
    )
    pieces = []
    for part in range(PARTS):
        pieces += call(
            functools.partial(tracer_kernel, part),
            (shape(PART, cols),) * 2,
            [],
            *kept,
            *sides,
            *swaps,
            inner,
            outer,
        )

    strips = [swap(strip_0, "lon", even_first), swap(strip_1, "lon", odd_first)]
    made = pieces[:4]
    block = call(
        functools.partial(join_kernel, 3),
        tiles(BLOCK + 2 * STRIP),
        [],
        block,
        *strips,
        *made,
        ins=[VMEM] * 3 + [ANY] * len(made),
    )
    chip_0, chip_1 = swap(block, "lat", chip_even_first), swap(block, "lat", chip_odd_first)
    core = swap(block, "lat", even_first)
    made = [*pieces[4:], u_next, v_next]
    passed = call(
        pass_kernel,
        tiles(BLOCK + 2 * STRIP),
        [],
        chip_0,
        chip_1,
        *made,
        ins=[VMEM] * 2 + [ANY] * len(made),
    )
    passed = swap(passed, "lat", even_first)
    *results, stored = call(
        functools.partial(store_kernel, levels),
        (shape(levels * rows, cols),) * 4 + (shape(*TILE),),
        [pltpu.SemaphoreType.DMA((2 * PARTS,)), pltpu.SemaphoreType.DMA((2,))],
        u_next,
        v_next,
        *pieces,
        out_specs=(HBM,) * 4 + (VMEM,),
    )
    height = call(
        functools.partial(solve_kernel, levels),
        plane,
        [pltpu.VMEM((5 * ROWS, COLS), jnp.float32)] * 2,
        block,
        core,
        chip_0,
        chip_1,
        passed,
        parting,
        stored,
        ins=[VMEM] * 6 + [ANY],
    )
    return *[x.reshape(levels, rows, cols) for x in results], height


def solution(mesh):
    cells, plane = P(None, "lat", "lon"), P("lat", "lon")
    return jax.shard_map(
        per_device,
        mesh=mesh,
        in_specs=(cells,) * 4 + (plane,) * 2,
        out_specs=(cells,) * 4 + (plane,),
        check_vma=False,
    )
```

```python
import functools

import jax
import jax.numpy as jnp
from jax import lax
from jax.experimental import pallas as pl
from jax.experimental.pallas import tpu as pltpu
from jax.sharding import PartitionSpec as P

ITERATIONS = 32

TIME_STEP = 0.1
MIX_TRACER = 0.05
MIX_MOMENTUM = 0.05
HEAT_INDEX = 0.2
SALT_INDEX = 0.2
CORIOLIS = 2.0
SURFACE_TERM = 0.0005
TRANSPORT_SCALE = 0.05

ROWS = 16
COLS = 128
GROUP = 8
GROUPS = 8
TILE = (GROUP, COLS)
PADDED = GROUPS * GROUP * ROWS
PARTS = 4
PART = PADDED // PARTS
LOADS = 2
HALO = 2 * 4 * GROUPS
PACKS = 2 * GROUPS
SIDE = GROUPS + 1
CORNER = 2
BLOCK = 8
STRIP = 2


def chebyshev_weights(total_steps):
    low_bound = SURFACE_TERM / (SURFACE_TERM + 4.0)
    high_bound = 2.0 - low_bound
    spread_ratio = (high_bound - low_bound) / (high_bound + low_bound)
    middle = 0.5 * (high_bound + low_bound)
    weights = [1.0]
    for number in range(1, total_steps):
        if number == 1:
            weights.append(2.0 / (2.0 - spread_ratio * spread_ratio))
        else:
            weights.append(1.0 / (1.0 - spread_ratio * spread_ratio * weights[-1] / 4.0))
    return [weight / middle for weight in weights], [weight - 1.0 for weight in weights]


def lanes():
    return lax.broadcasted_iota(jnp.int32, TILE, 1)


def sublanes():
    return lax.broadcasted_iota(jnp.int32, TILE, 0)


def turn(value, by, axis=1):
    size = value.shape[axis]
    by = by % size
    return value if by == 0 else pltpu.roll(value, by, axis)


def row_of(ref, row):
    return jnp.broadcast_to(ref[pl.ds(row, 1), :], TILE)


def masked(mask, value):
    return jnp.where(mask, value, 0.0)


def place():
    return lax.axis_index("lat"), lax.axis_index("lon")


def evens():
    lat, lon = place()
    return lat % 2 == 0, lon % 2 == 0


def load_kernel(
    levels, t, s, u, v, depth_in, prior_in, t_out, s_out, u_out, v_out, own, side_0, side_1, depth_out,
    prior, depth, t_buf, s_buf, u_buf, v_buf, sems, sems_plane,
):
    _, lon_even = evens()
    fields, outs, kept = (t, s, u, v), (t_out, s_out, u_out, v_out), (t_buf, s_buf, u_buf, v_buf)
    planes = [
        pltpu.make_async_copy(src, dst, sems_plane.at[i])
        for i, (src, dst) in enumerate(((depth_in, depth), (prior_in, prior)))
    ]
    copies = []
    for part in range(LOADS):
        first = PADDED // LOADS * part
        span = pl.ds(first, min(PADDED // LOADS, levels * ROWS - first))
        for field in range(4):
            copies.append(
                pltpu.make_async_copy(
                    fields[field].at[span, :], kept[field].at[span, :], sems.at[4 * part + field]
                )
            )
    for copy in planes + copies:
        copy.start()
    for copy in planes:
        copy.wait()
    for half in range(2):
        rows = slice(GROUP * half, GROUP * (half + 1))
        depth_out[rows, :] = depth[rows, :].astype(jnp.float32)
    lane = lanes()
    slot, low = lane // 4, (lane & 3) < 2
    pack = jnp.zeros(TILE, jnp.float32)
    for r in range(ROWS):
        x = row_of(depth_out, r)
        for f in range(2):
            pack = jnp.where(slot == 16 * f + r, turn(x, 64 * f + 4 * r + 2), pack)
    own[PACKS] = pack
    side_0[GROUPS] = pack
    side_1[GROUPS] = pack

    def body(g, carry):
        packs = []
        for pair in range(2):
            pack = jnp.zeros(TILE, jnp.float32)
            for f in range(2):
                for r in range(ROWS):
                    x = kept[2 * pair + f][pl.ds(GROUP * ROWS * g + r, GROUP, stride=ROWS), :]
                    outs[2 * pair + f][GROUPS * r + g] = x
                    pack = jnp.where(slot == 16 * f + r, turn(x, 64 * f + 4 * r + 2), pack)
            own[pair * GROUPS + g] = pack
            packs.append(pack)
        to_east = jnp.where(low, packs[0], turn(packs[1], 2))
        to_west = jnp.where(low, turn(packs[1], -2), packs[0])
        side_0[g] = jnp.where(lon_even, to_east, to_west)
        side_1[g] = jnp.where(lon_even, to_west, to_east)
        return carry

    for part in range(LOADS):
        for copy in copies[4 * part : 4 * part + 4]:
            copy.wait()
        for g in range(GROUPS // LOADS * part, GROUPS // LOADS * (part + 1)):
            body(g, 0)


def rows_kernel(t, s, u, v, depth, swap_0, swap_1):
    lat_even, _ = evens()
    fields = (t, s, u, v)
    outer = jnp.where(lat_even, ROWS - 2, 0)

    def body(g, carry):
        for field in range(4):
            for r in range(2):
                for swap, row in ((swap_0, outer), (swap_1, ROWS - 2 - outer)):
                    swap[(r * 4 + field) * GROUPS + g] = fields[field][GROUPS * (row + r) + g]
        return carry

    lax.fori_loop(0, GROUPS, body, 0)
    for half in range(2):
        x = depth[GROUP * half : GROUP * (half + 1), :]
        swap_0[HALO + half] = x
        swap_1[HALO + half] = x


class Around:
    def __init__(self, own, side_0, side_1, swap_0=None, swap_1=None, corner_0=None, corner_1=None):
        lat, _ = place()
        self.lat_even, self.lon_even = evens()
        self.first, self.final = lat == 0, lat == lax.axis_size("lat") - 1
        lane = lanes()
        self.lane, self.column, self.row = lane, lane & 3, (lane // 4) & 15
        self.low, self.column_2 = self.column < 2, self.column == 2
        self.own, self.sides, self.swaps = own, (side_0, side_1), (swap_0, swap_1)
        self.corners = corner_0, corner_1

    def beside(self, tile):
        a, b = self.sides[0][tile], self.sides[1][tile]
        return jnp.where(self.lon_even, a, b), jnp.where(self.lon_even, b, a)

    def beyond(self, north, index):
        a, b = self.swaps if north else self.swaps[::-1]
        return jnp.where(self.lat_even, a[index], b[index])

    def cornered(self, north, index):
        a, b = self.corners if north else self.corners[::-1]
        return jnp.where(self.lat_even, a[index], b[index])

    def columns(self, pair, g):
        east, west = self.beside(g)
        if pair == 1:
            east, west = turn(east, 2), turn(west, -2)
        own = self.own[pair * GROUPS + g]
        return jnp.where(self.low, west, own), jnp.where(self.low, own, east)

    def depth_columns(self):
        east, west = self.beside(GROUPS)
        own = self.own[PACKS]
        return jnp.where(self.low, west, own), jnp.where(self.low, own, east)

    def corner(self, pair, g):
        at = 4 * (g + GROUPS * pair)
        south = pltpu.roll(self.cornered(False, 0), (COLS - at) % COLS, 1)
        north = pltpu.roll(self.cornered(True, 0), (COLS + 60 - at) % COLS, 1)
        return jnp.where(self.row == 0, south, north)

    def corner_depth(self):
        south = jnp.where(self.first, 0.0, self.cornered(False, 1))
        north = jnp.where(self.final, 0.0, self.cornered(True, 1))
        return jnp.where(self.row == 0, south, north)

    def row_depth(self, j):
        if j < 0:
            x, outside = self.beyond(False, HALO + 1)[GROUP + j : GROUP + j + 1, :], self.first
        else:
            x, outside = self.beyond(True, HALO)[j - ROWS : j - ROWS + 1, :], self.final
        return jnp.where(outside, 0.0, jnp.broadcast_to(x, TILE))

    def level_row(self, ref, field, g, j):
        if 0 <= j < ROWS:
            return ref[GROUPS * j + g]
        return self.beyond(j >= ROWS, ((j - ROWS if j >= ROWS else j + 2) * 4 + field) * GROUPS + g)

    def neighbours(self, q, corner):
        north = jnp.where(self.row == ROWS - 1, corner, turn(q, -4))
        south = jnp.where(self.row == 0, corner, turn(q, 4))
        return turn(q, -1), turn(q, 1), north, south

    def join(self, west, east):
        return jnp.where(self.column_2, east, turn(west, 2))

    def sideways(self, q, edge, f, r):
        edge = turn(edge, 127 - (64 * f + 4 * r + 2))
        east = jnp.where(self.lane == COLS - 1, edge, turn(q, -1))
        west = jnp.where(self.lane == 0, edge, turn(q, 1))
        return east, west


def corner_kernel(own, side_0, side_1, corner_0, corner_1):
    near = Around(own, side_0, side_1)
    slot = near.row
    for corner, upper in ((corner_0, near.lat_even), (corner_1, jnp.logical_not(near.lat_even))):
        from_row = jnp.where(upper, 4 * (ROWS - 1), 0)
        tile = jnp.zeros(TILE, jnp.float32)
        for pair in range(2):
            for g in range(GROUPS):
                west, east = near.columns(pair, g)
                at = g + GROUPS * pair
                moved = pltpu.roll(jnp.where(near.low, west, east), (4 * at + COLS - from_row) % COLS, 1)
                tile = jnp.where(slot == at, moved, tile)
        corner[0] = tile
        west, east = near.depth_columns()
        shift = jnp.where(upper, COLS - 60, 60)
        corner[1] = pltpu.roll(jnp.where(near.low, west, east), shift, 1)


class Depths:
    def __init__(self, inner, outer=None):
        self.inner, self.outer = inner, outer

    def tile(self, j, which):
        if 0 <= j < ROWS:
            return self.inner[3 * j + which]
        return self.outer[3 * (j + 2 if j < 0 else j - ROWS + 2) + which]

    def build_inner(self, near, depth):
        ring = near.join(*near.depth_columns())
        for j in range(ROWS):
            d = row_of(depth, j)
            self.inner[3 * j] = d
            self.inner[3 * j + 1], self.inner[3 * j + 2] = near.sideways(d, ring, 0, j)

    def build_outer(self, near):
        corner = near.corner_depth()
        ring = near.join(corner, corner)
        for j in (-2, -1, ROWS, ROWS + 1):
            at = 3 * (j + 2 if j < 0 else j - ROWS + 2)
            d = near.row_depth(j)
            self.outer[at] = d
            d_e, d_w = near.sideways(d, ring, 0, 0 if j < 0 else ROWS - 1)
            self.outer[at + 1], self.outer[at + 2] = d_e, d_w


class Edges:
    def __init__(self, near, g, level, with_laplacian, corners):
        self.ring, self.corner, self.lap = {}, {}, {}
        corner_d = near.corner_depth() if corners else jnp.zeros(TILE, jnp.float32)
        depths = [(d, *near.neighbours(d, corner_d)) for d in near.depth_columns()]
        for pair in range(2):
            corner = jnp.zeros(TILE, jnp.float32)
            if corners:
                corner = masked(level < corner_d, near.corner(pair, g))
            sides, laps = [], []
            for q, d_all in zip(near.columns(pair, g), depths):
                here = level < d_all[0]
                q = masked(here, q)
                sides.append(q)
                if pair in with_laplacian:
                    e, w, n, s = near.neighbours(q, corner)
                    count = sum(jnp.where(level < d, 1.0, 0.0) for d in d_all[1:])
                    laps.append(masked(here, ((e + w) + n) + s - count * q))
            self.ring[pair] = near.join(*sides)
            self.corner[pair] = near.join(corner, corner)
            if laps:
                self.lap[pair] = near.join(*laps)

    def edge(self, pair, j):
        return self.ring[pair] if 0 <= j < ROWS else self.corner[pair]


def prefix(x, sub):
    for by in (1, 2, 4):
        x = x + jnp.where(sub >= by, turn(x, by, 0), 0.0)
    return x


def wet_sides(dep, level, wet, j):
    return (
        jnp.where(level < dep.tile(j, 1), 1.0, 0.0) + jnp.where(level < dep.tile(j, 2), 1.0, 0.0)
    ) + (jnp.where(wet[j + 1], 1.0, 0.0) + jnp.where(wet[j - 1], 1.0, 0.0))


def laplace_row(near, dep, level, wet, q, edges, pair, j):
    count = wet_sides(dep, level, wet, j)
    laps, sides = [], []
    for f in range(2):
        e, w = near.sideways(q[j][f], edges.edge(pair, j), f, min(max(j, 0), ROWS - 1))
        sides.append((e, w))
        total = (e + w) + (q[j + 1][f] + q[j - 1][f])
        laps.append(masked(wet[j], total - count * q[j][f]))
    return laps, sides, count


def momentum_levels(
    near, dep, lat_total, windows, corners, t, s, u, v, write, kept, sum_x, sum_y, sum_u, sum_v
):
    sub = sublanes()
    zero = jnp.zeros(TILE, jnp.float32)
    for first, last in windows:
        for r in range(first, last + 1):
            for ref in (sum_x, sum_y):
                ref[GROUP * r : GROUP * (r + 1), :] = zero
            for ref in (sum_u, sum_v):
                ref[r] = zero
    first_row = (place()[0] * ROWS).astype(jnp.float32)

    def body(g, carry):
        level = (GROUP * g + sub).astype(jnp.float32)
        edges = Edges(near, g, level, (1,), corners)
        edge_load = turn(edges.ring[0], 64) - edges.ring[0]
        for first, last in windows:
            wet, q, lap, dens, count = {}, {}, {}, {}, {}
            for j in range(first - 2, last + 3):
                if not corners or j not in (3, ROWS - 4):
                    wet[j] = level < dep.tile(j, 0)
                    q[j] = [masked(wet[j], near.level_row(ref, i, g, j)) for i, ref in ((2, u), (3, v))]
                if first - 1 <= j <= last + 1:
                    dens[j] = masked(wet[j], near.level_row(s, 1, g, j) - near.level_row(t, 0, g, j))
                i = j - 1
                if j >= first:
                    if corners and i in KEPT:
                        lap[i] = [kept[KEPT.index(i) * 2 + f, g] for f in range(2)]
                        if first <= i <= last:
                            count[i] = wet_sides(dep, level, wet, i)
                    else:
                        lap[i], _, count[i] = laplace_row(near, dep, level, wet, q, edges, 1, i)
                        if not corners and i in KEPT:
                            for f in range(2):
                                kept[KEPT.index(i) * 2 + f, g] = lap[i][f]
                r = j - 2
                if r < first:
                    continue
                mixes = []
                for f in range(2):
                    e, w = near.sideways(lap[r][f], edges.lap[1], f, r)
                    mixes.append((e + w) + (lap[r + 1][f] + lap[r - 1][f]) - count[r] * lap[r][f])
                e, w = near.sideways(dens[r], edge_load, 0, r)
                final = GROUP * r + GROUP - 1
                grad_x = prefix(e - w, sub) + row_of(sum_x, final)
                grad_y = prefix(dens[r + 1] - dens[r - 1], sub) + row_of(sum_y, final)
                sum_x[GROUP * r : GROUP * (r + 1), :] = grad_x
                sum_y[GROUP * r : GROUP * (r + 1), :] = grad_y
                turning = TIME_STEP * CORIOLIS * (2.0 * (first_row + (r + 0.5)) / lat_total - 1.0)
                pull = TIME_STEP * 0.5 * SALT_INDEX
                mix = TIME_STEP * MIX_MOMENTUM
                new_u = masked(
                    wet[r], q[r][0] + ((turning * q[r][1] - pull * grad_x) - mix * mixes[0])
                )
                new_v = masked(
                    wet[r], q[r][1] - ((turning * q[r][0] + pull * grad_y) + mix * mixes[1])
                )
                write(g, r, new_u, new_v)
                sum_u[r] += new_u
                sum_v[r] += new_v
        return carry

    lax.fori_loop(0, GROUPS, body, 0, unroll=4 if corners else 1)


def write_sums(windows, sum_u, sum_v, block):
    for first, last in windows:
        for r in range(first, last + 1):
            half, row = divmod(r, GROUP)
            block[half, row : row + 1, :] = jnp.sum(sum_u[r], axis=0, keepdims=True)
            block[2 + half, row : row + 1, :] = jnp.sum(sum_v[r], axis=0, keepdims=True)


INNER = ((2, ROWS - 3),)
OUTER = ((0, 1), (ROWS - 2, ROWS - 1))
OUTER_ROWS = (0, 1, ROWS - 2, ROWS - 1)
KEPT = (1, 2, ROWS - 3, ROWS - 2)


def inner_kernel(
    lat_total, t, s, u, v, depth, own, side_0, side_1, u_next, v_next, sums, inner, kept,
    sum_x, sum_y, sum_u, sum_v,
):
    near, dep = Around(own, side_0, side_1), Depths(inner)
    dep.build_inner(near, depth)

    def write(g, r, new_u, new_v):
        u_next[GROUPS * r + g] = new_u
        v_next[GROUPS * r + g] = new_v

    momentum_levels(
        near, dep, lat_total, INNER, False, t, s, u, v, write, kept, sum_x, sum_y, sum_u, sum_v
    )
    sums[...] = jnp.zeros(sums.shape, jnp.float32)
    write_sums(INNER, sum_u, sum_v, sums)


def outer_kernel(
    lat_total, t, s, u, v, depth, prior, own, side_0, side_1, swap_0, swap_1, corner_0, corner_1,
    sums, inner, kept, u_outer, v_outer, block, strip_0, strip_1, outer, sum_x, sum_y, sum_u, sum_v, total,
):
    near = Around(own, side_0, side_1, swap_0, swap_1, corner_0, corner_1)
    dep = Depths(inner, outer)
    dep.build_outer(near)
    total[...] = sums[...]

    def write(g, r, new_u, new_v):
        u_outer[OUTER_ROWS.index(r), g] = new_u
        v_outer[OUTER_ROWS.index(r), g] = new_v

    momentum_levels(
        near, dep, lat_total, OUTER, True, t, s, u, v, write, kept, sum_x, sum_y, sum_u, sum_v
    )
    write_sums(OUTER, sum_u, sum_v, total)
    quarter = lanes() // 32
    for half in range(2):
        rows = slice(GROUP * half, GROUP * (half + 1))
        planes = [depth[rows, :], prior[rows, :], total[half], total[2 + half]]
        for plane, x in enumerate(planes):
            block[2 * plane + half] = x
        strips = []
        for first in (96, 0):
            strip = jnp.zeros(TILE, jnp.float32)
            for plane, x in enumerate(planes):
                strip = jnp.where(quarter == plane, turn(x, 32 * plane - first), strip)
            strips.append(strip)
        strip_0[half] = jnp.where(near.lon_even, strips[0], strips[1])
        strip_1[half] = jnp.where(near.lon_even, strips[1], strips[0])


def merge_kernel(u_inner, v_inner, u_outer, v_outer, u_next, v_next, parting):
    for inner, outer, out in ((u_inner, u_outer, u_next), (v_inner, v_outer, v_next)):
        for g in range(GROUPS):
            for r in range(ROWS):
                tile = outer[OUTER_ROWS.index(r), g] if r in OUTER_ROWS else inner[GROUPS * r + g]
                out[pl.ds(GROUP * ROWS * g + r, GROUP, stride=ROWS), :] = tile
    source = lax.broadcasted_iota(jnp.int32, parting.shape, 0)
    target = lax.broadcasted_iota(jnp.int32, parting.shape, 1)
    rim = source - COLS
    column = jnp.where(
        source < COLS, source + 32, jnp.where(rim < 32, rim + 160, jnp.where(rim >= 96, rim - 96, -1))
    )
    wanted = jnp.where(target < COLS, 2 * target, 2 * (target - COLS) + 1)
    parting[...] = jnp.where(column == wanted, 1.0, 0.0).astype(jnp.bfloat16)


def tracer_kernel(
    part, t, s, u, v, own, side_0, side_1, swap_0, swap_1, corner_0, corner_1, inner, outer, t_next, s_next
):
    near = Around(own, side_0, side_1, swap_0, swap_1, corner_0, corner_1)
    dep = Depths(inner, outer)
    sub = sublanes()

    def body(g, carry):
        start = GROUP * ROWS * g - PART * part
        level = (GROUP * g + sub).astype(jnp.float32)
        edges = Edges(near, g, level, (0,), True)
        wet, q, sides, lap, flow, count = {}, {}, {}, {}, {}, {}
        for j in range(-2, ROWS + 2):
            wet[j] = level < dep.tile(j, 0)
            q[j] = [masked(wet[j], near.level_row(ref, i, g, j)) for i, ref in ((0, t), (1, s))]
            if -1 <= j <= ROWS:
                flow[j] = [masked(wet[j], near.level_row(ref, i, g, j)) for i, ref in ((2, u), (3, v))]
            if j >= 0:
                lap[j - 1], sides[j - 1], count[j - 1] = laplace_row(
                    near, dep, level, wet, q, edges, 0, j - 1
                )
            r = j - 2
            if r < 0:
                continue
            e, w = near.sideways(flow[r][0], edges.ring[1], 0, r)
            u_e = masked(level < dep.tile(r, 1), flow[r][0] + e)
            u_w = masked(level < dep.tile(r, 2), flow[r][0] + w)
            v_n = masked(wet[r + 1], flow[r][1] + flow[r + 1][1])
            v_s = masked(wet[r - 1], flow[r][1] + flow[r - 1][1])
            for f, out in ((0, t_next), (1, s_next)):
                e, w = near.sideways(lap[r][f], edges.lap[0], f, r)
                mix = (e + w) + (lap[r + 1][f] + lap[r - 1][f]) - count[r] * lap[r][f]
                mid = q[r][f]
                e, w = sides[r][f]
                advected = (u_e * (mid + e) - u_w * (mid + w)) + (
                    v_n * (mid + q[r + 1][f]) - v_s * (mid + q[r - 1][f])
                )
                out[pl.ds(start + r, GROUP, stride=ROWS), :] = masked(
                    wet[r],
                    mid - (0.25 * TIME_STEP * advected + TIME_STEP * MIX_TRACER * mix),
                )
        return carry

    lax.fori_loop(2 * part, 2 * part + 2, body, 0)


def store_kernel(levels, u_next, v_next, *refs):
    pieces, (t_out, s_out, u_out, v_out, stored, sems, sems_flow) = refs[:-7], refs[-7:]
    stored[...] = jnp.zeros(TILE, jnp.float32)
    copies = []
    for i, (src, dst) in enumerate(((u_next, u_out), (v_next, v_out))):
        copies.append(
            pltpu.make_async_copy(src.at[pl.ds(0, levels * ROWS), :], dst, sems_flow.at[i])
        )
    for part in range(PARTS):
        size = min(PART, levels * ROWS - PART * part)
        for i, dst in enumerate((t_out, s_out)):
            copies.append(
                pltpu.make_async_copy(
                    pieces[2 * part + i].at[pl.ds(0, size), :],
                    dst.at[pl.ds(PART * part, size), :],
                    sems.at[2 * part + i],
                )
            )
    for copy in copies:
        copy.start()
    for copy in copies:
        copy.wait()


STEPS = 5 * ROWS // GROUP


class Plane:
    def __init__(self, even, odd):
        self.even, self.odd = even, odd

    def map(self, other, fn):
        if isinstance(other, Plane):
            return Plane(
                [fn(a, b) for a, b in zip(self.even, other.even)],
                [fn(a, b) for a, b in zip(self.odd, other.odd)],
            )
        return Plane([fn(a, other) for a in self.even], [fn(a, other) for a in self.odd])

    def __add__(self, other):
        return self.map(other, lambda a, b: a + b)

    def __sub__(self, other):
        return self.map(other, lambda a, b: a - b)

    def __mul__(self, other):
        return self.map(other, lambda a, b: a * b)

    def low(self, other):
        return self.map(other, jnp.minimum)

    def east(self):
        return Plane(self.odd, [turn(x, -1) for x in self.even])

    def west(self):
        return Plane([turn(x, 1) for x in self.odd], self.even)

    def north(self):
        return Plane(*[x[1:] + [turn(x[0], -1, 0)] for x in (self.even, self.odd)])

    def south(self):
        return Plane(*[[turn(x[-1], 1, 0)] + x[:-1] for x in (self.even, self.odd)])


def one_hot(x, matrix, side, terms):
    total = None
    for _ in range(terms):
        term = x.astype(jnp.bfloat16)
        x = x - term.astype(jnp.float32)
        product = lax.dot_general(
            term, matrix, (((1,), (side,)), ((), ())), preferred_element_type=jnp.float32
        )
        total = product if total is None else total + product
    return total


def solve_kernel(levels, own, core, chip_0, chip_1, passed, parting, stored, out, own_buf, rim_buf):
    del stored
    lat, _ = place()
    lat_even, lon_even = evens()
    chip_even = lat // 2 % 2 == 0
    lane = lanes()

    def tile(b, index):
        if b == 0:
            return own[index]
        if abs(b) == 2:
            to_first = chip_even if b > 0 else jnp.logical_not(chip_even)
            return jnp.where(to_first, chip_0[index], chip_1[index])
        on_chip = lat_even if b > 0 else jnp.logical_not(lat_even)
        return jnp.where(on_chip, core[index], passed[index])

    def gather(plane):
        for b in range(-2, 3):
            inside = (lat + b >= 0) & (lat + b < lax.axis_size("lat"))
            for half in range(2):
                at = ROWS * (b + 2) + GROUP * half
                mid = tile(b, 2 * plane + half)
                first, second = tile(b, BLOCK + half), tile(b, BLOCK + STRIP + half)
                east = turn(jnp.where(lon_even, first, second), -32 * plane)
                west = turn(jnp.where(lon_even, second, first), 96 - 32 * plane)
                rim = jnp.where(lane < 32, east, jnp.where(lane >= 96, west, 0.0))
                if b != 0:
                    mid, rim = jnp.where(inside, mid, 0.0), jnp.where(inside, rim, 0.0)
                own_buf[at : at + GROUP, :] = mid
                rim_buf[at : at + GROUP, :] = rim
        both = one_hot(
            jnp.concatenate([own_buf[...], rim_buf[...]], axis=1), parting[...], 0, 1 if plane == 0 else 3
        )
        own_buf[...], rim_buf[...] = both[:, :COLS], both[:, COLS:]
        return Plane(
            *[[buf[pl.ds(t, GROUP, stride=STEPS), :] for t in range(STEPS)] for buf in (own_buf, rim_buf)]
        )

    depth, prior, zonal, northward = [gather(plane) for plane in range(4)]

    ocean = depth.map(0.0, lambda a, b: jnp.where(a > b, 1.0, 0.0))
    depth_east, depth_north = depth.low(depth.east()), depth.low(depth.north())
    zonal_flow = zonal.map(depth_east, lambda a, b: masked(b > 0.0, a))
    north_flow = northward.map(depth_north, lambda a, b: masked(b > 0.0, a))
    divergence = (zonal_flow - zonal_flow.west()) + (north_flow - north_flow.south())
    right_side = prior * SURFACE_TERM - divergence * TRANSPORT_SCALE
    east_face, north_face = depth_east * (1.0 / levels), depth_north * (1.0 / levels)
    west_face, south_face = east_face.west(), north_face.south()
    diagonal = (((east_face + west_face) + north_face) + south_face) + SURFACE_TERM
    inverse = diagonal.map(1.0, lambda a, b: b / a)
    right_side, east_face, west_face, north_face, south_face = [
        x * inverse for x in (right_side, east_face, west_face, north_face, south_face)
    ]
    height, change = prior, None
    scales, carries = chebyshev_weights(ITERATIONS)
    for scale, carry in zip(scales, carries):
        spread = (east_face * height.east() + west_face * height.west()) + (
            north_face * height.north() + south_face * height.south()
        )
        residual = (right_side - height) + spread
        step = residual * scale
        change = step if change is None else step + change * carry
        height = height + change
    height = height * ocean
    for t in range(STEPS):
        own_buf[pl.ds(t, GROUP, stride=STEPS), :] = height.even[t]
        rim_buf[pl.ds(t, GROUP, stride=STEPS), :] = height.odd[t]
    rows = slice(2 * ROWS, 3 * ROWS)
    out[...] = one_hot(
        jnp.concatenate([own_buf[rows, :], rim_buf[rows, :]], axis=1), parting[:COLS, :], 1, 3
    )


def join_kernel(count, *refs):
    at = 0
    for ref in refs[:count]:
        refs[-1][at : at + ref.shape[0]] = ref[...]
        at += ref.shape[0]


def pass_kernel(chip_0, chip_1, *refs):
    lat, _ = place()
    refs[-1][...] = jnp.where((lat % 2 == 0) == (lat // 2 % 2 == 0), chip_0[...], chip_1[...])


def swap(value, axis, partner):
    count = lax.axis_size(axis)
    return lax.ppermute(value, axis, [(i, partner(i) % count) for i in range(count)])


def even_first(i):
    return i + 1 if i % 2 == 0 else i - 1


def odd_first(i):
    return i - 1 if i % 2 == 0 else i + 1


def chip_even_first(i):
    return i + 2 if i // 2 % 2 == 0 else i - 2


def chip_odd_first(i):
    return i - 2 if i // 2 % 2 == 0 else i + 2


def shape(*dims):
    return jax.ShapeDtypeStruct(dims, jnp.float32)


VMEM = pl.BlockSpec(memory_space=pltpu.VMEM)
ANY = pl.BlockSpec(memory_space=pl.ANY)
HBM = pl.BlockSpec(memory_space=pltpu.HBM)


def call(kernel, outs, scratch, *args, ins=None, out_specs=None):
    return pl.pallas_call(
        kernel,
        out_shape=outs,
        in_specs=ins or [VMEM] * len(args),
        out_specs=out_specs or jax.tree.map(lambda _: VMEM, outs),
        scratch_shapes=scratch,
        compiler_params=pltpu.CompilerParams(vmem_limit_bytes=32 * 2**20),
        cost_estimate=pl.CostEstimate(flops=0, bytes_accessed=4 * 2**20, transcendentals=0),
    )(*args)


def per_device(
    heat_anomaly,
    saltiness_anomaly,
    zonal_current_array,
    meridional_current_array,
    sea_height_prior,
    ocean_layer_number,
):
    levels, rows, cols = heat_anomaly.shape
    lat_total = rows * lax.axis_size("lat")
    fields = [
        x.reshape(levels * rows, cols)
        for x in (heat_anomaly, saltiness_anomaly, zonal_current_array, meridional_current_array)
    ]
    padded, plane = shape(PADDED, cols), shape(rows, cols)

    def tiles(n):
        return shape(n, *TILE)

    by_rows = tiles(ROWS * GROUPS)

    *kept, own, to_0, to_1, depth, prior = call(
        functools.partial(load_kernel, levels),
        (by_rows,) * 4 + (tiles(PACKS + 1), tiles(SIDE), tiles(SIDE), plane, plane),
        [
            pltpu.VMEM((rows, cols), jnp.int32),
            *[pltpu.VMEM((PADDED, cols), jnp.float32)] * 4,
            pltpu.SemaphoreType.DMA((4 * LOADS,)),
            pltpu.SemaphoreType.DMA((2,)),
        ],
        *[
            pltpu.with_memory_space_constraint(x, pltpu.HBM)
            for x in (*fields, ocean_layer_number, sea_height_prior)
        ],
        ins=[HBM] * 6,
    )
    sides = (own, swap(to_0, "lon", even_first), swap(to_1, "lon", odd_first))
    rows_0, rows_1 = call(rows_kernel, (tiles(HALO + 2),) * 2, [], *kept, depth)
    swaps = (swap(rows_0, "lat", even_first), swap(rows_1, "lat", odd_first))
    to_0, to_1 = call(corner_kernel, (tiles(CORNER),) * 2, [], *sides)
    swaps += (swap(to_0, "lat", even_first), swap(to_1, "lat", odd_first))

    scratch = [pltpu.VMEM((GROUP * ROWS, COLS), jnp.float32)] * 2
    scratch += [pltpu.VMEM((ROWS, *TILE), jnp.float32)] * 2
    u_inner, v_inner, sums, inner, kept_laps = call(
        functools.partial(inner_kernel, lat_total),
        (by_rows, by_rows, tiles(4), tiles(3 * ROWS), shape(2 * len(KEPT), GROUPS, *TILE)),
        scratch,
        *kept,
        depth,
        *sides,
    )
    some_rows = shape(len(OUTER_ROWS), GROUPS, *TILE)
    u_outer, v_outer, block, strip_0, strip_1, outer = call(
        functools.partial(outer_kernel, lat_total),
        (some_rows, some_rows, tiles(BLOCK), tiles(STRIP), tiles(STRIP), tiles(12)),
        scratch + [pltpu.VMEM((4, *TILE), jnp.float32)],
        *kept,
        depth,
        prior,
        *sides,
        *swaps,
        sums,
        inner,
        kept_laps,
    )
    matrix = jax.ShapeDtypeStruct((2 * COLS, 2 * COLS), jnp.bfloat16)
    u_next, v_next, parting = call(
        merge_kernel, (padded, padded, matrix), [], u_inner, v_inner, u_outer, v_outer
    )
    pieces = []
    for part in range(PARTS):
        pieces += call(
            functools.partial(tracer_kernel, part),
            (shape(PART, cols),) * 2,
            [],
            *kept,
            *sides,
            *swaps,
            inner,
            outer,
        )

    strips = [swap(strip_0, "lon", even_first), swap(strip_1, "lon", odd_first)]
    made = pieces[:4]
    block = call(
        functools.partial(join_kernel, 3),
        tiles(BLOCK + 2 * STRIP),
        [],
        block,
        *strips,
        *made,
        ins=[VMEM] * 3 + [ANY] * len(made),
    )
    chip_0, chip_1 = swap(block, "lat", chip_even_first), swap(block, "lat", chip_odd_first)
    core = swap(block, "lat", even_first)
    made = [*pieces[4:], u_next, v_next]
    passed = call(
        pass_kernel,
        tiles(BLOCK + 2 * STRIP),
        [],
        chip_0,
        chip_1,
        *made,
        ins=[VMEM] * 2 + [ANY] * len(made),
    )
    passed = swap(passed, "lat", even_first)
    *results, stored = call(
        functools.partial(store_kernel, levels),
        (shape(levels * rows, cols),) * 4 + (shape(*TILE),),
        [pltpu.SemaphoreType.DMA((2 * PARTS,)), pltpu.SemaphoreType.DMA((2,))],
        u_next,
        v_next,
        *pieces,
        out_specs=(HBM,) * 4 + (VMEM,),
    )
    height = call(
        functools.partial(solve_kernel, levels),
        plane,
        [pltpu.VMEM((5 * ROWS, COLS), jnp.float32)] * 2,
        block,
        core,
        chip_0,
        chip_1,
        passed,
        parting,
        stored,
        ins=[VMEM] * 6 + [ANY],
    )
    return *[x.reshape(levels, rows, cols) for x in results], height


def solution(mesh):
    cells, plane = P(None, "lat", "lon"), P("lat", "lon")
    return jax.shard_map(
        per_device,
        mesh=mesh,
        in_specs=(cells,) * 4 + (plane,) * 2,
        out_specs=(cells,) * 4 + (plane,),
        check_vma=False,
    )
```
